32 devices in a mesh: dp: 4 (over y, x), seq: 8 (over z, core).
Axes of the slice: x: 2, y: 2, z: 4, core: 2. Of those that a mesh axis runs over, the one named last changes fastest.
Arguments:
- frames: float32 [16, 2048, 256], P('dp', 'seq'), may hold values from -6 to 6
- flow_embed: float32 [16, 1024], P('dp'), may hold values from -6 to 6
- lengths: int32 [16], P('dp'), may hold values from 256 to 2048, as said below
- cotangent: float32 [16, 1024, 256], P('dp', 'seq'), may hold values from -6 to 6
- conv_one: bfloat16 [2, 3, 256, 256], replicated, may hold values from -0.21875 to 0.21875
- conv_two: bfloat16 [2, 3, 256, 256], replicated, may hold values from -0.21875 to 0.21875
- res_weight: bfloat16 [2, 256, 256], replicated, may hold values from -0.375 to 0.375
- norm_gain: bfloat16 [2, 2, 256], replicated, may hold values from 0.25 to 1.75
- norm_bias: bfloat16 [2, 2, 256], replicated, may hold values from -3 to 3
- time_weight: bfloat16 [2, 1024, 256], replicated, may hold values from -0.1875 to 0.1875
- time_bias: bfloat16 [2, 256], replicated, may hold values from -3 to 3
- layer_gain: bfloat16 [2, 2, 256], replicated, may hold values from 0.25 to 1.75
- layer_bias: bfloat16 [2, 2, 256], replicated, may hold values from -1.75 to 1.75
- qkv_weight: bfloat16 [2, 256, 384], replicated, may hold values from -0.375 to 0.375
- out_weight: bfloat16 [2, 128, 256], replicated, may hold values from -1.5 to 1.5
- out_bias: bfloat16 [2, 256], replicated, may hold values from -1.75 to 1.75
- up_weight: bfloat16 [2, 256, 1024], replicated, may hold values from -0.375 to 0.375
- up_bias: bfloat16 [2, 1024], replicated, may hold values from -3 to 3
- snake_alpha: bfloat16 [2, 1024], replicated, may hold values from -1 to 1
- snake_beta: bfloat16 [2, 1024], replicated, may hold values from -0.5 to 0.5
- down_weight: bfloat16 [2, 1024, 256], replicated, may hold values from -0.1875 to 0.1875
- down_bias: bfloat16 [2, 256], replicated, may hold values from -1.75 to 1.75
- shrink_weight: bfloat16 [3, 256, 256], replicated, may hold values from -0.21875 to 0.21875
- shrink_bias: bfloat16 [256], replicated, may hold values from -1.75 to 1.75
Outputs:
- output: float32 [16, 1024, 256], P('dp', 'seq')
- input_grad: float32 [16, 2048, 256], P('dp', 'seq')
- grad_conv_one: float32 [2, 3, 256, 256], replicated
- grad_conv_two: float32 [2, 3, 256, 256], replicated
- grad_res_weight: float32 [2, 256, 256], replicated
- grad_norm_gain: float32 [2, 2, 256], replicated
- grad_norm_bias: float32 [2, 2, 256], replicated
- grad_time_weight: float32 [2, 1024, 256], replicated
- grad_time_bias: float32 [2, 256], replicated
- grad_layer_gain: float32 [2, 2, 256], replicated
- grad_layer_bias: float32 [2, 2, 256], replicated
- grad_qkv_weight: float32 [2, 256, 384], replicated
- grad_out_weight: float32 [2, 128, 256], replicated
- grad_out_bias: float32 [2, 256], replicated
- grad_up_weight: float32 [2, 256, 1024], replicated
- grad_up_bias: float32 [2, 1024], replicated
- grad_snake_alpha: float32 [2, 1024], replicated
- grad_snake_beta: float32 [2, 1024], replicated
- grad_down_weight: float32 [2, 1024, 256], replicated
- grad_down_bias: float32 [2, 256], replicated
- grad_shrink_weight: float32 [3, 256, 256], replicated
- grad_shrink_bias: float32 [256], replicated
The draws below stay inside these ranges and needn't reach their ends.
Inputs may be any that keep to these rules, and one draw needn't show every extreme that they name: `lengths`: of the two utterances 2 i and 2 i + 1, one has exactly 2048 frames.
All inputs are finite; a program needn't handle non-finite values.
Results may differ from the reference program's by a relative error of at most 0.0003.
Values sent between devices are 32-bit elements; how exact they have to be, the bound alone decides.
A program may use at most 640 MiB of HBM per device.

```python
import math
import jax
import jax.numpy as jnp
from jax import lax

CHANNELS = 256
TIME_DIM = 1024
FF = 1024
HEADS = 2
HEAD_DIM = 64
GROUPS = 8
LEN = 2048
UTTERANCES = 16


def draw_lengths(key, part):
    key = jax.random.fold_in(key, 11)
    key_length, key_choose = jax.random.split(key)
    drawn = jax.random.randint(key_length, (UTTERANCES,), LEN // 8, LEN + 1)
    chosen = jax.random.randint(key_choose, (UTTERANCES // 2,), 0, 2)
    full_one = jnp.arange(UTTERANCES) % 2 == jnp.repeat(chosen, 2)
    return jnp.where(full_one, LEN, drawn).astype(jnp.int32)


def steps_of(stream_key, shape, shards, least, high):
    factor_of, own = 1.0, jax.random.fold_in(stream_key, 6)
    for position, shards_of in shards:
        steps = jnp.exp(jax.random.uniform(jax.random.fold_in(own, position), (shards_of,), jnp.float32, least / len(shards), high / len(shards)))
        factor_of = factor_of * jnp.repeat(steps, shape[position] // shards_of).reshape([-1 if axis == position else 1 for axis in range(len(shape))])
    return factor_of


def normal_values(key, shape, spread, most, cuts=(), dtype=jnp.bfloat16):
    values = jax.random.normal(key, shape, jnp.float32) * spread
    if len(cuts) > 0:
        values = steps_of(key, shape, cuts, -0.22, 0.18) * values
    return jnp.clip(values, min=-most, max=most).astype(dtype)


def setup_inputs(seed: int = 0) -> dict:
    key_of = jax.random.split(jax.random.key(seed), 25)
    return {
        "frames": normal_values(key_of[0], (UTTERANCES, LEN, CHANNELS), 1.0, 6.0, ((0, 4), (1, 8)), jnp.float32),
        "flow_embed": normal_values(key_of[1], (UTTERANCES, TIME_DIM), 1.0, 6.0, ((0, 4),), jnp.float32),
        "lengths": draw_lengths(jax.random.fold_in(key_of[24], 71), 0),
        "cotangent": normal_values(key_of[3], (UTTERANCES, LEN // 2, CHANNELS), 1.0, 6.0, ((0, 4), (1, 8)), jnp.float32),
        "conv_one": normal_values(key_of[4], (2, 3, CHANNELS, CHANNELS), (3 * CHANNELS) ** -0.5, 0.21875),
        "conv_two": normal_values(key_of[5], (2, 3, CHANNELS, CHANNELS), (3 * CHANNELS) ** -0.5, 0.21875),
        "res_weight": normal_values(key_of[6], (2, CHANNELS, CHANNELS), CHANNELS ** -0.5, 0.375),
        "norm_gain": jnp.clip(1.0 + 0.15 * jax.random.normal(key_of[7], (2, 2, CHANNELS), jnp.float32), 0.25, 1.75).astype(jnp.bfloat16),
        "norm_bias": normal_values(key_of[8], (2, 2, CHANNELS), 0.5, 3.0),
        "time_weight": normal_values(key_of[9], (2, TIME_DIM, CHANNELS), TIME_DIM ** -0.5, 0.1875),
        "time_bias": normal_values(key_of[10], (2, CHANNELS), 0.5, 3.0),
        "layer_gain": jnp.clip(1.0 + 0.15 * jax.random.normal(key_of[11], (2, 2, CHANNELS), jnp.float32), 0.25, 1.75).astype(jnp.bfloat16),
        "layer_bias": normal_values(key_of[12], (2, 2, CHANNELS), 0.3, 1.75),
        "qkv_weight": normal_values(key_of[13], (2, CHANNELS, 3 * HEADS * HEAD_DIM), CHANNELS ** -0.5, 0.375),
        "out_weight": normal_values(key_of[14], (2, HEADS * HEAD_DIM, CHANNELS), (HEADS * HEAD_DIM // 8) ** -0.5, 1.5),
        "out_bias": normal_values(key_of[15], (2, CHANNELS), 0.3, 1.75),
        "up_weight": normal_values(key_of[16], (2, CHANNELS, FF), CHANNELS ** -0.5, 0.375),
        "up_bias": normal_values(key_of[17], (2, FF), 0.5, 3.0),
        "snake_alpha": jnp.clip(jax.random.uniform(key_of[18], (2, FF), jnp.float32, -1.0, 1.0), -1.0, 1.0).astype(jnp.bfloat16),
        "snake_beta": jnp.clip(jax.random.uniform(key_of[19], (2, FF), jnp.float32, -0.5, 0.5), -0.5, 0.5).astype(jnp.bfloat16),
        "down_weight": normal_values(key_of[20], (2, FF, CHANNELS), FF ** -0.5, 0.1875),
        "down_bias": normal_values(key_of[21], (2, CHANNELS), 0.3, 1.75),
        "shrink_weight": normal_values(key_of[22], (3, CHANNELS, CHANNELS), (3 * CHANNELS) ** -0.5, 0.21875),
        "shrink_bias": normal_values(key_of[23], (CHANNELS,), 0.3, 1.75),
    }


precise = lax.Precision.HIGHEST
epsilon = 1e-05

@jax.custom_vjp
def low(v):
    return lax.optimization_barrier(v.astype(jnp.bfloat16)).astype(jnp.float32)

@jax.custom_vjp
def low_back(v):
    return v

def low_keep(v):
    return (low(v), None)

def low_pass(kept, grad):
    return (grad,)

def back_keep(v):
    return (v, None)

def back_low(kept, grad):
    return (low(grad),)
low.defvjp(low_keep, low_pass)
low_back.defvjp(back_keep, back_low)

def mish_curve(value_in):
    return value_in * jnp.tanh(jax.nn.softplus(value_in))

def conv_piece(padded, weight):
    frames_out = padded.shape[1] - 2
    summed = jnp.einsum('ufc,cd->ufd', padded[:, :frames_out], weight[0], precision=precise)
    summed = summed + jnp.einsum('ufc,cd->ufd', padded[:, 1:frames_out + 1], weight[1], precision=precise)
    return summed + jnp.einsum('ufc,cd->ufd', padded[:, 2:], weight[2], precision=precise)

def shrink_piece(padded, weight, bias_vec):
    span_len = padded.shape[1] - 1
    summed = jnp.einsum('ufc,cd->ufd', padded[:, 0:span_len:2], weight[0], precision=precise)
    summed = summed + jnp.einsum('ufc,cd->ufd', padded[:, 1:span_len:2], weight[1], precision=precise)
    summed = summed + jnp.einsum('ufc,cd->ufd', padded[:, 2:span_len + 1:2], weight[2], precision=precise)
    return summed + bias_vec

def group_sums(conv_out, mask_row):
    utterances, frames_in, channels = conv_out.shape
    masked = conv_out * mask_row[:, :, None]
    shape_new = (utterances, frames_in, GROUPS, channels // GROUPS)
    first_sum = lax.optimization_barrier(jnp.sum(masked.reshape(shape_new), axis=(1, 3)))
    second_sum = lax.optimization_barrier(jnp.sum((masked * conv_out).reshape(shape_new), axis=(1, 3)))
    return (first_sum, second_sum)

def group_apply(conv_out, first_sum, second_sum, counts, gain_vec, bias_vec, mask_row):
    group_width = conv_out.shape[2] // GROUPS
    mean_val = first_sum / counts[:, None]
    var_val = second_sum / counts[:, None] - mean_val * mean_val
    scale_val = lax.rsqrt(var_val + epsilon)
    mean_full = jnp.repeat(mean_val, group_width, axis=1)[:, None, :]
    scale_full = jnp.repeat(scale_val, group_width, axis=1)[:, None, :]
    normed = (conv_out - mean_full) * scale_full * gain_vec + bias_vec
    return mish_curve(normed) * mask_row[:, :, None]

def time_piece(embedding, weight, bias_vec):
    return jnp.dot(mish_curve(embedding), weight, precision=precise) + bias_vec

def layer_norm(value_in, gain_vec, bias_vec):
    mean_val = lax.optimization_barrier(jnp.mean(value_in, axis=-1, keepdims=True))
    centered = value_in - mean_val
    var_val = lax.optimization_barrier(jnp.mean(centered * centered, axis=-1, keepdims=True))
    return centered * lax.rsqrt(var_val + epsilon) * gain_vec + bias_vec

def attend_in(value_in, gain_vec, bias_vec, qkv_weight):
    normed = layer_norm(value_in, gain_vec, bias_vec)
    packed = jnp.einsum('ufc,ce->ufe', normed, qkv_weight, precision=precise)
    inner_dim = packed.shape[2] // 3
    return (packed[:, :, :inner_dim], packed[:, :, inner_dim:2 * inner_dim], packed[:, :, 2 * inner_dim:])

def attend_out(value_in, queries, key_full, value_full, key_mask, later_weights):
    out_weight, out_bias, gain_vec, bias_vec, up_weight, up_bias, snake_alpha, snake_beta, down_weight, down_bias = later_weights
    utterances, frames_in, inner_dim = queries.shape
    head_dim = inner_dim // HEADS
    key_count = key_full.shape[1]
    query_heads = queries.reshape(utterances, frames_in, HEADS, head_dim)
    key_heads = key_full.reshape(utterances, key_count, HEADS, head_dim)
    value_heads = value_full.reshape(utterances, key_count, HEADS, head_dim)
    scores = jnp.einsum('uqhd,ukhd->uhqk', query_heads, key_heads, precision=precise) / math.sqrt(head_dim)
    scores = jnp.where(key_mask[:, None, None, :] > 0.5, scores, -1e+30)
    scores = scores - lax.optimization_barrier(jnp.max(scores, axis=3, keepdims=True))
    raised = jnp.exp(scores)
    weights_soft = raised / lax.optimization_barrier(jnp.sum(raised, axis=3, keepdims=True))
    attended = jnp.einsum('uhqk,ukhd->uqhd', weights_soft, value_heads, precision=precise)
    attended = attended.reshape(utterances, frames_in, inner_dim)
    current = value_in + jnp.einsum('ufe,ec->ufc', attended, out_weight, precision=precise) + out_bias
    normed = layer_norm(current, gain_vec, bias_vec)
    raised_up = jnp.einsum('ufc,ce->ufe', normed, up_weight, precision=precise) + up_bias
    snake_out = raised_up + jnp.sin(raised_up * jnp.exp(snake_alpha)) ** 2 / (jnp.exp(snake_beta) + 1e-09)
    return current + jnp.einsum('ufe,ec->ufc', snake_out, down_weight, precision=precise) + down_bias

def layer_weights(stacked, layer_index):
    conv_one, conv_two, res_weight, norm_gain, norm_bias, time_weight, time_bias, layer_gain, layer_bias, qkv_weight, out_weight, out_bias, up_weight, up_bias, snake_alpha, snake_beta, down_weight, down_bias = stacked
    resnet_part = (conv_one[layer_index], conv_two[layer_index], res_weight[layer_index], norm_gain[layer_index], norm_bias[layer_index], time_weight[layer_index], time_bias[layer_index])
    first_part = (layer_gain[layer_index, 0], layer_bias[layer_index, 0], qkv_weight[layer_index])
    later_part = (out_weight[layer_index], out_bias[layer_index], layer_gain[layer_index, 1], layer_bias[layer_index, 1], up_weight[layer_index], up_bias[layer_index], snake_alpha[layer_index], snake_beta[layer_index], down_weight[layer_index], down_bias[layer_index])
    return (resnet_part, first_part, later_part)

def resnet_ref(inputs, mask_row, counts, embed_row, weights):
    conv_first, conv_second, res_weight, norm_gain, norm_bias, time_weight, time_bias = weights
    column = mask_row[:, :, None]
    masked = inputs * column
    first_conv = conv_piece(jnp.pad(masked, ((0, 0), (1, 1), (0, 0))), conv_first)
    first_sum, second_sum = group_sums(first_conv, mask_row)
    hidden = group_apply(first_conv, first_sum, second_sum, counts, norm_gain[0], norm_bias[0], mask_row)
    hidden = hidden + time_piece(embed_row, time_weight, time_bias)[:, None, :]
    second = conv_piece(jnp.pad(hidden * column, ((0, 0), (1, 1), (0, 0))), conv_second)
    first_sum, second_sum = group_sums(second, mask_row)
    result = group_apply(second, first_sum, second_sum, counts, norm_gain[1], norm_bias[1], mask_row)
    return result + jnp.einsum('ufc,cd->ufd', masked, res_weight, precision=precise)

def block_ref(current, mask_row, first_weights, later_weights):
    queries, key_full, value_full = attend_in(current, first_weights[0], first_weights[1], first_weights[2])
    return attend_out(current, queries, key_full, value_full, mask_row, later_weights)

def forward_one(inputs, embedding, length, weights):
    stacked = weights[:18]
    shrink_weight = weights[18]
    shrink_bias = weights[19]
    long_len = inputs.shape[0]
    group_width = inputs.shape[1] // GROUPS
    mask_one = (jnp.arange(long_len)[None, :] < length).astype(jnp.float32)
    mask_two = (2 * jnp.arange(long_len // 2)[None, :] < length).astype(jnp.float32)
    counts_one = lax.optimization_barrier(jnp.sum(mask_one, axis=1)) * group_width
    counts_two = lax.optimization_barrier(jnp.sum(mask_two, axis=1)) * group_width
    embed_row = embedding[None, :]
    res_zero, first_zero, later_zero = layer_weights(stacked, 0)
    res_one, first_one, later_one = layer_weights(stacked, 1)
    current = resnet_ref(inputs[None], mask_one, counts_one, embed_row, res_zero)
    current = block_ref(current, mask_one, first_zero, later_zero)
    padded = jnp.pad(current * mask_one[:, :, None], ((0, 0), (1, 0), (0, 0)))
    current = shrink_piece(padded, shrink_weight, shrink_bias)
    current = resnet_ref(current, mask_two, counts_two, embed_row, res_one)
    current = block_ref(current, mask_two, first_one, later_one)
    return (current * mask_two[:, :, None])[0]

def reference(frames, flow_embed, lengths, cotangent, conv_one, conv_two, res_weight, norm_gain, norm_bias, time_weight, time_bias, layer_gain, layer_bias, qkv_weight, out_weight, out_bias, up_weight, up_bias, snake_alpha, snake_beta, down_weight, down_bias, shrink_weight, shrink_bias):
    weights = tuple((weight_in.astype(jnp.float32) for weight_in in (conv_one, conv_two, res_weight, norm_gain, norm_bias, time_weight, time_bias, layer_gain, layer_bias, qkv_weight, out_weight, out_bias, up_weight, up_bias, snake_alpha, snake_beta, down_weight, down_bias, shrink_weight, shrink_bias)))

    def one_utterance(running, element):
        inputs, embedding, length, grad_out = element

        def forward(current, weights_in):
            return forward_one(current, embedding, length, weights_in)
        result, pull_back = jax.vjp(forward, inputs, weights)
        grad_inputs, grad_weights = pull_back(grad_out)
        running = jax.tree.map(jnp.add, running, grad_weights)
        return (running, (result, grad_inputs))
    start_sums = tuple((jnp.zeros_like(weight_in) for weight_in in weights))
    summed, (output, input_grad) = lax.scan(one_utterance, start_sums, (frames, flow_embed, lengths, cotangent))
    grad_conv_one, grad_conv_two, grad_res_weight, grad_norm_gain, grad_norm_bias, grad_time_weight, grad_time_bias, grad_layer_gain, grad_layer_bias, grad_qkv_weight, grad_out_weight, grad_out_bias, grad_up_weight, grad_up_bias, grad_snake_alpha, grad_snake_beta, grad_down_weight, grad_down_bias, grad_shrink_weight, grad_shrink_bias = summed
    return (output, input_grad, grad_conv_one, grad_conv_two, grad_res_weight, grad_norm_gain, grad_norm_bias, grad_time_weight, grad_time_bias, grad_layer_gain, grad_layer_bias, grad_qkv_weight, grad_out_weight, grad_out_bias, grad_up_weight, grad_up_bias, grad_snake_alpha, grad_snake_beta, grad_down_weight, grad_down_bias, grad_shrink_weight, grad_shrink_bias)
```

```python
import math
import typing
from types import SimpleNamespace
from typing import Any

import jax
import jax.numpy as jnp
from jax import lax
from jax.experimental import pallas as pl
from jax.experimental.pallas import tpu as pltpu
from jax.sharding import PartitionSpec as P

HEADS = 2
GROUPS = 8


precise = lax.Precision.HIGHEST
epsilon = 1e-05


def with_halo(value, sides, width):
    for axis, dim in sides:
        count, length = (lax.axis_size(axis), value.shape[dim])
        up = [(i, (i + 1) % count) for i in range(count - 1)]
        down = [(j, i) for i, j in up]
        last = lax.slice_in_dim(value, length - width, length, axis=dim)
        first = lax.slice_in_dim(value, 0, width, axis=dim)
        before = lax.ppermute(last, axis, up)
        after = lax.ppermute(first, axis, down)
        value = jnp.concatenate([before, value, after], axis=dim)
    return value


def shifted(value, axis, by):
    count = lax.axis_size(axis)
    pairs = [(i, i + by) for i in range(count) if 0 <= i + by < count]
    return lax.ppermute(value, axis, pairs)


def mish_curve(value_in):
    return value_in * jnp.tanh(jax.nn.softplus(value_in))


def conv_piece(padded, weight):
    frames_out = padded.shape[1] - 2
    summed = jnp.einsum("ufc,cd->ufd", padded[:, :frames_out], weight[0], precision=precise)
    summed = summed + jnp.einsum(
        "ufc,cd->ufd", padded[:, 1 : frames_out + 1], weight[1], precision=precise
    )
    return summed + jnp.einsum("ufc,cd->ufd", padded[:, 2:], weight[2], precision=precise)


def shrink_piece(padded, weight, bias_vec):
    span_len = padded.shape[1] - 1
    summed = jnp.einsum("ufc,cd->ufd", padded[:, 0:span_len:2], weight[0], precision=precise)
    summed = summed + jnp.einsum(
        "ufc,cd->ufd", padded[:, 1:span_len:2], weight[1], precision=precise
    )
    summed = summed + jnp.einsum(
        "ufc,cd->ufd", padded[:, 2 : span_len + 1 : 2], weight[2], precision=precise
    )
    return summed + bias_vec


def group_sums(conv_out, mask_row):
    utterances, frames_in, channels = conv_out.shape
    masked = conv_out * mask_row[:, :, None]
    shape_new = (utterances, frames_in, GROUPS, channels // GROUPS)
    first_sum = jnp.sum(masked.reshape(shape_new), axis=(1, 3))
    second_sum = jnp.sum((masked * conv_out).reshape(shape_new), axis=(1, 3))
    return (first_sum, second_sum)


def group_apply(conv_out, first_sum, second_sum, counts, gain_vec, bias_vec, mask_row):
    group_width = conv_out.shape[2] // GROUPS
    mean_val = first_sum / counts[:, None]
    var_val = second_sum / counts[:, None] - mean_val * mean_val
    scale_val = lax.rsqrt(var_val + epsilon)
    mean_full = jnp.repeat(mean_val, group_width, axis=1)[:, None, :]
    scale_full = jnp.repeat(scale_val, group_width, axis=1)[:, None, :]
    normed = (conv_out - mean_full) * scale_full * gain_vec + bias_vec
    return mish_curve(normed) * mask_row[:, :, None]


def time_piece(embedding, weight, bias_vec):
    return jnp.dot(mish_curve(embedding), weight, precision=precise) + bias_vec


def layer_norm(value_in, gain_vec, bias_vec):
    mean_val = jnp.mean(value_in, axis=-1, keepdims=True)
    centered = value_in - mean_val
    var_val = jnp.mean(centered * centered, axis=-1, keepdims=True)
    return centered * lax.rsqrt(var_val + epsilon) * gain_vec + bias_vec


def attend_in(value_in, gain_vec, bias_vec, qkv_weight):
    normed = layer_norm(value_in, gain_vec, bias_vec)
    packed = jnp.einsum("ufc,ce->ufe", normed, qkv_weight, precision=precise)
    inner_dim = packed.shape[2] // 3
    return (
        packed[:, :, :inner_dim],
        packed[:, :, inner_dim : 2 * inner_dim],
        packed[:, :, 2 * inner_dim :],
    )


def attend_out(value_in, queries, key_full, value_full, key_mask, later_weights):
    (
        out_weight,
        out_bias,
        gain_vec,
        bias_vec,
        up_weight,
        up_bias,
        snake_alpha,
        snake_beta,
        down_weight,
        down_bias,
    ) = later_weights
    utterances, frames_in, inner_dim = queries.shape
    head_dim = inner_dim // HEADS
    key_count = key_full.shape[1]
    query_heads = queries.reshape(utterances, frames_in, HEADS, head_dim)
    key_heads = key_full.reshape(utterances, key_count, HEADS, head_dim)
    value_heads = value_full.reshape(utterances, key_count, HEADS, head_dim)
    scores = jnp.einsum("uqhd,ukhd->uhqk", query_heads, key_heads, precision=precise) / math.sqrt(
        head_dim
    )
    scores = jnp.where(key_mask[:, None, None, :] > 0.5, scores, -1e30)
    scores = scores - jnp.max(scores, axis=3, keepdims=True)
    raised = jnp.exp(scores)
    weights_soft = raised / jnp.sum(raised, axis=3, keepdims=True)
    attended = jnp.einsum("uhqk,ukhd->uqhd", weights_soft, value_heads, precision=precise)
    attended = attended.reshape(utterances, frames_in, inner_dim)
    current = (
        value_in + jnp.einsum("ufe,ec->ufc", attended, out_weight, precision=precise) + out_bias
    )
    normed = layer_norm(current, gain_vec, bias_vec)
    raised_up = jnp.einsum("ufc,ce->ufe", normed, up_weight, precision=precise) + up_bias
    snake_out = raised_up + jnp.sin(raised_up * jnp.exp(snake_alpha)) ** 2 / (
        jnp.exp(snake_beta) + 1e-09
    )
    return (
        current + jnp.einsum("ufe,ec->ufc", snake_out, down_weight, precision=precise) + down_bias
    )


def layer_weights(stacked, layer_index):
    (
        conv_one,
        conv_two,
        res_weight,
        norm_gain,
        norm_bias,
        time_weight,
        time_bias,
        layer_gain,
        layer_bias,
        qkv_weight,
        out_weight,
        out_bias,
        up_weight,
        up_bias,
        snake_alpha,
        snake_beta,
        down_weight,
        down_bias,
    ) = stacked
    resnet_part = (
        conv_one[layer_index],
        conv_two[layer_index],
        res_weight[layer_index],
        norm_gain[layer_index],
        norm_bias[layer_index],
        time_weight[layer_index],
        time_bias[layer_index],
    )
    first_part = (layer_gain[layer_index, 0], layer_bias[layer_index, 0], qkv_weight[layer_index])
    later_part = (
        out_weight[layer_index],
        out_bias[layer_index],
        layer_gain[layer_index, 1],
        layer_bias[layer_index, 1],
        up_weight[layer_index],
        up_bias[layer_index],
        snake_alpha[layer_index],
        snake_beta[layer_index],
        down_weight[layer_index],
        down_bias[layer_index],
    )
    return (resnet_part, first_part, later_part)


def layer_grads(resnet_grads, first_grads, later_grads):
    gains = jnp.stack([first_grads[0], later_grads[2]])
    biases = jnp.stack([first_grads[1], later_grads[3]])
    return (
        resnet_grads
        + (gains, biases, first_grads[2], later_grads[0], later_grads[1])
        + later_grads[4:]
    )


def flatten_all(arrays):
    return jnp.concatenate([array_in.reshape(-1) for array_in in arrays])


def unflatten_all(flat, shapes):
    pieces = []
    offset_at = 0
    for shape_in in shapes:
        size_in = math.prod(shape_in)
        pieces.append(flat[offset_at : offset_at + size_in].reshape(shape_in))
        offset_at = offset_at + size_in
    return pieces


def frame_halo(value_in):
    return with_halo(value_in, (("seq", 1),), 1)


def rim_return(grad_padded):
    rim_rows = jnp.concatenate([grad_padded[:, :1], grad_padded[:, -1:]], axis=1)
    arrived = with_halo(rim_rows, (("seq", 1),), 1)
    inner_rows = grad_padded[:, 1:-1]
    inner_rows = inner_rows.at[:, 0].add(arrived[:, 0])
    return inner_rows.at[:, -1].add(arrived[:, 3])


def group_total(conv_out, mask_row):
    first_sum, second_sum = group_sums(conv_out, mask_row)
    return lax.psum((first_sum, second_sum), "seq")


def group_return(conv_out, mask_row, grad_first, grad_second):
    grad_first, grad_second = lax.psum((grad_first, grad_second), "seq")

    def sums_local(conv_in):
        return group_sums(conv_in, mask_row)

    pull_back = jax.vjp(sums_local, conv_out)[1]
    return pull_back((grad_first, grad_second))[0]


def resnet_forward(inputs, mask_row, counts, embedding, weights):
    conv_first, conv_second, res_weight, norm_gain, norm_bias, time_weight, time_bias = weights
    column = mask_row[:, :, None]
    masked = inputs * column
    padded_one = frame_halo(masked)
    first_conv = conv_piece(padded_one, conv_first)
    sums_one = group_total(first_conv, mask_row)
    hidden = group_apply(
        first_conv, sums_one[0], sums_one[1], counts, norm_gain[0], norm_bias[0], mask_row
    )
    hidden = hidden + time_piece(embedding, time_weight, time_bias)[:, None, :]
    padded_two = frame_halo(hidden * column)
    second = conv_piece(padded_two, conv_second)
    sums_two = group_total(second, mask_row)
    result = group_apply(
        second, sums_two[0], sums_two[1], counts, norm_gain[1], norm_bias[1], mask_row
    )
    result = result + jnp.einsum("ufc,cd->ufd", masked, res_weight, precision=precise)
    return (result, (masked, padded_one, first_conv, sums_one, padded_two, second, sums_two))


def resnet_backward(grad_out, saved, mask_row, counts, embedding, weights):
    conv_first, conv_second, res_weight, norm_gain, norm_bias, time_weight, time_bias = weights
    masked, padded_one, first_conv, sums_one, padded_two, second, sums_two = saved
    column = mask_row[:, :, None]

    def norm_local(conv_out, first_sum, second_sum, gain_vec, bias_vec):
        return group_apply(conv_out, first_sum, second_sum, counts, gain_vec, bias_vec, mask_row)

    pull_two = jax.vjp(norm_local, second, sums_two[0], sums_two[1], norm_gain[1], norm_bias[1])[1]
    grad_second, grad_first_sum, grad_second_sum, gain_grad_two, bias_grad_two = pull_two(grad_out)
    grad_second = grad_second + group_return(second, mask_row, grad_first_sum, grad_second_sum)
    grad_res = jnp.einsum("ufc,ufd->cd", masked, grad_out, precision=precise)
    grad_masked = jnp.einsum("ufd,cd->ufc", grad_out, res_weight, precision=precise)
    pull_conv = jax.vjp(conv_piece, padded_two, conv_second)[1]
    grad_padded, grad_conv_second = pull_conv(grad_second)
    grad_hidden = rim_return(grad_padded) * column

    def time_local(weight, bias_vec):
        return time_piece(embedding, weight, bias_vec)

    pull_time = jax.vjp(time_local, time_weight, time_bias)[1]
    grad_time_weight, grad_time_bias = pull_time(jnp.sum(grad_hidden, axis=1))
    pull_one = jax.vjp(
        norm_local, first_conv, sums_one[0], sums_one[1], norm_gain[0], norm_bias[0]
    )[1]
    grad_first, grad_first_sum, grad_second_sum, gain_grad_one, bias_grad_one = pull_one(
        grad_hidden
    )
    grad_first = grad_first + group_return(first_conv, mask_row, grad_first_sum, grad_second_sum)
    pull_conv = jax.vjp(conv_piece, padded_one, conv_first)[1]
    grad_padded, grad_conv_first = pull_conv(grad_first)
    grad_inputs = (rim_return(grad_padded) + grad_masked) * column
    grads = (
        grad_conv_first,
        grad_conv_second,
        grad_res,
        jnp.stack([gain_grad_one, gain_grad_two]),
        jnp.stack([bias_grad_one, bias_grad_two]),
        grad_time_weight,
        grad_time_bias,
    )
    return (grad_inputs, grads)


def block_forward(value_in, key_mask, first_weights, later_weights):
    queries, key_here, value_here = attend_in(
        value_in, first_weights[0], first_weights[1], first_weights[2]
    )
    key_full, value_full = (
        lax.all_gather(key_here, "seq", axis=1, tiled=True),
        lax.all_gather(value_here, "seq", axis=1, tiled=True),
    )
    result = attend_out(value_in, queries, key_full, value_full, key_mask, later_weights)
    kept_pair = (key_full, value_full)
    return (result, (value_in, queries, kept_pair))


def block_backward(grad_out, saved, key_mask, first_weights, later_weights):
    value_in, queries, kept_pair = saved
    key_full, value_full = kept_pair

    def attend_local(current, query_in, key_in, value_full_in, weights_in):
        return attend_out(current, query_in, key_in, value_full_in, key_mask, weights_in)

    pull_out = jax.vjp(attend_local, value_in, queries, key_full, value_full, later_weights)[1]
    grad_value, grad_queries, grad_keys, grad_values, grad_later = pull_out(grad_out)
    grad_keys, grad_values = (
        lax.psum_scatter(grad_keys, "seq", scatter_dimension=1, tiled=True),
        lax.psum_scatter(grad_values, "seq", scatter_dimension=1, tiled=True),
    )
    pull_in = jax.vjp(attend_in, value_in, first_weights[0], first_weights[1], first_weights[2])[1]
    grad_input, grad_gain, grad_bias, grad_qkv = pull_in((grad_queries, grad_keys, grad_values))
    return (grad_value + grad_input, (grad_gain, grad_bias, grad_qkv), grad_later)


def shrink_forward(value_in, mask_row, weight, bias_vec):
    masked = value_in * mask_row[:, :, None]
    carried = shifted(masked[:, -1:], "seq", 1)
    padded = jnp.concatenate([carried, masked], axis=1)
    return (shrink_piece(padded, weight, bias_vec), padded)


def shrink_backward(grad_out, padded, mask_row, weight, bias_vec):
    pull_back = jax.vjp(shrink_piece, padded, weight, bias_vec)[1]
    grad_padded, grad_weight, grad_bias = pull_back(grad_out)
    returned = shifted(grad_padded[:, :1], "seq", -1)
    grad_masked = grad_padded[:, 1:].at[:, -1:].add(returned)
    return (grad_masked * mask_row[:, :, None], grad_weight, grad_bias)


def general_local(
    frames,
    flow_embed,
    lengths,
    cotangent,
    conv_one,
    conv_two,
    res_weight,
    norm_gain,
    norm_bias,
    time_weight,
    time_bias,
    layer_gain,
    layer_bias,
    qkv_weight,
    out_weight,
    out_bias,
    up_weight,
    up_bias,
    snake_alpha,
    snake_beta,
    down_weight,
    down_bias,
    shrink_weight,
    shrink_bias,
):
    stacked = tuple(
        (
            weight_in.astype(jnp.float32)
            for weight_in in (
                conv_one,
                conv_two,
                res_weight,
                norm_gain,
                norm_bias,
                time_weight,
                time_bias,
                layer_gain,
                layer_bias,
                qkv_weight,
                out_weight,
                out_bias,
                up_weight,
                up_bias,
                snake_alpha,
                snake_beta,
                down_weight,
                down_bias,
            )
        )
    )
    shrink_w = shrink_weight.astype(jnp.float32)
    shrink_b = shrink_bias.astype(jnp.float32)
    seq_count = lax.axis_size("seq")
    seq_index = lax.axis_index("seq")
    frames_one = frames.shape[1]
    frames_two = frames_one // 2
    group_width = frames.shape[2] // GROUPS
    place_one = seq_index * frames_one + jnp.arange(frames_one, dtype=jnp.int32)
    place_two = seq_index * frames_two + jnp.arange(frames_two, dtype=jnp.int32)
    mask_one = (place_one[None, :] < lengths[:, None]).astype(jnp.float32)
    mask_two = (2 * place_two[None, :] < lengths[:, None]).astype(jnp.float32)
    keys_one = (
        jnp.arange(frames_one * seq_count, dtype=jnp.int32)[None, :] < lengths[:, None]
    ).astype(jnp.float32)
    keys_two = (
        2 * jnp.arange(frames_two * seq_count, dtype=jnp.int32)[None, :] < lengths[:, None]
    ).astype(jnp.float32)
    counts_one = (lengths * group_width).astype(jnp.float32)
    counts_two = ((lengths + 1) // 2 * group_width).astype(jnp.float32)
    res_zero, first_zero, later_zero = layer_weights(stacked, 0)
    res_one, first_one, later_one = layer_weights(stacked, 1)
    current, saved_first = resnet_forward(frames, mask_one, counts_one, flow_embed, res_zero)
    current, saved_second = block_forward(current, keys_one, first_zero, later_zero)
    current, saved_shrink = shrink_forward(current, mask_one, shrink_w, shrink_b)
    current, saved_third = resnet_forward(current, mask_two, counts_two, flow_embed, res_one)
    current, saved_fourth = block_forward(current, keys_two, first_one, later_one)
    output = current * mask_two[:, :, None]
    grad_now = cotangent * mask_two[:, :, None]
    grad_now, first_grads, later_grads = block_backward(
        grad_now, saved_fourth, keys_two, first_one, later_one
    )
    grad_now, resnet_grads = resnet_backward(
        grad_now, saved_third, mask_two, counts_two, flow_embed, res_one
    )
    grads_top = layer_grads(resnet_grads, first_grads, later_grads)
    shapes = [array_in.shape for array_in in grads_top]
    top_size = sum((math.prod(shape_in) for shape_in in shapes))
    grad_now, grad_shrink_w, grad_shrink_b = shrink_backward(
        grad_now, saved_shrink, mask_one, shrink_w, shrink_b
    )
    grad_now, first_grads, later_grads = block_backward(
        grad_now, saved_second, keys_one, first_zero, later_zero
    )
    grad_now, resnet_grads = resnet_backward(
        grad_now, saved_first, mask_one, counts_one, flow_embed, res_zero
    )
    grads_low = layer_grads(resnet_grads, first_grads, later_grads)
    low_flat = jnp.concatenate([flatten_all(grads_low), grad_shrink_w.reshape(-1), grad_shrink_b])
    summed_all = lax.psum(jnp.concatenate([flatten_all(grads_top), low_flat]), ("dp", "seq"))
    summed_top = summed_all[:top_size]
    summed_low = summed_all[top_size:]
    parts_top = unflatten_all(summed_top, shapes)
    parts_low = unflatten_all(summed_low, shapes + [shrink_w.shape, shrink_b.shape])
    grads_out = tuple(
        (jnp.stack([parts_low[number], parts_top[number]]) for number in range(len(shapes)))
    )
    return (output, grad_now) + grads_out + (parts_low[-2], parts_low[-1])


F32, BF = jnp.float32, jnp.bfloat16
MESH = pl.DeviceIdType.MESH
NN = (((1,), (0,)), ((), ()))
NT = (((1,), (1,)), ((), ()))
LOG2E = math.log2(math.e)
LN2 = math.log(2.0)
ANY = pl.BlockSpec(memory_space=pl.ANY)
WHOLE = pl.BlockSpec(memory_space=pltpu.VMEM)

SIN_SQUARE = (
    9.869604400158673,
    -32.46969664558586,
    42.72838511691944,
    -30.121754360183303,
    13.206610351651772,
    -3.913077711416514,
    0.7419801200174108,
)
SIN_TWICE = (
    6.283185302511503,
    -41.34170040531735,
    81.605131385789,
    -76.703015353733,
    42.025926985052664,
    -14.89984666534637,
    3.238137506736557,
)

UP, DOWN, OUT, LATER_SMALL = 0, 1024, 2048, 2176
BUCKET_ROWS = (2304, 3072, 2304, 1280, 1024)
BUCKET_AT = (0, 2304, 5376, 7680, 8960)
CORE_AT, CORE_ROWS = (0, 1152, 0, 2688, 3328), 3840
LATER_AT = (5376, 0)
CONV_TWO_AT = (7680, 2304)
RES_AT = (8448, 3072)
QUERY_KEY_AT = (8704, 3328)
CONV_ONE_AT = (8960, 3584)
VALUE_AT = (9728, 4352)
SMALL_AT = (9856, 4480)
SHRINK_AT, EMBED_AT = 4504, 5272


def pick(total, most):
    best = 16
    for size in range(16, most + 1, 16):
        if total % size == 0:
            best = size
    return best


def fits(shape, utterances, frames_in):
    return shape["seq"] == 2 * utterances and frames_in == 256 and shape["dp"] * utterances == 16


def split(value):
    high = value.astype(BF)
    return high, (value - high.astype(F32)).astype(BF)


def dot(left, right, dims=NN):
    return lax.dot_general(left, right, dims, preferred_element_type=F32)


def dot_weight(value, weight, dims=NN):
    rows = value.shape[0]
    both = dot(jnp.concatenate(split(value), 0), weight, dims)
    return both[:rows] + both[rows:]


def dot_pair(left, right):
    rows = left[0].shape[0]
    both = dot(jnp.concatenate(left, 0), right[0])
    return both[:rows] + both[rows:] + dot(left[0], right[1])


def fold8(value):
    return jnp.sum(value.reshape(value.shape[0] // 8, 8, value.shape[1]), axis=0)


def polynomial(coefficients, at):
    total = jnp.full_like(at, coefficients[-1])
    for number in coefficients[-2::-1]:
        total = total * at + number
    return total


def mish_terms(value):
    raised = jnp.exp(jnp.minimum(value, 20.0))
    top = raised * (raised + 2.0)
    return raised, top, 1.0 / (top + 2.0)


def mish_of(value):
    raised, top, inverse = mish_terms(value)
    return value * (top * inverse)


def mish_slope(value):
    raised, top, inverse = mish_terms(value)
    return inverse * (top + 4.0 * value * (raised * (raised + 1.0)) * inverse)


def loop(count, body):
    def step(index, carry):
        body(index)
        return carry

    lax.fori_loop(0, count, step, 0)


def at8(start, size):
    return pl.ds(pl.multiple_of(start, 8), size)


def at16(start, size):
    return pl.ds(pl.multiple_of(start, 16), size)


class Arguments(typing.NamedTuple):
    frames: Any
    flow_embed: Any
    lengths: Any
    cotangent: Any
    conv_one: Any
    conv_two: Any
    res_weight: Any
    norm_gain: Any
    norm_bias: Any
    time_weight: Any
    time_bias: Any
    layer_gain: Any
    layer_bias: Any
    qkv_weight: Any
    out_weight: Any
    out_bias: Any
    up_weight: Any
    up_bias: Any
    snake_alpha: Any
    snake_beta: Any
    down_weight: Any
    down_bias: Any
    shrink_weight: Any
    shrink_bias: Any


def matrices(found):
    return (
        found.conv_one,
        found.conv_two,
        found.res_weight,
        found.qkv_weight,
        found.out_weight,
        found.up_weight,
        found.down_weight,
        found.shrink_weight,
    )


def scratch_of(shape):
    depth = shape["seq"] // 2
    own_rows = (256 * depth, 128 * depth)

    def array(*size):
        return pltpu.VMEM(size, F32)

    def short(*size):
        return pltpu.VMEM(size, BF)

    def semaphores(*size):
        return pltpu.SemaphoreType.DMA(size)

    shared = dict(
        w_conv_one=short(2, 3, 256, 256),
        w_conv_two=short(2, 3, 256, 256),
        w_res_weight=short(2, 256, 256),
        w_qkv_weight=short(2, 256, 384),
        w_out_weight=short(2, 128, 256),
        w_up_weight=short(2, 256, 1024),
        w_down_weight=short(2, 1024, 256),
        w_shrink_weight=short(3, 256, 256),
        first=array(2, own_rows[0] + 64, 128),
        cot=array(own_rows[1], 256),
        last=array(own_rows[1], 256),
        dfirst=array(2, own_rows[0], 128),
        dy=array(own_rows[0], 256),
        dkr=array(own_rows[0], 256),
        dx=array(own_rows[0] + 32, 256),
        da=array(own_rows[1] + 32, 256),
        vt=short(2, own_rows[0], 256),
        dd=short(2, own_rows[0], 128),
        qq=short(2, own_rows[0], 128),
        tall=array(256, 4 * 256),
        wide=array(2 * depth, 256, 256),
        half=short(4 * depth, 256, 256),
        te=array(2, 8, 256),
        sums=array(8, 16, 256),
        sums_in=array(8, 16, 256),
        stat=array(4, 8, 256),
        narrow_acc=array(8, 8, 256),
        wide_acc=array(3, 8, 1024),
        gather=short(256, 256),
        grads=array(sum(BUCKET_ROWS), 256),
        core=array(CORE_ROWS, 256),
        s_weight=semaphores(16),
        s_frames=semaphores(4, depth),
        s_cot=semaphores(2, depth),
        s_last=semaphores(2, depth),
        s_grad=semaphores(2, depth),
        s_sums=semaphores(2, 8),
        s_kv=semaphores(4, depth),
        s_first=semaphores(2),
        s_dk=semaphores(4),
        s_dx=semaphores(4),
        s_total=semaphores(len(BUCKET_ROWS), 17),
    )
    layers = [
        dict(
            a=array(own + 32, 256),
            c1=array(own + 32, 256),
            h=array(own + 32, 256),
            c2=array(own + 32, 256),
            x=array(own, 256),
            att=array(own, 128),
            qh=short(2, own, 256),
            kv=array(2 * own, 256),
            kh=short(2, 2 * own, 256),
            vh=short(2, 2 * own, 256),
            kt=short(2, own // 128, 128, 256),
        )
        for own in own_rows
    ]
    arrivals = [
        dict(
            near=array(size // 4, 256),
            next=array(size // 8, 256),
            far=array(depth - 1, size // 32, 256),
        )
        for size in BUCKET_ROWS
    ]
    return [shared] + layers + arrivals


def named(groups, refs):
    found, at = [], 0
    for group in groups:
        found.append(SimpleNamespace(**dict(zip(group, refs[at : at + len(group)]))))
        at += len(group)
    return found


def fused_kernel(shape, groups, *refs):
    inputs = Arguments(*refs[:24])
    output, input_grad, grad_total = refs[24:27]
    r, *rest = named(groups, refs[27:])
    layers, arrivals = rest[:2], rest[2:]
    dp_count, seq_count = shape["dp"], shape["seq"]
    depth = seq_count // 2
    dp, seq = lax.axis_index("dp"), lax.axis_index("seq")
    member, place = lax.rem(seq, 2), lax.div(seq, 2)
    partner = seq + 1 - 2 * member
    half = depth
    own_rows = (256 * depth, 128 * depth)
    utterance = dp * depth + place
    length = inputs.lengths[place]
    lane128 = lax.broadcasted_iota(jnp.int32, (1, 128), 1)
    low_half = lane128 < 64

    def there(index):
        return {"dp": dp, "seq": index}

    def remote(source, target, sent, arrived, device):
        return pltpu.make_async_remote_copy(
            source, target, sent, arrived, device_id=device, device_id_type=MESH
        )

    held = (
        r.w_conv_one,
        r.w_conv_two,
        r.w_res_weight,
        r.w_qkv_weight,
        r.w_out_weight,
        r.w_up_weight,
        r.w_down_weight,
        r.w_shrink_weight,
    )
    weight_copies = [
        pltpu.make_async_copy(matrix, target, r.s_weight.at[number])
        for number, (matrix, target) in enumerate(zip(matrices(inputs), held))
    ]
    time_copies = []
    for layer in (0, 1):
        for part in range(4):
            time_copies.append(
                pltpu.make_async_copy(
                    inputs.time_weight.at[layer, pl.ds(256 * part, 256)],
                    r.half.at[4 * layer + part],
                    r.s_weight.at[len(held) + 4 * layer + part],
                )
            )
    for copy in time_copies + weight_copies:
        copy.start()

    def zero(ref, start, size):
        ref[pl.ds(start, size), :] = jnp.zeros((size, ref.shape[1]), F32)

    for mine, own in zip(layers, own_rows):
        for ref in (mine.a, mine.h, mine.c2):
            zero(ref, 0, 16)
            zero(ref, own + 16, 16)
    for part in (0, 1):
        zero(r.first.at[part], 0, 32)
        zero(r.first.at[part], own_rows[0] + 32, 32)
    zero(r.da, 0, 16)
    zero(r.da, own_rows[1] + 16, 16)
    for start in (0, own_rows[1] + 16, own_rows[0] + 16):
        zero(r.dx, start, 16)

    barrier = pltpu.get_barrier_semaphore()
    for step in range(1, seq_count):
        pl.semaphore_signal(
            barrier,
            inc=1,
            device_id=there(lax.rem(seq + step, seq_count)),
            device_id_type=MESH,
        )
    for step in range(1, dp_count):
        pl.semaphore_signal(
            barrier,
            inc=1,
            device_id={"dp": lax.rem(dp + step, dp_count), "seq": seq},
            device_id_type=MESH,
        )
    pl.semaphore_wait(barrier, seq_count - 1 + dp_count - 1)

    def spread(source_of, target_of, sems, item, target_seq, arrived_at):
        away = remote(
            source_of, target_of, sems.at[0, item], sems.at[1, arrived_at], there(target_seq)
        )
        here = pltpu.make_async_copy(source_of, target_of, sems.at[1, arrived_at])

        def start():
            @pl.when(target_seq != seq)
            def _():
                away.start()

            @pl.when(target_seq == seq)
            def _():
                here.start()

        def wait_sent():
            @pl.when(target_seq != seq)
            def _():
                away.wait_send()

        return start, wait_sent

    def wait_arrived(target, sems, index):
        pltpu.make_async_copy(target, target, sems.at[1, index]).wait()

    group_of_block = lax.div(seq, half)
    block_in_group = lax.rem(seq, half)
    frame_sends = []
    a0 = layers[0].a
    for item in range(depth):
        target = 2 * item + group_of_block
        frame_sends.append(
            spread(
                inputs.frames.at[item],
                a0.at[at16(16 + 256 * block_in_group, 256)],
                r.s_frames,
                item,
                target,
                block_in_group,
            )
        )
    for start, _ in frame_sends:
        start()
    edge_sems = r.s_frames
    edge_sends = []
    for item in range(depth):
        after = remote(
            inputs.frames.at[item, pl.ds(248, 8)],
            a0.at[pl.ds(8, 8)],
            edge_sems.at[2, item],
            edge_sems.at[3, 0],
            there(2 * item + 1),
        )
        before = remote(
            inputs.frames.at[item, pl.ds(0, 8)],
            a0.at[pl.ds(16 + own_rows[0], 8)],
            edge_sems.at[2, item],
            edge_sems.at[3, 0],
            there(2 * item),
        )
        after_here = pltpu.make_async_copy(
            inputs.frames.at[item, pl.ds(248, 8)], a0.at[pl.ds(8, 8)], edge_sems.at[3, 0]
        )
        before_here = pltpu.make_async_copy(
            inputs.frames.at[item, pl.ds(0, 8)],
            a0.at[pl.ds(16 + own_rows[0], 8)],
            edge_sems.at[3, 0],
        )
        edge_sends.append((after, before, after_here, before_here, item))
    sends_after = seq == half - 1
    sends_before = seq == half
    for after, before, after_here, before_here, item in edge_sends:

        @pl.when(sends_after & (seq != 2 * item + 1))
        def _(after=after):
            after.start()

        @pl.when(sends_after & (seq == 2 * item + 1))
        def _(after_here=after_here):
            after_here.start()

        @pl.when(sends_before & (seq != 2 * item))
        def _(before=before):
            before.start()

        @pl.when(sends_before & (seq == 2 * item))
        def _(before_here=before_here):
            before_here.start()

    def zero_grads(index):
        r.grads[at8(64 * index, 64), :] = jnp.zeros((64, 256), F32)

    loop(sum(BUCKET_ROWS) // 64, zero_grads)
    same_group = (
        lax.broadcasted_iota(jnp.int32, (256, 256), 0) // 32
        == lax.broadcasted_iota(jnp.int32, (256, 256), 1) // 32
    )
    r.gather[...] = jnp.where(same_group, 1.0, 0.0).astype(BF)
    for copy in time_copies:
        copy.wait()
    embedded = mish_of(inputs.flow_embed[pl.ds(place, 1), :])
    wide_embed = jnp.broadcast_to(embedded, (16, 1024))
    time_bias = inputs.time_bias[...].astype(F32)
    for layer in (0, 1):
        weight = jnp.concatenate([r.half[4 * layer + part] for part in range(4)], 0)
        projected = dot_weight(wide_embed, weight)
        r.te[layer] = projected[:8] + time_bias[layer : layer + 1]
    row16 = lax.broadcasted_iota(jnp.int32, (16, 256), 0)
    for part in range(4):
        chosen = jnp.where(
            row16 == utterance + 64 * member, embedded[:, 256 * part : 256 * part + 256], 0.0
        )
        r.grads[pl.ds(EMBED_AT + 16 * part, 16), :] = chosen
    for copy in weight_copies:
        copy.wait()

    def valid_rows(start, rows, layer):
        at = lax.broadcasted_iota(jnp.int32, (rows, 256), 0) + (start - 16)
        frame = at + member * own_rows[layer]
        valid = (frame >= 0) & (frame * (1 + layer) < length)
        return valid, valid & (at >= 0) & (at < own_rows[layer])

    def conv_block(source, start, rows, taps, dims=NN):
        value = source[at8(start, rows + 16), :]
        both = jnp.concatenate(split(value), 0)
        total = None
        for tap, weight in enumerate(taps):
            part = dot(both, weight, dims)
            part = part[: rows + 16] + part[rows + 16 :]
            part = part[7 + tap : 7 + tap + rows]
            total = part if total is None else total + part
        return total

    def send_sums(number):
        copy = remote(
            r.sums.at[number],
            r.sums_in.at[number],
            r.s_sums.at[0, number],
            r.s_sums.at[1, number],
            there(partner),
        )
        copy.start()
        return copy

    def group_total(value):
        high = value.astype(BF)
        rest = value - high.astype(F32)
        middle = rest.astype(BF)
        last = (rest - middle.astype(F32)).astype(BF)
        parts = dot(jnp.concatenate([high, middle, last], 0), r.gather[...])
        total = parts[0:16] + parts[16:32] + parts[32:48]
        return (
            jnp.sum(total[0:8], axis=0, keepdims=True),
            jnp.sum(total[8:16], axis=0, keepdims=True),
        )

    counts = (
        (length * 32).astype(F32),
        (lax.div(length + 1, 2) * 32).astype(F32),
    )

    def forward_sums(layer, which, copy):
        number = 2 * layer + which
        copy.wait()
        first_sum, second_sum = group_total(r.sums[number] + r.sums_in[number])
        mean = first_sum / counts[layer]
        variance = second_sum / counts[layer] - mean * mean
        r.stat[number, 0:1, :] = mean
        r.stat[number, 1:2, :] = lax.rsqrt(variance + epsilon)

    def norm_rows(layer, which):
        number = 2 * layer + which
        gain = inputs.norm_gain[...].astype(F32)[layer, which : which + 1]
        bias = inputs.norm_bias[...].astype(F32)[layer, which : which + 1]
        return r.stat[number, 0:1, :], r.stat[number, 1:2, :], gain, bias

    def add_sums(number, first, second):
        r.sums[number, 0:8, :] += fold8(first)
        r.sums[number, 8:16, :] += fold8(second)

    def clear_sums(number):
        r.sums[number] = jnp.zeros((16, 256), F32)

    def normed_layer(value):
        mean = jnp.mean(value, axis=1, keepdims=True)
        centered = value - mean
        variance = jnp.mean(centered * centered, axis=1, keepdims=True)
        scale = lax.rsqrt(variance + epsilon)
        return centered * scale, scale

    def normed_back(grad, normed, scale):
        return scale * (
            grad
            - jnp.mean(grad, axis=1, keepdims=True)
            - normed * jnp.mean(grad * normed, axis=1, keepdims=True)
        )

    def layer_rows(layer, which):
        gain = inputs.layer_gain[...].astype(F32)[layer, which : which + 1]
        bias = inputs.layer_bias[...].astype(F32)[layer, which : which + 1]
        return gain, bias

    def row_of(ref, layer):
        return ref[...].astype(F32)[layer : layer + 1]

    def keys_aux(start, rows, layer):
        lane = lax.broadcasted_iota(jnp.int32, (rows, 128), 1)
        key = lax.broadcasted_iota(jnp.int32, (rows, 128), 0) + start
        masked = jnp.where(key * (1 + layer) < length, 0.0, -1e30)
        ones = jnp.where((lane >= 65) & (lane < 68), 1.0, 0.0)
        return jnp.where(lane == 64, masked, ones)

    def both_heads(value):
        high = value.astype(BF).astype(F32)
        low = value - high
        return high, low, pltpu.roll(high, 64, 1), pltpu.roll(low, 64, 1)

    def key_tiles(value, aux):
        high, low, high_turned, low_turned = both_heads(value)
        tiles = (
            (jnp.where(low_half, high, low_turned), jnp.where(low_half, high, aux)),
            (jnp.where(low_half, high_turned, low), jnp.where(low_half, high_turned, aux)),
        )
        return [(a.astype(BF), b.astype(BF)) for a, b in tiles]

    def query_tiles(value, aux):
        high, low, high_turned, low_turned = both_heads(value)
        tiles = (
            (jnp.where(low_half, high, high_turned), jnp.where(low_half, low, aux[0])),
            (jnp.where(low_half, high_turned, high), jnp.where(low_half, low_turned, aux[1])),
        )
        return [(a.astype(BF), b.astype(BF)) for a, b in tiles]

    def three_lanes(value, first):
        lane = lax.broadcasted_iota(jnp.int32, value.shape, 1)
        high = value.astype(BF).astype(F32)
        rest = value - high
        middle = rest.astype(BF).astype(F32)
        spread_out = jnp.where(lane == 66, middle, rest - middle)
        spread_out = jnp.where(lane == 65, high, spread_out)
        spread_out = jnp.where(lane == 64, first, spread_out)
        return jnp.where((lane >= 64) & (lane < 68), spread_out, 0.0)

    def res_forward(layer):
        own = own_rows[layer]
        extended = own + 16
        rows = pick(extended, 256)
        small = pick(extended, 96)
        a, c1, h, c2 = layers[layer].a, layers[layer].c1, layers[layer].h, layers[layer].c2

        def convolve(source, target, weights, number):
            clear_sums(number)

            def block(index):
                out = conv_block(source, rows * index, rows, [weights[layer, k] for k in range(3)])
                start = rows * index + 8
                target[at8(start, rows), :] = out
                kept = jnp.where(valid_rows(start, rows, layer)[1], out, 0.0)
                add_sums(number, kept, kept * out)

            loop(extended // rows, block)
            return send_sums(number)

        copy = convolve(a, c1, r.w_conv_one, 2 * layer)
        forward_sums(layer, 0, copy)
        mean, scale, gain, bias = norm_rows(layer, 0)
        added = r.te[layer, 0:1, :]

        def normed(index):
            start = small * index + 8
            value = (c1[at8(start, small), :] - mean) * scale * gain + bias
            valid = valid_rows(start, small, layer)[0]
            h[at8(start, small), :] = jnp.where(valid, mish_of(value) + added, 0.0)

        loop(extended // small, normed)
        copy = convolve(h, c2, r.w_conv_two, 2 * layer + 1)
        forward_sums(layer, 1, copy)

    def kv_copy(layer, index):
        own = own_rows[layer]
        part = layers[layer].kv.at[at16(member * own + 256 * index, 256)]
        return remote(
            part,
            part,
            r.s_kv.at[2 * layer, index],
            r.s_kv.at[2 * layer + 1, index],
            there(partner),
        )

    def qkv_forward(layer):
        own = own_rows[layer]
        a, c2, x, kv, qh = layers[layer].a, layers[layer].c2, layers[layer].x, layers[layer].kv, layers[layer].qh
        mean, scale, gain, bias = norm_rows(layer, 1)
        layer_gain, layer_bias = layer_rows(layer, 0)
        lane = lax.broadcasted_iota(jnp.int32, (256, 128), 1)
        aux = jnp.where(lane == 64, 1.0, 0.0)

        def block(index):
            start = 256 * index
            value = (c2[at16(start + 16, 256), :] - mean) * scale * gain + bias
            valid = valid_rows(start + 16, 256, layer)[0]
            out = jnp.where(valid, mish_of(value), 0.0)
            out = out + dot_weight(a[at16(start + 16, 256), :], r.w_res_weight[layer])
            x[at16(start, 256), :] = out
            packed = dot_weight(
                normed_layer(out)[0] * layer_gain + layer_bias, r.w_qkv_weight[layer]
            )
            kv[at16(member * own + start, 256), :] = packed[:, 128:]
            kv_copy(layer, index).start()
            tiles = query_tiles(packed[:, :128] * (LOG2E / 8.0), (aux, aux))
            for head in (0, 1):
                qh[head, at16(start, 256), 0:128] = tiles[head][0]
                qh[head, at16(start, 256), 128:256] = tiles[head][1]

        loop(own // 256, block)

    def keys_forward(layer):
        own = own_rows[layer]
        kv, kh, vh, kt, vt = layers[layer].kv, layers[layer].kh, layers[layer].vh, layers[layer].kt, r.vt
        for index in range(own // 256):
            kv_copy(layer, index).wait()

        def block(index):
            start = 256 * index
            value = kv[at16(start, 256), :]
            aux = keys_aux(start, 256, layer)
            for part, target in ((value[:, :128], kh), (value[:, 128:], vh)):
                tiles = key_tiles(part, aux)
                for head in (0, 1):
                    target[head, at16(start, 256), 0:128] = tiles[head][0]
                    target[head, at16(start, 256), 128:256] = tiles[head][1]
            for column in (0, 128):
                high, low = split(jnp.transpose(value[:, column : column + 128]))
                for head in (0, 1):
                    both = jnp.concatenate([high[64 * head : 64 * head + 64], low[64 * head : 64 * head + 64]], 0)
                    if column == 0:
                        kt[head, index] = both
                    else:
                        vt[head, at16(128 * index, 128), :] = both

        loop(2 * own // 256, block)

    def snake_rows(layer):
        alpha = jnp.exp(row_of(inputs.snake_alpha, layer))
        beta = jnp.exp(row_of(inputs.snake_beta, layer))
        return alpha, beta, 1.0 / (beta + 1e-9)

    def later_forward(layer):
        own = own_rows[layer]
        x, att, kh, qh, vt = layers[layer].x, layers[layer].att, layers[layer].kh, layers[layer].qh, r.vt
        wide, part16 = r.wide, r.half
        blocks = 2 * own // 256
        gain, bias = layer_rows(layer, 1)
        out_bias, down_bias, up_bias = row_of(inputs.out_bias, layer), row_of(inputs.down_bias, layer), row_of(inputs.up_bias, layer)
        alpha, beta, inverse = snake_rows(layer)
        turns = alpha * (1.0 / math.pi)

        def block(index):
            start = 256 * index
            attended = []
            for head in (0, 1):
                query = qh[head, at16(start, 256), :]

                most = jnp.full((8, 256), -3e38, F32)
                for key in range(blocks):
                    out = dot(kh[head, 256 * key : 256 * key + 256, :], query, NT)
                    wide[key] = out
                    most = jnp.maximum(most, jnp.max(out.reshape(32, 8, 256), axis=0))
                most = jnp.max(most, axis=0, keepdims=True)
                total = jnp.zeros((8, 256), F32)
                for key in range(blocks):
                    for piece in range(4):
                        rows = pl.ds(64 * piece, 64)
                        raised = jnp.exp2(wide[key, rows, :] - most)
                        total = total + fold8(raised)
                        high, low = split(raised)
                        part16[key, rows, :] = high
                        part16[blocks + key, rows, :] = low
                total = jnp.sum(total, axis=0, keepdims=True)
                values = jnp.concatenate([vt[head, 128 * key : 128 * key + 128, :] for key in range(blocks)], 1)
                out = dot(values, jnp.concatenate([part16[key] for key in range(blocks)], 0))
                out = out + dot(values, jnp.concatenate([part16[blocks + key] for key in range(blocks)], 0))
                attended.append((out[:64] + out[64:]) * (1.0 / total))
                level = jnp.transpose(jnp.broadcast_to(most + jnp.log2(total), (128, 256)))
                aux = three_lanes(-level, 1.0)
                old = qh[head, at16(start, 256), 128:256]
                qh[head, at16(start, 256), 128:256] = jnp.where(low_half, old, aux.astype(BF))
            joined = jnp.transpose(jnp.concatenate(attended, 0))
            att[at16(start, 256), :] = joined
            y = x[at16(start, 256), :] + dot_weight(joined, r.w_out_weight[layer]) + out_bias
            lifted = dot_weight(normed_layer(y)[0] * gain + bias, r.w_up_weight[layer])
            for column in range(4):
                wide[column] = lifted[:, 256 * column : 256 * column + 256]
            for column in range(4):
                lanes = slice(256 * column, 256 * column + 256)

                def snake(piece, column=column, lanes=lanes):
                    rows = pl.ds(64 * piece, 64)
                    z = wide[column, rows, :] + up_bias[:, lanes]
                    turn = z * turns[:, lanes]
                    turn = turn - jnp.round(turn)
                    square = turn * turn
                    s = z + square * polynomial(SIN_SQUARE, square) * inverse[:, lanes]
                    high, low = split(s)
                    part16[column, rows, :] = high
                    part16[4 + column, rows, :] = low

                for piece in range(4):
                    snake(piece)
            both = jnp.concatenate(
                [jnp.concatenate([part16[4 * part + column] for column in range(4)], 1) for part in (0, 1)], 0
            )
            lowered = dot(both, r.w_down_weight[layer])
            out = y + lowered[:256] + lowered[256:] + down_bias
            out = jnp.where(valid_rows(start + 16, 256, layer)[0], out, 0.0)
            if layer == 0:
                for lanes in (0, 1):
                    r.first[lanes, at16(start + 32, 256), :] = out[:, 128 * lanes : 128 * lanes + 128]
            else:
                r.last[at16(start, 256), :] = out

        loop(own // 256, block)

    def shrink_forward_part():
        own = own_rows[0]
        first = r.first
        source = pl.multiple_of((1 - member) * (16 + own) + member * 32, 16)
        target = pl.multiple_of((1 - member) * 16 + member * (32 + own), 16)
        copy = remote(
            first.at[:, pl.ds(source, 16), :],
            first.at[:, pl.ds(target, 16), :],
            r.s_first.at[0],
            r.s_first.at[1],
            there(partner),
        )
        copy.start()
        copy.wait()
        extended = own_rows[1] + 16
        rows = pick(extended, 256)
        bias = inputs.shrink_bias[...].astype(F32).reshape(1, 256)

        def block(index):
            start = rows * index + 8
            total = bias
            for tap in range(3):
                taken = taken_rows(start - 16, rows, tap)
                total = total + dot_weight(taken, r.w_shrink_weight[tap])
            valid = valid_rows(start, rows, 1)[0]
            layers[1].a[at8(start, rows), :] = jnp.where(valid, total, 0.0)

        loop(extended // rows, block)

    def taken_rows(row, rows, tap):
        at = 32 + 2 * row - 1 + tap
        return jnp.concatenate([r.first[lanes, pl.ds(at, rows, stride=2), :] for lanes in (0, 1)], 1)

    def clear_layer():
        r.narrow_acc[...] = jnp.zeros((8, 8, 256), F32)
        r.wide_acc[...] = jnp.zeros((3, 8, 1024), F32)

    def later_backward(layer, advances={}):
        own = own_rows[layer]
        base = LATER_AT[layer]
        x, att, qh = layers[layer].x, layers[layer].att, layers[layer].qh
        wide, part16, grads = r.wide, r.half, r.grads
        doh = r.vt
        gain, bias = layer_rows(layer, 1)
        out_bias, up_bias = row_of(inputs.out_bias, layer), row_of(inputs.up_bias, layer)
        alpha, beta, inverse = snake_rows(layer)
        turns = alpha * (1.0 / math.pi)
        slope = alpha * inverse
        r.tall[...] = jnp.zeros((256, 1024), F32)
        clear_layer()
        narrow, broad = r.narrow_acc, r.wide_acc

        def block(index):
            start = 256 * index
            if layer == 0:
                dout = jnp.concatenate([r.dfirst[lanes, at16(start, 256), :] for lanes in (0, 1)], 1)
            else:
                dout = r.cot[at16(start, 256), :]
            joined = att[at16(start, 256), :]
            y = x[at16(start, 256), :] + dot_weight(joined, r.w_out_weight[layer]) + out_bias
            normed, scale = normed_layer(y)
            entered = normed * gain + bias
            lifted = dot_weight(entered, r.w_up_weight[layer])
            for column in range(4):
                wide[column] = lifted[:, 256 * column : 256 * column + 256]
            risen = dot_weight(dout, r.w_down_weight[layer], NT)
            for column in range(4):
                wide[4 + column] = risen[:, 256 * column : 256 * column + 256]
            for column in range(4):
                lanes = slice(256 * column, 256 * column + 256)

                dz_sum = turn_sum = sine_sum = jnp.zeros((8, 256), F32)
                for piece in range(8):
                    rows = pl.ds(32 * piece, 32)
                    z = wide[column, rows, :] + up_bias[:, lanes]
                    ds = wide[4 + column, rows, :]
                    whole = z * turns[:, lanes]
                    turn = whole - jnp.round(whole)
                    square = turn * turn
                    sine2 = square * polynomial(SIN_SQUARE, square)
                    twice = turn * polynomial(SIN_TWICE, square)
                    s = z + sine2 * inverse[:, lanes]
                    dtwice = ds * twice
                    dz = ds + dtwice * slope[:, lanes]
                    dz_sum += fold8(dz)
                    turn_sum += fold8(dtwice * whole)
                    sine_sum += fold8(ds * sine2)
                    high, low = split(s)
                    part16[column, rows, :] = high
                    part16[4 + column, rows, :] = low
                    high, low = split(dz)
                    part16[8 + column, rows, :] = high
                    part16[12 + column, rows, :] = low
                broad[0, :, lanes] += dz_sum
                broad[1, :, lanes] += turn_sum
                broad[2, :, lanes] += sine_sum

            def gathered(number):
                return jnp.concatenate([part16[number + column] for column in range(4)], 1)

            r.tall[...] += dot_pair(split(jnp.transpose(dout)), (gathered(0), gathered(4)))
            raised = dot_pair(split(jnp.transpose(entered)), (gathered(8), gathered(12)))
            for column in range(4):
                grads[pl.ds(base + UP + 256 * column, 256), :] += raised[:, 256 * column : 256 * column + 256]
            both = dot(jnp.concatenate([gathered(8), gathered(12)], 0), r.w_up_weight[layer], NT)
            dentered = both[:256] + both[256:]
            dy = dout + normed_back(dentered * gain, normed, scale)
            r.dy[at16(start, 256), :] = dy
            narrow[0] += fold8(dout)
            narrow[1] += fold8(dy)
            narrow[2] += fold8(dentered * normed)
            narrow[3] += fold8(dentered)
            grads[pl.ds(base + OUT, 128), :] += dot_pair(split(jnp.transpose(joined)), split(dy))
            datt = dot_weight(dy, r.w_out_weight[layer], NT)
            product = datt * joined
            sums = [
                jnp.sum(jnp.where(low_half, product, 0.0), axis=1, keepdims=True),
                jnp.sum(jnp.where(low_half, 0.0, product), axis=1, keepdims=True),
            ]
            aux = [three_lanes(jnp.broadcast_to(-total, (256, 128)), 0.0) for total in sums]
            tiles = query_tiles(datt, aux)
            pairs = key_tiles(datt, aux[0])
            for head in (0, 1):
                doh[head, at16(start, 256), 0:128] = tiles[head][0]
                doh[head, at16(start, 256), 128:256] = tiles[head][1]
                r.dd[head, at16(start, 256), :] = pairs[head][0]
                query = qh[head, at16(start, 256), 0:128].astype(F32)
                rest = pltpu.roll(qh[head, at16(start, 256), 128:256].astype(F32), 64, 1)
                r.qq[head, at16(start, 256), :] = jnp.where(low_half, query, rest).astype(BF)

        loop_with(own // 256, block, advances)

        def turn_down(index):
            taken = r.tall[:, pl.ds(pl.multiple_of(256 * index, 256), 256)]
            grads[at16(base + DOWN + 256 * index, 256), :] = jnp.transpose(taken)

        loop(4, turn_down)
        small = base + LATER_SMALL
        for number in range(4):
            grads[pl.ds(small + number, 1), :] = jnp.sum(narrow[number], axis=0, keepdims=True)
        bias_row = jnp.sum(broad[0], axis=0, keepdims=True)
        alpha_row = jnp.sum(broad[1], axis=0, keepdims=True) * (math.pi * inverse)
        beta_row = jnp.sum(broad[2], axis=0, keepdims=True) * (-beta * inverse * inverse)
        for number, row in enumerate((bias_row, alpha_row, beta_row)):
            for column in range(4):
                grads[pl.ds(small + 4 + 4 * number + column, 1), :] = row[:, 256 * column : 256 * column + 256]

    def dk_copy(layer):
        own = own_rows[layer]
        return remote(
            layers[layer].kv.at[at16((1 - member) * own, own)],
            r.dkr.at[pl.ds(0, own)],
            r.s_dk.at[2 * layer],
            r.s_dk.at[2 * layer + 1],
            there(partner),
        )

    def attend_backward(layer, advances={}, more={}):
        own = own_rows[layer]
        kh, vh, qh, kt, dkv = layers[layer].kh, layers[layer].vh, layers[layer].qh, layers[layer].kt, layers[layer].kv
        doh, dd, qq, part16 = r.vt, r.dd, r.qq, r.half
        blocks, queries = 2 * own // 256, own // 256
        for head in (0, 1):
            r.tall[pl.ds(128 * head, 128), 0:own] = jnp.zeros((128, own), F32)

        def block(index):
            key = lax.rem((1 - member) * queries + index, blocks)
            found = []
            for head in (0, 1):
                keys = kh[head, at16(256 * key, 256), :]
                values = vh[head, at16(256 * key, 256), :]
                for query in range(queries):
                    rows = pl.ds(256 * query, 256)
                    weights = jnp.exp2(dot(keys, qh[head, rows, :], NT))
                    grad = weights * dot(values, doh[head, rows, :], NT)
                    high, low = split(weights)
                    part16[query] = high
                    part16[4 + query] = low
                    high, low = split(grad)
                    part16[8 + query] = high
                    part16[12 + query] = low

                def gathered(number):
                    return jnp.concatenate([part16[number + query] for query in range(queries)], 1)

                dscores, dscores_rest = gathered(8), gathered(12)
                both = dot(jnp.concatenate([gathered(0), gathered(4)], 0), dd[head, 0:own, :])
                dvalue = both[:256] + both[256:]
                both = dot(jnp.concatenate([dscores, dscores_rest], 0), qq[head, 0:own, :])
                dkey = both[:256] + both[256:]
                found.append((dkey, dvalue))
                r.tall[pl.ds(128 * head, 128), 0:own] += dot(kt[head, key], dscores) + dot(kt[head, key], dscores_rest)
            for column, part in ((0, 0), (128, 1)):
                zeroth = found[0][part] + pltpu.roll(found[0][part], 64, 1)
                other = found[1][part] + pltpu.roll(found[1][part], 64, 1)
                joined = jnp.where(low_half, zeroth, other)
                if part == 0:
                    joined = joined * LN2
                dkv[at16(256 * key, 256), column : column + 128] = joined

        loop_with(queries, block, advances)
        copy = dk_copy(layer)
        copy.start()
        loop_with(queries, lambda index: block(index + queries), more)
        copy.wait()

    def qkv_backward(layer, advances={}):
        own = own_rows[layer]
        x, c2, dkv, dkr = layers[layer].x, layers[layer].c2, layers[layer].kv, r.dkr
        grads, narrow = r.grads, r.narrow_acc
        gain, bias = layer_rows(layer, 0)
        mean2, scale2, gain2, bias2 = norm_rows(layer, 1)
        number = 4 + 2 * layer
        clear_sums(number)

        def block(index):
            start = 256 * index
            lanes = pl.ds(pl.multiple_of(start, 256), 256)
            dquery = [r.tall[pl.ds(128 * head, 64), lanes] + r.tall[pl.ds(128 * head + 64, 64), lanes] for head in (0, 1)]
            dquery = jnp.transpose(jnp.concatenate(dquery, 0)) * 0.125
            dkeys = dkv[at16(member * own + start, 256), :] + dkr[at16(start, 256), :]
            packed = jnp.concatenate([dquery, dkeys], 1)
            normed, scale = normed_layer(x[at16(start, 256), :])
            entered = normed * gain + bias
            weight = dot_pair(split(jnp.transpose(entered)), split(packed))
            grads[pl.ds(QUERY_KEY_AT[layer], 256), :] += weight[:, :256]
            grads[pl.ds(VALUE_AT[layer], 128), 0:128] += weight[:128, 256:]
            grads[pl.ds(VALUE_AT[layer], 128), 128:256] += weight[128:, 256:]
            dentered = dot_weight(packed, r.w_qkv_weight[layer], NT)
            narrow[4] += fold8(dentered * normed)
            narrow[5] += fold8(dentered)
            dx = r.dy[at16(start, 256), :] + normed_back(dentered * gain, normed, scale)
            r.dx[at16(start + 16, 256), :] = dx
            unit = (c2[at16(start + 16, 256), :] - mean2) * scale2
            dvalue = dx * mish_slope(unit * gain2 + bias2)
            add_sums(number, dvalue, dvalue * unit)

        loop_with(own // 256, block, advances)
        for row in (4, 5):
            grads[pl.ds(SMALL_AT[layer] + row, 1), :] = jnp.sum(narrow[row], axis=0, keepdims=True)
        copy = send_sums(number)
        source = pl.multiple_of((1 - member) * (8 + own) + member * 16, 8)
        target = pl.multiple_of((1 - member) * 8 + member * (16 + own), 8)
        edge = remote(
            r.dx.at[pl.ds(source, 8)],
            r.dx.at[pl.ds(target, 8)],
            r.s_dx.at[2 * layer],
            r.s_dx.at[2 * layer + 1],
            there(partner),
        )
        edge.start()
        return copy, edge

    def norm_back(layer, which, copy):
        number = 4 + 2 * layer + (1 - which)
        base = SMALL_AT[layer]
        copy.wait()
        mean, scale, gain, bias = norm_rows(layer, which)
        mine = r.sums[number]
        r.grads[pl.ds(base + 2 + which, 1), :] = jnp.sum(mine[0:8], axis=0, keepdims=True)
        r.grads[pl.ds(base + which, 1), :] = jnp.sum(mine[8:16], axis=0, keepdims=True)
        from_bias, from_gain = group_total((mine + r.sums_in[number]) * gain)
        return mean, scale, gain, bias, from_bias / counts[layer], from_gain / counts[layer]

    def weight_rows(at, taken, grad):
        left = [split(jnp.transpose(value)) for value in taken]
        high = jnp.concatenate([pair[0] for pair in left], 0)
        low = jnp.concatenate([pair[1] for pair in left], 0)
        r.grads[pl.ds(at, 256 * len(taken)), :] += dot_pair((high, low), split(grad))

    def conv_weight(source, target, own, at):
        def block(index):
            value = source[at8(256 * index + 8, 272), :]
            grad = target[at16(256 * index + 16, 256), :]
            weight_rows(at, [value[7 + tap : 263 + tap] for tap in range(3)], grad)

        loop(own // 256, block)

    def res_backward(layer, copies, advances=((), ())):
        own = own_rows[layer]
        extended = own + 16
        rows, small = pick(extended, 256), pick(extended, 96)
        a, c1, h, c2 = layers[layer].a, layers[layer].c1, layers[layer].h, layers[layer].c2
        dx, dv = r.dx, layers[0].kv
        copy, edge = copies
        edge.wait()
        zero(dv, 0, 16)
        zero(dv, own + 16, 16)
        mean, scale, gain, bias, from_bias, from_gain = norm_back(layer, 1, copy)

        def second(index):
            start = small * index + 8
            unit = (c2[at8(start, small), :] - mean) * scale
            grad = dx[at8(start, small), :] * mish_slope(unit * gain + bias)
            out = scale * (gain * grad - (from_bias + unit * from_gain))
            c2[at8(start, small), :] = jnp.where(valid_rows(start, small, layer)[0], out, 0.0)

        loop(extended // small, second)
        mean1, scale1, gain1, bias1 = norm_rows(layer, 0)
        number = 5 + 2 * layer
        clear_sums(number)
        r.narrow_acc[6] = jnp.zeros((8, 256), F32)

        def hidden(index):
            start = rows * index + 8
            taps = [r.w_conv_two[layer, 2 - tap] for tap in range(3)]
            out = conv_block(c2, rows * index, rows, taps, NT)
            valid, mine = valid_rows(start, rows, layer)
            out = jnp.where(valid, out, 0.0)
            unit = (c1[at8(start, rows), :] - mean1) * scale1
            grad = out * mish_slope(unit * gain1 + bias1)
            dv[at8(start, rows), :] = grad
            r.narrow_acc[6] += fold8(jnp.where(mine, out, 0.0))
            grad = jnp.where(mine, grad, 0.0)
            add_sums(number, grad, grad * unit)

        loop(extended // rows, hidden)
        copy = send_sums(number)
        conv_weight(h, c2, own, CONV_TWO_AT[layer])

        def res_part(index):
            value = a[at16(256 * index + 16, 256), :]
            weight_rows(RES_AT[layer], [value], dx[at16(256 * index + 16, 256), :])

        loop(own // 256, res_part)
        advance(*advances[0])
        summed = jnp.sum(r.narrow_acc[6], axis=0, keepdims=True)
        r.grads[pl.ds(SMALL_AT[layer] + 8, 16), :] = jnp.where(row16 == utterance, summed, 0.0)
        mean, scale, gain, bias, from_bias, from_gain = norm_back(layer, 0, copy)

        def first_part(index):
            start = small * index + 8
            unit = (c1[at8(start, small), :] - mean) * scale
            out = scale * (gain * dv[at8(start, small), :] - (from_bias + unit * from_gain))
            dv[at8(start, small), :] = jnp.where(valid_rows(start, small, layer)[0], out, 0.0)

        loop(extended // small, first_part)
        taps = [r.w_conv_one[layer, 2 - tap] for tap in range(3)]

        def inputs(start, size):
            out = conv_block(dv, start, size, taps, NT)
            out = out + dot_weight(dx[at8(start + 8, size), :], r.w_res_weight[layer], NT)
            return jnp.where(valid_rows(start + 8, size, layer)[0], out, 0.0)

        if layer == 1:

            def block(index):
                r.da[at8(rows * index + 8, rows), :] = inputs(rows * index, rows)

            loop(extended // rows, block)
        else:

            def block(index):
                r.dy[at16(256 * index, 256), :] = inputs(256 * index + 8, 256)

            loop(own // 256, block)
            send_blocks(r.dy, 256, input_grad, r.s_grad)
        advance(*advances[1])
        conv_weight(a, dv, own, CONV_ONE_AT[layer])

    def shrink_backward_part():
        da, own = r.da, own_rows[1]
        acc = r.narrow_acc
        acc[7] = jnp.zeros((8, 256), F32)

        def block(index):
            value = da[at16(128 * index + 16, 144), :]
            both = jnp.concatenate(split(value), 0)
            parts = [dot(both, r.w_shrink_weight[tap], NT) for tap in range(3)]
            parts = [part[:144] + part[144:] for part in parts]
            even = parts[1][:128]
            odd = parts[2][:128] + parts[0][1:129]
            at = lax.broadcasted_iota(jnp.int32, (128, 256), 0) + 128 * index
            frame = 2 * (at + member * own)
            even = jnp.where(frame < length, even, 0.0)
            odd = jnp.where(frame + 1 < length, odd, 0.0)
            for lanes in (0, 1):
                columns = slice(128 * lanes, 128 * lanes + 128)
                r.dfirst[lanes, pl.ds(256 * index, 128, stride=2), :] = even[:, columns]
                r.dfirst[lanes, pl.ds(256 * index + 1, 128, stride=2), :] = odd[:, columns]
            acc[7] += fold8(value[:128])

        loop(own // 128, block)

        def weights(index):
            grad = da[at16(256 * index + 16, 256), :]
            weight_rows(SHRINK_AT, [taken_rows(256 * index, 256, tap) for tap in range(3)], grad)

        loop(own // 256, weights)
        r.grads[pl.ds(SMALL_AT[1] + 6, 1), :] = jnp.sum(acc[7], axis=0, keepdims=True)

    def block_sends(source, size, target, sems):
        return [
            spread(
                source.at[pl.ds(size * item, size)],
                target.at[place],
                sems,
                item,
                half * member + item,
                place,
            )
            for item in range(half)
        ]

    def send_blocks(source, size, target, sems):
        for start, _ in block_sends(source, size, target, sems):
            start()

    def finish_blocks(source, size, target, sems):
        for _, wait_sent in block_sends(source, size, target, sems):
            wait_sent()
        for item in range(depth):
            wait_arrived(target.at[item], sems, item)

    def bucket(number):
        grads, sems, arrived = r.grads, r.s_total, arrivals[number]
        size = BUCKET_ROWS[number]
        first = size // 512 * 256
        if first == 0:
            first = size
        x, y = lax.rem(dp, 2), lax.div(dp, 2)
        over_x, over_y = (x, dp + 1 - 2 * x), (y, dp + 2 - 4 * y)
        lanes = []
        for at, count, order in (
            (BUCKET_AT[number], size - first, (over_x, over_y)),
            (BUCKET_AT[number] + size - first, first, (over_y, over_x)),
        ):
            if count == 0:
                continue
            size1, size2, size3, size4 = count // 2, count // 4, count // 8, count // (8 * depth)
            start1 = at + member * size1
            start2 = start1 + order[0][0] * size2
            start3 = start2 + order[1][0] * size3
            start4 = start3 + place * size4
            lanes.append(
                (
                    (at + (1 - member) * size1, start1, size1, there(partner)),
                    (
                        start1 + (1 - order[0][0]) * size2,
                        start2,
                        size2,
                        {"dp": order[0][1], "seq": seq},
                    ),
                    (
                        start2 + (1 - order[1][0]) * size3,
                        start3,
                        size3,
                        {"dp": order[1][1], "seq": seq},
                    ),
                    (start3, start4, size4),
                )
            )

        def rows_at(ref, start, count):
            return ref.at[at8(start, count)]

        def wait_bytes(count, sem):
            some = rows_at(grads, BUCKET_AT[number], count)
            pltpu.make_async_copy(some, some, sem).wait()

        def total_of(stage):
            return sum(lane[stage][2] for lane in lanes)

        def arriving(stage):
            if stage == 0:
                return r.core, CORE_AT[number]
            return (arrived.near, arrived.next)[stage - 1], 0

        def pair_out(stage):
            into, at = arriving(stage)
            for lane in lanes:
                given, _, count, device = lane[stage]
                remote(
                    rows_at(grads, given, count),
                    into.at[pl.ds(at, count)],
                    sems.at[number, 2 * stage],
                    sems.at[number, 2 * stage + 1],
                    device,
                ).start()
                at += count

        def pair_in(stage):
            wait_bytes(total_of(stage), sems.at[number, 2 * stage])
            wait_bytes(total_of(stage), sems.at[number, 2 * stage + 1])
            into, at = arriving(stage)
            for lane in lanes:
                _, start, count, _ = lane[stage]
                add_all(start, count, [into.at[pl.ds(at, count)]])
                at += count

        def far_peers():
            for step in range(1, depth):
                yield step, lax.rem(place + step, depth)

        def far_out():
            at = 0
            for lane in lanes:
                start3, _, count = lane[3]
                for step, other in far_peers():
                    remote(
                        rows_at(grads, start3 + other * count, count),
                        arrived.far.at[step - 1, pl.ds(at, count)],
                        sems.at[number, 6],
                        sems.at[number, 7],
                        there(2 * other + member),
                    ).start()
                at += count

        def far_in():
            wait_bytes(total_of(3) * (depth - 1), sems.at[number, 6])
            wait_bytes(total_of(3) * (depth - 1), sems.at[number, 7])
            at = 0
            for lane in lanes:
                _, start4, count = lane[3]
                parts = [arrived.far.at[step, pl.ds(at, count)] for step in range(depth - 1)]
                add_all(start4, count, parts)
                at += count

        def far_back():
            for lane in lanes:
                _, start4, count = lane[3]
                for _, other in far_peers():
                    remote(
                        rows_at(grads, start4, count),
                        rows_at(grad_total, start4, count),
                        sems.at[number, 8],
                        sems.at[number, 9],
                        there(2 * other + member),
                    ).start()
                pltpu.make_async_copy(
                    rows_at(grads, start4, count),
                    rows_at(grad_total, start4, count),
                    sems.at[number, 16],
                ).start()

        def far_back_in():
            wait_bytes(total_of(3) * (depth - 1), sems.at[number, 8])
            wait_bytes(total_of(3) * (depth - 1), sems.at[number, 9])
            wait_bytes(total_of(3), sems.at[number, 16])

        def pair_back(stage):
            for lane in lanes:
                _, start, count, device = lane[stage]
                remote(
                    rows_at(grad_total, start, count),
                    rows_at(grad_total, start, count),
                    sems.at[number, 14 - 2 * stage],
                    sems.at[number, 15 - 2 * stage],
                    device,
                ).start()

        def pair_back_in(stage):
            wait_bytes(total_of(stage), sems.at[number, 14 - 2 * stage])
            wait_bytes(total_of(stage), sems.at[number, 15 - 2 * stage])

        def add_all(start, count, parts):
            unit = pick8(count, 64)

            def piece(index):
                rows = at8(start + unit * index, unit)
                value = grads[rows, :]
                for part in parts:
                    value = value + part[at8(unit * index, unit), :]
                grads[rows, :] = value

            loop(count // unit, piece)

        def step(which):
            if which in (1, 2, 3):
                pair_in(which - 1)
            if which == 4:
                far_in()
            if which == 5:
                far_back_in()
            if which in (6, 7, 8):
                pair_back_in(8 - which)
            if which in (0, 1, 2):
                pair_out(which)
            if which == 3:
                far_out()
            if which == 4:
                far_back()
            if which in (5, 6, 7):
                pair_back(7 - which)

        return step

    all_steps = [bucket(number) for number in range(len(BUCKET_ROWS))]

    def advance(*pairs):
        for number, which in pairs:
            all_steps[number](which)

    def loop_with(count, body, advances):
        def step(index):
            for at, pairs in advances.items():

                @pl.when(index == at)
                def _(pairs=pairs):
                    advance(*pairs)

            body(index)

        loop(count, step)

    for item in range(depth):
        wait_arrived(a0.at[pl.ds(16 + 256 * item, 256)], r.s_frames, item)
    pltpu.make_async_copy(a0.at[pl.ds(8, 8)], a0.at[pl.ds(8, 8)], edge_sems.at[3, 0]).wait()

    def mask_frames(index):
        rows = at8(pick(own_rows[0] + 16, 96) * index + 8, pick(own_rows[0] + 16, 96))
        valid = valid_rows(pick(own_rows[0] + 16, 96) * index + 8, pick(own_rows[0] + 16, 96), 0)[0]
        a0[rows, :] = jnp.where(valid, a0[rows, :], 0.0)

    loop((own_rows[0] + 16) // pick(own_rows[0] + 16, 96), mask_frames)
    cot_sends = [
        spread(
            inputs.cotangent.at[item],
            r.cot.at[at16(128 * block_in_group, 128)],
            r.s_cot,
            item,
            2 * item + group_of_block,
            block_in_group,
        )
        for item in range(depth)
    ]
    for start, _ in cot_sends:
        start()
    res_forward(0)
    qkv_forward(0)
    keys_forward(0)
    later_forward(0)
    shrink_forward_part()
    res_forward(1)
    qkv_forward(1)
    keys_forward(1)
    later_forward(1)
    send_blocks(r.last, 128, output, r.s_last)
    for item in range(depth):
        wait_arrived(r.cot.at[pl.ds(128 * item, 128)], r.s_cot, item)

    def mask_cot(index):
        valid = valid_rows(128 * index + 16, 128, 1)[0]
        rows = at16(128 * index, 128)
        r.cot[rows, :] = jnp.where(valid, r.cot[rows, :], 0.0)

    loop(own_rows[1] // 128, mask_cot)
    later_backward(1)
    advance((0, 0))
    attend_backward(1)
    advance((0, 1))
    copies = qkv_backward(1)
    res_backward(1, copies)
    shrink_backward_part()
    advance((0, 2), (1, 0))
    later_backward(0, {1: [(0, 3), (1, 1)], 3: [(0, 4), (1, 2)]})
    advance((2, 0))
    attend_backward(0, {1: [(1, 3)], 2: [(0, 5), (2, 1)]}, {0: [(0, 6)], 2: [(1, 4), (2, 2)]})
    advance((0, 7))
    copies = qkv_backward(0, {2: [(2, 3)]})
    advance((1, 5))
    res_backward(0, copies, [[(3, 0)], [(2, 4), (1, 6), (3, 1)]])
    advance((4, 0), (3, 2), (4, 1), (2, 5), (3, 3), (4, 2), (1, 7), (0, 8), (2, 6))
    advance((4, 3), (3, 4), (4, 4), (3, 5), (2, 7), (1, 8), (4, 5), (3, 6), (2, 8), (4, 6), (3, 7), (4, 7), (3, 8), (4, 8))
    for _, wait_sent in frame_sends + cot_sends:
        wait_sent()
    for after, before, _, _, item in edge_sends:

        @pl.when(sends_after & (seq != 2 * item + 1))
        def _(after=after):
            after.wait_send()

        @pl.when(sends_before & (seq != 2 * item))
        def _(before=before):
            before.wait_send()

    finish_blocks(r.last, 128, output, r.s_last)
    finish_blocks(r.dy, 256, input_grad, r.s_grad)


def pick8(total, most):
    best = 8
    for size in range(8, most + 1, 8):
        if total % size == 0:
            best = size
    return best


GRAD_SHAPES = (
    (2, 3, 256, 256),
    (2, 3, 256, 256),
    (2, 256, 256),
    (2, 2, 256),
    (2, 2, 256),
    (2, 1024, 256),
    (2, 256),
    (2, 2, 256),
    (2, 2, 256),
    (2, 256, 384),
    (2, 128, 256),
    (2, 256),
    (2, 256, 1024),
    (2, 1024),
    (2, 1024),
    (2, 1024),
    (2, 1024, 256),
    (2, 256),
    (3, 256, 256),
    (256,),
)

class Gradients(typing.NamedTuple):
    conv_one: Any
    conv_two: Any
    res_weight: Any
    norm_gain: Any
    norm_bias: Any
    time_weight: Any
    time_bias: Any
    layer_gain: Any
    layer_bias: Any
    qkv_weight: Any
    out_weight: Any
    out_bias: Any
    up_weight: Any
    up_bias: Any
    snake_alpha: Any
    snake_beta: Any
    down_weight: Any
    down_bias: Any
    shrink_weight: Any
    shrink_bias: Any


def unpack_kernel(shape, total, *refs):
    outs = Gradients(*refs[:20])
    held, sems, out_sems = refs[20:]
    loads, stores = [], []

    def rows(start, count):
        return total.at[pl.ds(start, count)], held.at[pl.ds(start, count)]

    def load(start, count):
        source, target = rows(start, count)
        loads.append(pltpu.make_async_copy(source, target, sems.at[len(loads)]))
        loads[-1].start()

    def store(start, count, target, lanes=pl.ds(0, 256)):
        source = held.at[pl.ds(start, count), lanes]
        stores.append((pltpu.make_async_copy(source, target, out_sems.at[len(stores)]), len(loads)))

    def move(start, count, target):
        load(start, count)
        store(start, count, target)

    for layer in (1, 0):
        later = LATER_AT[layer]
        for column in range(4):
            lanes = pl.ds(256 * column, 256)
            move(later + UP + 256 * column, 256, outs.up_weight.at[layer, :, lanes])
        move(later + DOWN, 1024, outs.down_weight.at[layer])
        move(later + OUT, 128, outs.out_weight.at[layer])
        load(later + LATER_SMALL, 16)
        for tap in range(3):
            move(CONV_TWO_AT[layer] + 256 * tap, 256, outs.conv_two.at[layer, tap])
        move(RES_AT[layer], 256, outs.res_weight.at[layer])
        move(QUERY_KEY_AT[layer], 256, outs.qkv_weight.at[layer, :, pl.ds(0, 256)])
        for tap in range(3):
            move(CONV_ONE_AT[layer] + 256 * tap, 256, outs.conv_one.at[layer, tap])
        load(VALUE_AT[layer], 128)
        for part in (0, 1):
            target = outs.qkv_weight.at[layer, pl.ds(128 * part, 128), pl.ds(256, 128)]
            store(VALUE_AT[layer], 128, target, pl.ds(128 * part, 128))
        load(SMALL_AT[layer], 24)
    for tap in range(3):
        move(SHRINK_AT + 256 * tap, 256, outs.shrink_weight.at[tap])
    load(EMBED_AT, 64)
    waited = 0
    for copy, needed in stores:
        for number in range(waited, needed):
            loads[number].wait()
        waited = needed
        copy.start()
    for number in range(waited, len(loads)):
        loads[number].wait()
    for layer in (0, 1):
        later = held[pl.ds(LATER_AT[layer] + LATER_SMALL, 16), :]
        res = held[pl.ds(SMALL_AT[layer], 24), :]
        outs.norm_gain[layer] = res[0:2]
        outs.norm_bias[layer] = res[2:4]
        outs.layer_gain[layer, 0:1, :] = res[4:5]
        outs.layer_gain[layer, 1:2, :] = later[2:3]
        outs.layer_bias[layer, 0:1, :] = res[5:6]
        outs.layer_bias[layer, 1:2, :] = later[3:4]
        outs.down_bias[layer : layer + 1, :] = later[0:1]
        outs.out_bias[layer : layer + 1, :] = later[1:2]
        for column in range(4):
            lanes = slice(256 * column, 256 * column + 256)
            outs.up_bias[layer : layer + 1, lanes] = later[4 + column : 5 + column]
            outs.snake_alpha[layer : layer + 1, lanes] = later[8 + column : 9 + column]
            outs.snake_beta[layer : layer + 1, lanes] = later[12 + column : 13 + column]
        summed = res[8:24]
        outs.time_bias[layer : layer + 1, :] = jnp.sum(summed, axis=0, keepdims=True)
        right = split(summed)
        blank = jnp.zeros((128 - 16, 256), F32)
        for column in range(4):
            tall = jnp.concatenate([held[pl.ds(EMBED_AT + 16 * column, 16), :], blank], 0)
            left = split(jnp.transpose(tall)[:, 0:16])
            outs.time_weight[layer, pl.ds(256 * column, 256), :] = dot_pair(left, right)
    outs.shrink_bias[...] = held[pl.ds(SMALL_AT[1] + 6, 1), :]
    for copy, _ in stores:
        copy.wait()


def fused_local(shape, *args):
    groups = scratch_of(shape)
    given = Arguments(*args)
    specs = Arguments(*(WHOLE,) * 24)._replace(
        frames=ANY,
        lengths=pl.BlockSpec(memory_space=pltpu.SMEM),
        cotangent=ANY,
        conv_one=ANY,
        conv_two=ANY,
        res_weight=ANY,
        time_weight=ANY,
        qkv_weight=ANY,
        out_weight=ANY,
        up_weight=ANY,
        down_weight=ANY,
        shrink_weight=ANY,
    )
    output, input_grad, total = pl.pallas_call(
        lambda *refs: fused_kernel(shape, groups, *refs),
        out_shape=(
            jax.ShapeDtypeStruct(given.cotangent.shape, F32),
            jax.ShapeDtypeStruct(given.frames.shape, F32),
            jax.ShapeDtypeStruct((sum(BUCKET_ROWS), 256), F32),
        ),
        in_specs=list(specs),
        out_specs=(ANY,) * 3,
        scratch_shapes=[one for group in groups for one in group.values()],
        name="layers",
        compiler_params=pltpu.CompilerParams(
            collective_id=0, has_side_effects=True, vmem_limit_bytes=VMEM_BYTES
        ),
    )(*given)
    shapes = [s if len(s) > 1 else (1,) + s for s in GRAD_SHAPES]
    grads = pl.pallas_call(
        lambda *refs: unpack_kernel(shape, *refs),
        out_shape=tuple(jax.ShapeDtypeStruct(s, F32) for s in shapes),
        in_specs=[ANY],
        out_specs=tuple(
            Gradients(*(WHOLE,) * 20)._replace(
                conv_one=ANY,
                conv_two=ANY,
                res_weight=ANY,
                qkv_weight=ANY,
                out_weight=ANY,
                up_weight=ANY,
                down_weight=ANY,
                shrink_weight=ANY,
            )
        ),
        scratch_shapes=[
            pltpu.VMEM((sum(BUCKET_ROWS), 256), F32),
            pltpu.SemaphoreType.DMA((48,)),
            pltpu.SemaphoreType.DMA((48,)),
        ],
        name="unpack",
        compiler_params=pltpu.CompilerParams(vmem_limit_bytes=VMEM_BYTES),
    )(total)
    grads = grads[:-1] + (grads[-1].reshape(256),)
    return (output, input_grad) + tuple(grads)


VMEM_BYTES = 64 * 2**20 - 2**18


ARG_SPECS = (P("dp", "seq", None), P("dp", None), P("dp"), P("dp", "seq", None)) + (P(),) * 20
OUT_SPECS = (P("dp", "seq", None), P("dp", "seq", None)) + (P(),) * 20


def solution(mesh):
    shape = dict(mesh.shape)

    def local(*args):
        utterances, frames_in = args[0].shape[:2]
        if fits(shape, utterances, frames_in):
            return fused_local(shape, *args)
        return general_local(*args)

    return jax.shard_map(
        local, mesh=mesh, in_specs=ARG_SPECS, out_specs=OUT_SPECS, check_vma=False
    )
```

```python
import math
import typing
from types import SimpleNamespace
from typing import Any

import jax
import jax.numpy as jnp
from jax import lax
from jax.experimental import pallas as pl
from jax.experimental.pallas import tpu as pltpu
from jax.sharding import PartitionSpec as P

HEADS = 2
GROUPS = 8


precise = lax.Precision.HIGHEST
epsilon = 1e-05


def with_halo(value, sides, width):
    for axis, dim in sides:
        count, length = (lax.axis_size(axis), value.shape[dim])
        up = [(i, (i + 1) % count) for i in range(count - 1)]
        down = [(j, i) for i, j in up]
        last = lax.slice_in_dim(value, length - width, length, axis=dim)
        first = lax.slice_in_dim(value, 0, width, axis=dim)
        before = lax.ppermute(last, axis, up)
        after = lax.ppermute(first, axis, down)
        value = jnp.concatenate([before, value, after], axis=dim)
    return value


def shifted(value, axis, by):
    count = lax.axis_size(axis)
    pairs = [(i, i + by) for i in range(count) if 0 <= i + by < count]
    return lax.ppermute(value, axis, pairs)


def mish_curve(value_in):
    return value_in * jnp.tanh(jax.nn.softplus(value_in))


def conv_piece(padded, weight):
    frames_out = padded.shape[1] - 2
    summed = jnp.einsum("ufc,cd->ufd", padded[:, :frames_out], weight[0], precision=precise)
    summed = summed + jnp.einsum(
        "ufc,cd->ufd", padded[:, 1 : frames_out + 1], weight[1], precision=precise
    )
    return summed + jnp.einsum("ufc,cd->ufd", padded[:, 2:], weight[2], precision=precise)


def shrink_piece(padded, weight, bias_vec):
    span_len = padded.shape[1] - 1
    summed = jnp.einsum("ufc,cd->ufd", padded[:, 0:span_len:2], weight[0], precision=precise)
    summed = summed + jnp.einsum(
        "ufc,cd->ufd", padded[:, 1:span_len:2], weight[1], precision=precise
    )
    summed = summed + jnp.einsum(
        "ufc,cd->ufd", padded[:, 2 : span_len + 1 : 2], weight[2], precision=precise
    )
    return summed + bias_vec


def group_sums(conv_out, mask_row):
    utterances, frames_in, channels = conv_out.shape
    masked = conv_out * mask_row[:, :, None]
    shape_new = (utterances, frames_in, GROUPS, channels // GROUPS)
    first_sum = jnp.sum(masked.reshape(shape_new), axis=(1, 3))
    second_sum = jnp.sum((masked * conv_out).reshape(shape_new), axis=(1, 3))
    return (first_sum, second_sum)


def group_apply(conv_out, first_sum, second_sum, counts, gain_vec, bias_vec, mask_row):
    group_width = conv_out.shape[2] // GROUPS
    mean_val = first_sum / counts[:, None]
    var_val = second_sum / counts[:, None] - mean_val * mean_val
    scale_val = lax.rsqrt(var_val + epsilon)
    mean_full = jnp.repeat(mean_val, group_width, axis=1)[:, None, :]
    scale_full = jnp.repeat(scale_val, group_width, axis=1)[:, None, :]
    normed = (conv_out - mean_full) * scale_full * gain_vec + bias_vec
    return mish_curve(normed) * mask_row[:, :, None]


def time_piece(embedding, weight, bias_vec):
    return jnp.dot(mish_curve(embedding), weight, precision=precise) + bias_vec


def layer_norm(value_in, gain_vec, bias_vec):
    mean_val = jnp.mean(value_in, axis=-1, keepdims=True)
    centered = value_in - mean_val
    var_val = jnp.mean(centered * centered, axis=-1, keepdims=True)
    return centered * lax.rsqrt(var_val + epsilon) * gain_vec + bias_vec


def attend_in(value_in, gain_vec, bias_vec, qkv_weight):
    normed = layer_norm(value_in, gain_vec, bias_vec)
    packed = jnp.einsum("ufc,ce->ufe", normed, qkv_weight, precision=precise)
    inner_dim = packed.shape[2] // 3
    return (
        packed[:, :, :inner_dim],
        packed[:, :, inner_dim : 2 * inner_dim],
        packed[:, :, 2 * inner_dim :],
    )


def attend_out(value_in, queries, key_full, value_full, key_mask, later_weights):
    (
        out_weight,
        out_bias,
        gain_vec,
        bias_vec,
        up_weight,
        up_bias,
        snake_alpha,
        snake_beta,
        down_weight,
        down_bias,
    ) = later_weights
    utterances, frames_in, inner_dim = queries.shape
    head_dim = inner_dim // HEADS
    key_count = key_full.shape[1]
    query_heads = queries.reshape(utterances, frames_in, HEADS, head_dim)
    key_heads = key_full.reshape(utterances, key_count, HEADS, head_dim)
    value_heads = value_full.reshape(utterances, key_count, HEADS, head_dim)
    scores = jnp.einsum("uqhd,ukhd->uhqk", query_heads, key_heads, precision=precise) / math.sqrt(
        head_dim
    )
    scores = jnp.where(key_mask[:, None, None, :] > 0.5, scores, -1e30)
    scores = scores - jnp.max(scores, axis=3, keepdims=True)
    raised = jnp.exp(scores)
    weights_soft = raised / jnp.sum(raised, axis=3, keepdims=True)
    attended = jnp.einsum("uhqk,ukhd->uqhd", weights_soft, value_heads, precision=precise)
    attended = attended.reshape(utterances, frames_in, inner_dim)
    current = (
        value_in + jnp.einsum("ufe,ec->ufc", attended, out_weight, precision=precise) + out_bias
    )
    normed = layer_norm(current, gain_vec, bias_vec)
    raised_up = jnp.einsum("ufc,ce->ufe", normed, up_weight, precision=precise) + up_bias
    snake_out = raised_up + jnp.sin(raised_up * jnp.exp(snake_alpha)) ** 2 / (
        jnp.exp(snake_beta) + 1e-09
    )
    return (
        current + jnp.einsum("ufe,ec->ufc", snake_out, down_weight, precision=precise) + down_bias
    )


def layer_weights(stacked, layer_index):
    (
        conv_one,
        conv_two,
        res_weight,
        norm_gain,
        norm_bias,
        time_weight,
        time_bias,
        layer_gain,
        layer_bias,
        qkv_weight,
        out_weight,
        out_bias,
        up_weight,
        up_bias,
        snake_alpha,
        snake_beta,
        down_weight,
        down_bias,
    ) = stacked
    resnet_part = (
        conv_one[layer_index],
        conv_two[layer_index],
        res_weight[layer_index],
        norm_gain[layer_index],
        norm_bias[layer_index],
        time_weight[layer_index],
        time_bias[layer_index],
    )
    first_part = (layer_gain[layer_index, 0], layer_bias[layer_index, 0], qkv_weight[layer_index])
    later_part = (
        out_weight[layer_index],
        out_bias[layer_index],
        layer_gain[layer_index, 1],
        layer_bias[layer_index, 1],
        up_weight[layer_index],
        up_bias[layer_index],
        snake_alpha[layer_index],
        snake_beta[layer_index],
        down_weight[layer_index],
        down_bias[layer_index],
    )
    return (resnet_part, first_part, later_part)


def layer_grads(resnet_grads, first_grads, later_grads):
    gains = jnp.stack([first_grads[0], later_grads[2]])
    biases = jnp.stack([first_grads[1], later_grads[3]])
    return (
        resnet_grads
        + (gains, biases, first_grads[2], later_grads[0], later_grads[1])
        + later_grads[4:]
    )


def flatten_all(arrays):
    return jnp.concatenate([array_in.reshape(-1) for array_in in arrays])


def unflatten_all(flat, shapes):
    pieces = []
    offset_at = 0
    for shape_in in shapes:
        size_in = math.prod(shape_in)
        pieces.append(flat[offset_at : offset_at + size_in].reshape(shape_in))
        offset_at = offset_at + size_in
    return pieces


def frame_halo(value_in):
    return with_halo(value_in, (("seq", 1),), 1)


def rim_return(grad_padded):
    rim_rows = jnp.concatenate([grad_padded[:, :1], grad_padded[:, -1:]], axis=1)
    arrived = with_halo(rim_rows, (("seq", 1),), 1)
    inner_rows = grad_padded[:, 1:-1]
    inner_rows = inner_rows.at[:, 0].add(arrived[:, 0])
    return inner_rows.at[:, -1].add(arrived[:, 3])


def group_total(conv_out, mask_row):
    first_sum, second_sum = group_sums(conv_out, mask_row)
    return lax.psum((first_sum, second_sum), "seq")


def group_return(conv_out, mask_row, grad_first, grad_second):
    grad_first, grad_second = lax.psum((grad_first, grad_second), "seq")

    def sums_local(conv_in):
        return group_sums(conv_in, mask_row)

    pull_back = jax.vjp(sums_local, conv_out)[1]
    return pull_back((grad_first, grad_second))[0]


def resnet_forward(inputs, mask_row, counts, embedding, weights):
    conv_first, conv_second, res_weight, norm_gain, norm_bias, time_weight, time_bias = weights
    column = mask_row[:, :, None]
    masked = inputs * column
    padded_one = frame_halo(masked)
    first_conv = conv_piece(padded_one, conv_first)
    sums_one = group_total(first_conv, mask_row)
    hidden = group_apply(
        first_conv, sums_one[0], sums_one[1], counts, norm_gain[0], norm_bias[0], mask_row
    )
    hidden = hidden + time_piece(embedding, time_weight, time_bias)[:, None, :]
    padded_two = frame_halo(hidden * column)
    second = conv_piece(padded_two, conv_second)
    sums_two = group_total(second, mask_row)
    result = group_apply(
        second, sums_two[0], sums_two[1], counts, norm_gain[1], norm_bias[1], mask_row
    )
    result = result + jnp.einsum("ufc,cd->ufd", masked, res_weight, precision=precise)
    return (result, (masked, padded_one, first_conv, sums_one, padded_two, second, sums_two))


def resnet_backward(grad_out, saved, mask_row, counts, embedding, weights):
    conv_first, conv_second, res_weight, norm_gain, norm_bias, time_weight, time_bias = weights
    masked, padded_one, first_conv, sums_one, padded_two, second, sums_two = saved
    column = mask_row[:, :, None]

    def norm_local(conv_out, first_sum, second_sum, gain_vec, bias_vec):
        return group_apply(conv_out, first_sum, second_sum, counts, gain_vec, bias_vec, mask_row)

    pull_two = jax.vjp(norm_local, second, sums_two[0], sums_two[1], norm_gain[1], norm_bias[1])[1]
    grad_second, grad_first_sum, grad_second_sum, gain_grad_two, bias_grad_two = pull_two(grad_out)
    grad_second = grad_second + group_return(second, mask_row, grad_first_sum, grad_second_sum)
    grad_res = jnp.einsum("ufc,ufd->cd", masked, grad_out, precision=precise)
    grad_masked = jnp.einsum("ufd,cd->ufc", grad_out, res_weight, precision=precise)
    pull_conv = jax.vjp(conv_piece, padded_two, conv_second)[1]
    grad_padded, grad_conv_second = pull_conv(grad_second)
    grad_hidden = rim_return(grad_padded) * column

    def time_local(weight, bias_vec):
        return time_piece(embedding, weight, bias_vec)

    pull_time = jax.vjp(time_local, time_weight, time_bias)[1]
    grad_time_weight, grad_time_bias = pull_time(jnp.sum(grad_hidden, axis=1))
    pull_one = jax.vjp(
        norm_local, first_conv, sums_one[0], sums_one[1], norm_gain[0], norm_bias[0]
    )[1]
    grad_first, grad_first_sum, grad_second_sum, gain_grad_one, bias_grad_one = pull_one(
        grad_hidden
    )
    grad_first = grad_first + group_return(first_conv, mask_row, grad_first_sum, grad_second_sum)
    pull_conv = jax.vjp(conv_piece, padded_one, conv_first)[1]
    grad_padded, grad_conv_first = pull_conv(grad_first)
    grad_inputs = (rim_return(grad_padded) + grad_masked) * column
    grads = (
        grad_conv_first,
        grad_conv_second,
        grad_res,
        jnp.stack([gain_grad_one, gain_grad_two]),
        jnp.stack([bias_grad_one, bias_grad_two]),
        grad_time_weight,
        grad_time_bias,
    )
    return (grad_inputs, grads)


def block_forward(value_in, key_mask, first_weights, later_weights):
    queries, key_here, value_here = attend_in(
        value_in, first_weights[0], first_weights[1], first_weights[2]
    )
    key_full, value_full = (
        lax.all_gather(key_here, "seq", axis=1, tiled=True),
        lax.all_gather(value_here, "seq", axis=1, tiled=True),
    )
    result = attend_out(value_in, queries, key_full, value_full, key_mask, later_weights)
    kept_pair = (key_full, value_full)
    return (result, (value_in, queries, kept_pair))


def block_backward(grad_out, saved, key_mask, first_weights, later_weights):
    value_in, queries, kept_pair = saved
    key_full, value_full = kept_pair

    def attend_local(current, query_in, key_in, value_full_in, weights_in):
        return attend_out(current, query_in, key_in, value_full_in, key_mask, weights_in)

    pull_out = jax.vjp(attend_local, value_in, queries, key_full, value_full, later_weights)[1]
    grad_value, grad_queries, grad_keys, grad_values, grad_later = pull_out(grad_out)
    grad_keys, grad_values = (
        lax.psum_scatter(grad_keys, "seq", scatter_dimension=1, tiled=True),
        lax.psum_scatter(grad_values, "seq", scatter_dimension=1, tiled=True),
    )
    pull_in = jax.vjp(attend_in, value_in, first_weights[0], first_weights[1], first_weights[2])[1]
    grad_input, grad_gain, grad_bias, grad_qkv = pull_in((grad_queries, grad_keys, grad_values))
    return (grad_value + grad_input, (grad_gain, grad_bias, grad_qkv), grad_later)


def shrink_forward(value_in, mask_row, weight, bias_vec):
    masked = value_in * mask_row[:, :, None]
    carried = shifted(masked[:, -1:], "seq", 1)
    padded = jnp.concatenate([carried, masked], axis=1)
    return (shrink_piece(padded, weight, bias_vec), padded)


def shrink_backward(grad_out, padded, mask_row, weight, bias_vec):
    pull_back = jax.vjp(shrink_piece, padded, weight, bias_vec)[1]
    grad_padded, grad_weight, grad_bias = pull_back(grad_out)
    returned = shifted(grad_padded[:, :1], "seq", -1)
    grad_masked = grad_padded[:, 1:].at[:, -1:].add(returned)
    return (grad_masked * mask_row[:, :, None], grad_weight, grad_bias)


def general_local(
    frames,
    flow_embed,
    lengths,
    cotangent,
    conv_one,
    conv_two,
    res_weight,
    norm_gain,
    norm_bias,
    time_weight,
    time_bias,
    layer_gain,
    layer_bias,
    qkv_weight,
    out_weight,
    out_bias,
    up_weight,
    up_bias,
    snake_alpha,
    snake_beta,
    down_weight,
    down_bias,
    shrink_weight,
    shrink_bias,
):
    stacked = tuple(
        (
            weight_in.astype(jnp.float32)
            for weight_in in (
                conv_one,
                conv_two,
                res_weight,
                norm_gain,
                norm_bias,
                time_weight,
                time_bias,
                layer_gain,
                layer_bias,
                qkv_weight,
                out_weight,
                out_bias,
                up_weight,
                up_bias,
                snake_alpha,
                snake_beta,
                down_weight,
                down_bias,
            )
        )
    )
    shrink_w = shrink_weight.astype(jnp.float32)
    shrink_b = shrink_bias.astype(jnp.float32)
    seq_count = lax.axis_size("seq")
    seq_index = lax.axis_index("seq")
    frames_one = frames.shape[1]
    frames_two = frames_one // 2
    group_width = frames.shape[2] // GROUPS
    place_one = seq_index * frames_one + jnp.arange(frames_one, dtype=jnp.int32)
    place_two = seq_index * frames_two + jnp.arange(frames_two, dtype=jnp.int32)
    mask_one = (place_one[None, :] < lengths[:, None]).astype(jnp.float32)
    mask_two = (2 * place_two[None, :] < lengths[:, None]).astype(jnp.float32)
    keys_one = (
        jnp.arange(frames_one * seq_count, dtype=jnp.int32)[None, :] < lengths[:, None]
    ).astype(jnp.float32)
    keys_two = (
        2 * jnp.arange(frames_two * seq_count, dtype=jnp.int32)[None, :] < lengths[:, None]
    ).astype(jnp.float32)
    counts_one = (lengths * group_width).astype(jnp.float32)
    counts_two = ((lengths + 1) // 2 * group_width).astype(jnp.float32)
    res_zero, first_zero, later_zero = layer_weights(stacked, 0)
    res_one, first_one, later_one = layer_weights(stacked, 1)
    current, saved_first = resnet_forward(frames, mask_one, counts_one, flow_embed, res_zero)
    current, saved_second = block_forward(current, keys_one, first_zero, later_zero)
    current, saved_shrink = shrink_forward(current, mask_one, shrink_w, shrink_b)
    current, saved_third = resnet_forward(current, mask_two, counts_two, flow_embed, res_one)
    current, saved_fourth = block_forward(current, keys_two, first_one, later_one)
    output = current * mask_two[:, :, None]
    grad_now = cotangent * mask_two[:, :, None]
    grad_now, first_grads, later_grads = block_backward(
        grad_now, saved_fourth, keys_two, first_one, later_one
    )
    grad_now, resnet_grads = resnet_backward(
        grad_now, saved_third, mask_two, counts_two, flow_embed, res_one
    )
    grads_top = layer_grads(resnet_grads, first_grads, later_grads)
    shapes = [array_in.shape for array_in in grads_top]
    top_size = sum((math.prod(shape_in) for shape_in in shapes))
    grad_now, grad_shrink_w, grad_shrink_b = shrink_backward(
        grad_now, saved_shrink, mask_one, shrink_w, shrink_b
    )
    grad_now, first_grads, later_grads = block_backward(
        grad_now, saved_second, keys_one, first_zero, later_zero
    )
    grad_now, resnet_grads = resnet_backward(
        grad_now, saved_first, mask_one, counts_one, flow_embed, res_zero
    )
    grads_low = layer_grads(resnet_grads, first_grads, later_grads)
    low_flat = jnp.concatenate([flatten_all(grads_low), grad_shrink_w.reshape(-1), grad_shrink_b])
    summed_all = lax.psum(jnp.concatenate([flatten_all(grads_top), low_flat]), ("dp", "seq"))
    summed_top = summed_all[:top_size]
    summed_low = summed_all[top_size:]
    parts_top = unflatten_all(summed_top, shapes)
    parts_low = unflatten_all(summed_low, shapes + [shrink_w.shape, shrink_b.shape])
    grads_out = tuple(
        (jnp.stack([parts_low[number], parts_top[number]]) for number in range(len(shapes)))
    )
    return (output, grad_now) + grads_out + (parts_low[-2], parts_low[-1])


F32, BF = jnp.float32, jnp.bfloat16
MESH = pl.DeviceIdType.MESH
NN = (((1,), (0,)), ((), ()))
NT = (((1,), (1,)), ((), ()))
LOG2E = math.log2(math.e)
LN2 = math.log(2.0)
ANY = pl.BlockSpec(memory_space=pl.ANY)
WHOLE = pl.BlockSpec(memory_space=pltpu.VMEM)

SIN_SQUARE = (
    9.869604311707743,
    -32.4696711717196,
    42.72719633650352,
    -30.101465841168043,
    13.050098919638232,
    -3.356592620742283,
)
SIN_TWICE = (
    6.283184916495428,
    -41.3415892326883,
    81.59994332977455,
    -76.61447253116356,
    41.34288235420472,
    -12.4712435344911,
)

UP, DOWN, OUT, LATER_SMALL = 0, 1024, 2048, 2176
BUCKET_ROWS = (2304, 3072, 2304, 1536, 768)
BUCKET_AT = (0, 2304, 5376, 7680, 9216)
GRAD_FIRST = 4
CORE_AT, CORE_ROWS = (0, 1152, 0, 1152, 1920), 2688
LATER_AT = (5376, 0)
CONV_TWO_AT = (7680, 2304)
RES_AT = (8448, 3072)
QUERY_KEY_AT = (8704, 3328)
CONV_ONE_AT = (9216, 3584)
VALUE_AT = (8960, 4352)
SMALL_AT = (9088, 4480)
SHRINK_AT, EMBED_AT = 4504, 5272


def pick(total, most):
    best = 16
    for size in range(16, most + 1, 16):
        if total % size == 0:
            best = size
    return best


def fits(shape, utterances, frames_in):
    return shape["seq"] == 2 * utterances and frames_in == 256 and shape["dp"] * utterances == 16


def split(value):
    high = value.astype(BF)
    return high, (value - high.astype(F32)).astype(BF)


def dot(left, right, dims=NN):
    return lax.dot_general(left, right, dims, preferred_element_type=F32)


def dot_weight(value, weight, dims=NN):
    rows = value.shape[0]
    both = dot(jnp.concatenate(split(value), 0), weight, dims)
    return both[:rows] + both[rows:]


def dot_pair(left, right):
    rows = left[0].shape[0]
    both = dot(jnp.concatenate(left, 0), right[0])
    return both[:rows] + both[rows:] + dot(left[0], right[1])


def fold8(value):
    return jnp.sum(value.reshape(value.shape[0] // 8, 8, value.shape[1]), axis=0)


def polynomial(coefficients, at):
    total = jnp.full_like(at, coefficients[-1])
    for number in coefficients[-2::-1]:
        total = total * at + number
    return total


def mish_terms(value):
    raised = jnp.exp(jnp.minimum(value, 20.0))
    top = raised * (raised + 2.0)
    return raised, top, 1.0 / (top + 2.0)


def mish_of(value):
    raised, top, inverse = mish_terms(value)
    return value * (top * inverse)


def mish_slope(value):
    raised, top, inverse = mish_terms(value)
    return inverse * (top + 4.0 * value * (raised * (raised + 1.0)) * inverse)


def loop(count, body, unrolled=False):
    if unrolled:
        for index in range(count):
            body(index)
        return

    def step(index, carry):
        body(index)
        return carry

    lax.fori_loop(0, count, step, 0)


def at8(start, size):
    return pl.ds(start if isinstance(start, int) else pl.multiple_of(start, 8), size)


def at16(start, size):
    return pl.ds(start if isinstance(start, int) else pl.multiple_of(start, 16), size)


class Arguments(typing.NamedTuple):
    frames: Any
    flow_embed: Any
    lengths: Any
    cotangent: Any
    conv_one: Any
    conv_two: Any
    res_weight: Any
    norm_gain: Any
    norm_bias: Any
    time_weight: Any
    time_bias: Any
    layer_gain: Any
    layer_bias: Any
    qkv_weight: Any
    out_weight: Any
    out_bias: Any
    up_weight: Any
    up_bias: Any
    snake_alpha: Any
    snake_beta: Any
    down_weight: Any
    down_bias: Any
    shrink_weight: Any
    shrink_bias: Any


def matrices(found):
    return (
        found.conv_one,
        found.conv_two,
        found.res_weight,
        found.qkv_weight,
        found.out_weight,
        found.up_weight,
        found.down_weight,
        found.shrink_weight,
    )


def scratch_of(shape):
    depth = shape["seq"] // 2
    own_rows = (256 * depth, 128 * depth)

    def array(*size):
        return pltpu.VMEM(size, F32)

    def short(*size):
        return pltpu.VMEM(size, BF)

    def semaphores(*size):
        return pltpu.SemaphoreType.DMA(size)

    shared = dict(
        w_conv_one=short(2, 3, 256, 256),
        w_conv_two=short(2, 3, 256, 256),
        w_res_weight=short(2, 256, 256),
        w_qkv_weight=short(2, 256, 384),
        w_out_weight=short(2, 128, 256),
        w_up_weight=short(2, 256, 1024),
        w_down_weight=short(2, 1024, 256),
        w_shrink_weight=short(3, 256, 256),
        first=array(2, own_rows[0] + 64, 128),
        cot=array(own_rows[1], 256),
        last=array(own_rows[1], 256),
        dy=array(own_rows[0], 256),
        kv=array(2 * own_rows[0], 256),
        dkr=array(own_rows[0], 256),
        dx=array(own_rows[0] + 32, 256),
        da=array(own_rows[1] + 32, 256),
        vt=short(2, own_rows[0], 256),
        dd=short(2, own_rows[0], 128),
        qq=short(2, own_rows[0], 128),
        tall=array(256, 4 * 256),
        wide=array(2 * depth, 256, 256),
        half=short(4 * depth, 256, 256),
        te=array(2, 8, 256),
        sums=array(8, 16, 256),
        sums_in=array(8, 16, 256),
        stat=array(4, 8, 256),
        narrow_acc=array(8, 8, 256),
        wide_acc=array(3, 8, 1024),
        gather=short(256, 256),
        grads=array(sum(BUCKET_ROWS), 256),
        core=array(CORE_ROWS, 256),
        s_weight=semaphores(16),
        s_frames=semaphores(4, depth),
        s_cot=semaphores(2, depth),
        s_last=semaphores(2, depth),
        s_grad=semaphores(2, 4 * depth),
        s_sums=semaphores(2, 8),
        s_kv=semaphores(4, depth),
        s_first=semaphores(2),
        s_dk=semaphores(4),
        s_dx=semaphores(4),
        s_total=semaphores(len(BUCKET_ROWS), 21),
    )
    layers = [
        dict(
            a=array(own + 32, 256),
            c1=array(own + 32, 256),
            h=array(own + 32, 256),
            c2=array(own + 32, 256),
            x=array(own, 256),
            att=array(own, 128),
            qh=short(2, own, 256),
            kh=short(2, 2 * own, 256),
            vh=short(2, 2 * own, 256),
            kt=short(2, own // 128, 128, 256),
        )
        for own in own_rows
    ]
    arrivals = [
        dict(
            near=array(size // 4, 256),
            next=array(size // 8, 256),
            far=array((depth - 1) * size // 32, 256),
        )
        for size in BUCKET_ROWS[:3]
    ]
    return [shared] + layers + arrivals


def named(groups, refs):
    found, at = [], 0
    for group in groups:
        found.append(SimpleNamespace(**dict(zip(group, refs[at : at + len(group)]))))
        at += len(group)
    return found


def fused_kernel(shape, groups, *refs):
    inputs = Arguments(*refs[:24])
    output, input_grad, grad_total = refs[24:27]
    r, *rest = named(groups, refs[27:])
    layers, arrivals = rest[:2], rest[2:]
    dp_count, seq_count = shape["dp"], shape["seq"]
    depth = seq_count // 2
    dp, seq = lax.axis_index("dp"), lax.axis_index("seq")
    member, place = lax.rem(seq, 2), lax.div(seq, 2)
    partner = seq + 1 - 2 * member
    half = depth
    own_rows = (256 * depth, 128 * depth)
    utterance = dp * depth + place
    length = inputs.lengths[place]
    lane128 = lax.broadcasted_iota(jnp.int32, (1, 128), 1)
    low_half = lane128 < 64

    def there(index):
        return {"dp": dp, "seq": index}

    def remote(source, target, sent, arrived, device):
        return pltpu.make_async_remote_copy(
            source, target, sent, arrived, device_id=device, device_id_type=MESH
        )

    held = (
        r.w_conv_one,
        r.w_conv_two,
        r.w_res_weight,
        r.w_qkv_weight,
        r.w_out_weight,
        r.w_up_weight,
        r.w_down_weight,
        r.w_shrink_weight,
    )
    weight_copies = [
        pltpu.make_async_copy(matrix, target, r.s_weight.at[number])
        for number, (matrix, target) in enumerate(zip(matrices(inputs), held))
    ]
    time_copies = []
    for layer in (0, 1):
        for part in range(4):
            time_copies.append(
                pltpu.make_async_copy(
                    inputs.time_weight.at[layer, pl.ds(256 * part, 256)],
                    r.half.at[4 * layer + part],
                    r.s_weight.at[len(held) + 4 * layer + part],
                )
            )
    for copy in time_copies + weight_copies:
        copy.start()

    def zero(ref, start, size):
        ref[pl.ds(start, size), :] = jnp.zeros((size, ref.shape[1]), F32)

    for mine, own in zip(layers, own_rows):
        for ref in (mine.a, mine.h, mine.c2):
            zero(ref, 0, 16)
            zero(ref, own + 16, 16)
    for part in (0, 1):
        zero(r.first.at[part], 0, 32)
        zero(r.first.at[part], own_rows[0] + 32, 32)
    zero(r.da, 0, 16)
    zero(r.da, own_rows[1] + 16, 16)
    for start in (0, own_rows[1] + 16, own_rows[0] + 16):
        zero(r.dx, start, 16)

    barrier = pltpu.get_barrier_semaphore()
    for step in range(1, seq_count):
        pl.semaphore_signal(
            barrier,
            inc=1,
            device_id=there(lax.rem(seq + step, seq_count)),
            device_id_type=MESH,
        )
    for step in range(1, dp_count):
        pl.semaphore_signal(
            barrier,
            inc=1,
            device_id={"dp": lax.rem(dp + step, dp_count), "seq": seq},
            device_id_type=MESH,
        )
    pl.semaphore_wait(barrier, seq_count - 1 + dp_count - 1)

    def spread(source_of, target_of, sems, item, target_seq, arrived_at):
        away = remote(
            source_of, target_of, sems.at[0, item], sems.at[1, arrived_at], there(target_seq)
        )
        here = pltpu.make_async_copy(source_of, target_of, sems.at[1, arrived_at])

        def start():
            @pl.when(target_seq != seq)
            def _():
                away.start()

            @pl.when(target_seq == seq)
            def _():
                here.start()

        def wait_sent():
            @pl.when(target_seq != seq)
            def _():
                away.wait_send()

        return start, wait_sent

    def wait_arrived(target, sems, index):
        pltpu.make_async_copy(target, target, sems.at[1, index]).wait()

    group_of_block = lax.div(seq, half)
    block_in_group = lax.rem(seq, half)
    frame_sends = []
    a0 = layers[0].a
    for turned in (2, 1, 3, 0):
        item = lax.rem(place + turned, depth)
        target = 2 * item + group_of_block
        frame_sends.append(
            spread(
                inputs.frames.at[item],
                a0.at[at16(16 + 256 * block_in_group, 256)],
                r.s_frames,
                item,
                target,
                block_in_group,
            )
        )
    for start, _ in frame_sends:
        start()
    edge_sems = r.s_frames
    edge_sends = []
    for item in range(depth):
        after = remote(
            inputs.frames.at[item, pl.ds(248, 8)],
            a0.at[pl.ds(8, 8)],
            edge_sems.at[2, item],
            edge_sems.at[3, 0],
            there(2 * item + 1),
        )
        before = remote(
            inputs.frames.at[item, pl.ds(0, 8)],
            a0.at[pl.ds(16 + own_rows[0], 8)],
            edge_sems.at[2, item],
            edge_sems.at[3, 0],
            there(2 * item),
        )
        after_here = pltpu.make_async_copy(
            inputs.frames.at[item, pl.ds(248, 8)], a0.at[pl.ds(8, 8)], edge_sems.at[3, 0]
        )
        before_here = pltpu.make_async_copy(
            inputs.frames.at[item, pl.ds(0, 8)],
            a0.at[pl.ds(16 + own_rows[0], 8)],
            edge_sems.at[3, 0],
        )
        edge_sends.append((after, before, after_here, before_here, item))
    sends_after = seq == half - 1
    sends_before = seq == half
    for after, before, after_here, before_here, item in edge_sends:

        @pl.when(sends_after & (seq != 2 * item + 1))
        def _(after=after):
            after.start()

        @pl.when(sends_after & (seq == 2 * item + 1))
        def _(after_here=after_here):
            after_here.start()

        @pl.when(sends_before & (seq != 2 * item))
        def _(before=before):
            before.start()

        @pl.when(sends_before & (seq == 2 * item))
        def _(before_here=before_here):
            before_here.start()

    def zero_grads(index):
        r.grads[at8(64 * index, 64), :] = jnp.zeros((64, 256), F32)

    loop(sum(BUCKET_ROWS) // 64, zero_grads)
    same_group = (
        lax.broadcasted_iota(jnp.int32, (256, 256), 0) // 32
        == lax.broadcasted_iota(jnp.int32, (256, 256), 1) // 32
    )
    r.gather[...] = jnp.where(same_group, 1.0, 0.0).astype(BF)
    for copy in time_copies:
        copy.wait()
    embedded = mish_of(inputs.flow_embed[pl.ds(place, 1), :])
    wide_embed = jnp.broadcast_to(embedded, (16, 1024))
    time_bias = inputs.time_bias[...].astype(F32)
    for layer in (0, 1):
        weight = jnp.concatenate([r.half[4 * layer + part] for part in range(4)], 0)
        projected = dot_weight(wide_embed, weight)
        r.te[layer] = projected[:8] + time_bias[layer : layer + 1]
    row16 = lax.broadcasted_iota(jnp.int32, (16, 256), 0)
    for part in range(4):
        chosen = jnp.where(
            row16 == utterance + 64 * member, embedded[:, 256 * part : 256 * part + 256], 0.0
        )
        r.grads[pl.ds(EMBED_AT + 16 * part, 16), :] = chosen
    for copy in weight_copies:
        copy.wait()

    def valid_rows(start, rows, layer):
        at = lax.broadcasted_iota(jnp.int32, (rows, 256), 0) + (start - 16)
        frame = at + member * own_rows[layer]
        valid = (frame >= 0) & (frame * (1 + layer) < length)
        return valid, valid & (at >= 0) & (at < own_rows[layer])

    def conv_block(source, start, rows, taps, dims=NN):
        value = source[at8(start, rows + 16), :]
        both = jnp.concatenate(split(value), 0)
        total = None
        for tap, weight in enumerate(taps):
            part = dot(both, weight, dims)
            part = part[: rows + 16] + part[rows + 16 :]
            part = part[7 + tap : 7 + tap + rows]
            total = part if total is None else total + part
        return total

    def send_sums(number):
        copy = remote(
            r.sums.at[number],
            r.sums_in.at[number],
            r.s_sums.at[0, number],
            r.s_sums.at[1, number],
            there(partner),
        )
        copy.start()
        return copy

    def group_total(value):
        high = value.astype(BF)
        rest = value - high.astype(F32)
        middle = rest.astype(BF)
        last = (rest - middle.astype(F32)).astype(BF)
        parts = dot(jnp.concatenate([high, middle, last], 0), r.gather[...])
        total = parts[0:16] + parts[16:32] + parts[32:48]
        return (
            jnp.sum(total[0:8], axis=0, keepdims=True),
            jnp.sum(total[8:16], axis=0, keepdims=True),
        )

    counts = (
        (length * 32).astype(F32),
        (lax.div(length + 1, 2) * 32).astype(F32),
    )

    def forward_sums(layer, which, copy):
        number = 2 * layer + which
        copy.wait()
        first_sum, second_sum = group_total(r.sums[number] + r.sums_in[number])
        mean = first_sum / counts[layer]
        variance = second_sum / counts[layer] - mean * mean
        r.stat[number, 0:1, :] = mean
        r.stat[number, 1:2, :] = lax.rsqrt(variance + epsilon)

    def norm_rows(layer, which):
        number = 2 * layer + which
        gain = inputs.norm_gain[...].astype(F32)[layer, which : which + 1]
        bias = inputs.norm_bias[...].astype(F32)[layer, which : which + 1]
        return r.stat[number, 0:1, :], r.stat[number, 1:2, :], gain, bias

    def add_sums(number, first, second):
        r.sums[number, 0:8, :] += fold8(first)
        r.sums[number, 8:16, :] += fold8(second)

    def clear_sums(number):
        r.sums[number] = jnp.zeros((16, 256), F32)

    def normed_layer(value):
        mean = jnp.mean(value, axis=1, keepdims=True)
        centered = value - mean
        variance = jnp.mean(centered * centered, axis=1, keepdims=True)
        scale = lax.rsqrt(variance + epsilon)
        return centered * scale, scale

    def normed_back(grad, normed, scale):
        return scale * (
            grad
            - jnp.mean(grad, axis=1, keepdims=True)
            - normed * jnp.mean(grad * normed, axis=1, keepdims=True)
        )

    def layer_rows(layer, which):
        gain = inputs.layer_gain[...].astype(F32)[layer, which : which + 1]
        bias = inputs.layer_bias[...].astype(F32)[layer, which : which + 1]
        return gain, bias

    def row_of(ref, layer):
        return ref[...].astype(F32)[layer : layer + 1]

    def keys_aux(start, rows, layer):
        lane = lax.broadcasted_iota(jnp.int32, (rows, 128), 1)
        key = lax.broadcasted_iota(jnp.int32, (rows, 128), 0) + start
        masked = jnp.where(key * (1 + layer) < length, 0.0, -1e30)
        ones = jnp.where((lane >= 65) & (lane < 68), 1.0, 0.0)
        return jnp.where(lane == 64, masked, ones)

    def both_heads(value):
        high = value.astype(BF).astype(F32)
        low = value - high
        return high, low, pltpu.roll(high, 64, 1), pltpu.roll(low, 64, 1)

    def key_tiles(value, aux):
        high, low, high_turned, low_turned = both_heads(value)
        tiles = (
            (jnp.where(low_half, high, low_turned), jnp.where(low_half, high, aux)),
            (jnp.where(low_half, high_turned, low), jnp.where(low_half, high_turned, aux)),
        )
        return [(a.astype(BF), b.astype(BF)) for a, b in tiles]

    def query_tiles(value, aux):
        high, low, high_turned, low_turned = both_heads(value)
        tiles = (
            (jnp.where(low_half, high, high_turned), jnp.where(low_half, low, aux[0])),
            (jnp.where(low_half, high_turned, high), jnp.where(low_half, low_turned, aux[1])),
        )
        return [(a.astype(BF), b.astype(BF)) for a, b in tiles]

    def three_lanes(value, first):
        lane = lax.broadcasted_iota(jnp.int32, value.shape, 1)
        high = value.astype(BF).astype(F32)
        rest = value - high
        middle = rest.astype(BF).astype(F32)
        spread_out = jnp.where(lane == 66, middle, rest - middle)
        spread_out = jnp.where(lane == 65, high, spread_out)
        spread_out = jnp.where(lane == 64, first, spread_out)
        return jnp.where((lane >= 64) & (lane < 68), spread_out, 0.0)

    def res_forward(layer):
        own = own_rows[layer]
        extended = own + 16
        rows = pick(extended, 256)
        small = pick(extended, 256)
        a, c1, h, c2 = layers[layer].a, layers[layer].c1, layers[layer].h, layers[layer].c2

        def convolve(source, target, weights, number):
            clear_sums(number)

            def block(index):
                out = conv_block(source, rows * index, rows, [weights[layer, k] for k in range(3)])
                start = rows * index + 8
                target[at8(start, rows), :] = out
                kept = jnp.where(valid_rows(start, rows, layer)[1], out, 0.0)
                add_sums(number, kept, kept * out)

            loop(extended // rows, block, True)
            return send_sums(number)

        copy = convolve(a, c1, r.w_conv_one, 2 * layer)
        forward_sums(layer, 0, copy)
        mean, scale, gain, bias = norm_rows(layer, 0)
        added = r.te[layer, 0:1, :]

        def normed(index):
            start = small * index + 8
            value = (c1[at8(start, small), :] - mean) * scale * gain + bias
            valid = valid_rows(start, small, layer)[0]
            h[at8(start, small), :] = jnp.where(valid, mish_of(value) + added, 0.0)

        loop(extended // small, normed, True)
        copy = convolve(h, c2, r.w_conv_two, 2 * layer + 1)

        def residual(index):
            value = a[at16(256 * index + 16, 256), :]
            layers[layer].x[at16(256 * index, 256), :] = dot_weight(value, r.w_res_weight[layer])

        loop(own // 256, residual, True)
        forward_sums(layer, 1, copy)

    def keys_of(layer):
        return (r.kv, r.dy)[layer]

    def kv_copy(layer, index):
        own = own_rows[layer]
        part = keys_of(layer).at[at16(member * own + 256 * index, 256)]
        return remote(
            part,
            part,
            r.s_kv.at[2 * layer, index],
            r.s_kv.at[2 * layer + 1, index],
            there(partner),
        )

    def qkv_forward(layer):
        own = own_rows[layer]
        c2, x, kv, qh = layers[layer].c2, layers[layer].x, keys_of(layer), layers[layer].qh
        mean, scale, gain, bias = norm_rows(layer, 1)
        layer_gain, layer_bias = layer_rows(layer, 0)
        lane = lax.broadcasted_iota(jnp.int32, (256, 128), 1)
        aux = jnp.where(lane == 64, 1.0, 0.0)

        def block(index):
            start = 256 * index
            value = (c2[at16(start + 16, 256), :] - mean) * scale * gain + bias
            valid = valid_rows(start + 16, 256, layer)[0]
            out = jnp.where(valid, mish_of(value), 0.0) + x[at16(start, 256), :]
            x[at16(start, 256), :] = out
            packed = dot_weight(
                normed_layer(out)[0] * layer_gain + layer_bias, r.w_qkv_weight[layer]
            )
            kv[at16(member * own + start, 256), :] = packed[:, 128:]
            kv_copy(layer, index).start()
            tiles = query_tiles(packed[:, :128] * (LOG2E / 8.0), (aux, aux))
            for head in (0, 1):
                qh[head, at16(start, 256), 0:128] = tiles[head][0]
                qh[head, at16(start, 256), 128:256] = tiles[head][1]

        loop(own // 256, block, True)

    def keys_forward(layer):
        own = own_rows[layer]
        kv, kh, vh, kt, vt = keys_of(layer), layers[layer].kh, layers[layer].vh, layers[layer].kt, r.vt
        mine = own // 256

        def block(number):
            index = lax.rem(member * mine + number, 2 * mine)
            start = 256 * index
            value = kv[at16(start, 256), :]
            aux = keys_aux(start, 256, layer)
            for part, target in ((value[:, :128], kh), (value[:, 128:], vh)):
                tiles = key_tiles(part, aux)
                for head in (0, 1):
                    target[head, at16(start, 256), 0:128] = tiles[head][0]
                    target[head, at16(start, 256), 128:256] = tiles[head][1]
            for column in (0, 128):
                high, low = split(jnp.transpose(value[:, column : column + 128]))
                for head in (0, 1):
                    both = jnp.concatenate([high[64 * head : 64 * head + 64], low[64 * head : 64 * head + 64]], 0)
                    if column == 0:
                        kt[head, index] = both
                    else:
                        vt[head, at16(128 * index, 128), :] = both

        loop(mine, block)
        for index in range(mine):
            kv_copy(layer, index).wait()
        loop(mine, lambda number: block(mine + number))

    def snake_rows(layer):
        alpha = jnp.exp(row_of(inputs.snake_alpha, layer))
        beta = jnp.exp(row_of(inputs.snake_beta, layer))
        return alpha, beta, 1.0 / (beta + 1e-9)

    def later_forward(layer):
        own = own_rows[layer]
        x, att, kh, qh, vt = layers[layer].x, layers[layer].att, layers[layer].kh, layers[layer].qh, r.vt
        wide, part16 = r.wide, r.half
        blocks = 2 * own // 256
        gain, bias = layer_rows(layer, 1)
        out_bias, down_bias, up_bias = row_of(inputs.out_bias, layer), row_of(inputs.down_bias, layer), row_of(inputs.up_bias, layer)
        alpha, beta, inverse = snake_rows(layer)
        turns = alpha * (1.0 / math.pi)

        def block(index):
            start = 256 * index
            parts = [(head, part) for head in (0, 1) for part in (0, 1)]
            keys_in = blocks // 2
            queries = [qh[head, at16(start, 256), :] for head in (0, 1)]
            most, total, found = {}, {}, {}

            def scores(unit):
                head, part = parts[unit]
                highest = jnp.full((8, 256), -3e38, F32)
                for key in range(keys_in):
                    at = 256 * (keys_in * part + key)
                    out = dot(kh[head, at : at + 256, :], queries[head], NT)
                    wide[4 * (unit % 2) + key] = out
                    highest = jnp.maximum(highest, jnp.max(out.reshape(32, 8, 256), axis=0))
                most[unit] = jnp.max(highest, axis=0, keepdims=True)
                if part == 1:
                    most[unit] = jnp.maximum(most[unit], most[unit - 1])

            def exponentials(unit):
                summed = jnp.zeros((8, 256), F32)
                for key in range(keys_in):
                    for piece in range(4):
                        rows = pl.ds(64 * piece, 64)
                        raised = jnp.exp2(wide[4 * (unit % 2) + key, rows, :] - most[unit])
                        summed = summed + fold8(raised)
                        high, low = split(raised)
                        part16[8 * (unit % 2) + key, rows, :] = high
                        part16[8 * (unit % 2) + 4 + key, rows, :] = low
                total[unit] = jnp.sum(summed, axis=0, keepdims=True)

            def weighted(unit):
                head, part = parts[unit]
                first_key = keys_in * part
                values = jnp.concatenate(
                    [vt[head, 128 * key : 128 * key + 128, :] for key in range(first_key, first_key + keys_in)], 1
                )
                out = None
                for which in (0, 4):
                    at = 8 * (unit % 2) + which
                    taken = jnp.concatenate([part16[at + key] for key in range(keys_in)], 0)
                    taken = dot(values, taken)
                    out = taken if out is None else out + taken
                found[unit] = out[:64] + out[64:]

            scores(0)
            for unit in range(4):
                if unit < 3:
                    scores(unit + 1)
                if unit > 0:
                    weighted(unit - 1)
                exponentials(unit)
            weighted(3)
            attended = []
            for head in (0, 1):
                before, after = 2 * head, 2 * head + 1
                lowered = jnp.exp2(most[before] - most[after])
                summed = total[before] * lowered + total[after]
                attended.append((found[before] * lowered + found[after]) * (1.0 / summed))
                level = jnp.transpose(jnp.broadcast_to(most[after] + jnp.log2(summed), (128, 256)))
                aux = three_lanes(-level, 1.0)
                old = qh[head, at16(start, 256), 128:256]
                qh[head, at16(start, 256), 128:256] = jnp.where(low_half, old, aux.astype(BF))
            joined = jnp.transpose(jnp.concatenate(attended, 0))
            att[at16(start, 256), :] = joined
            y = x[at16(start, 256), :] + dot_weight(joined, r.w_out_weight[layer]) + out_bias
            entered = jnp.concatenate(split(normed_layer(y)[0] * gain + bias), 0)

            def lift(column):
                both = dot(entered, r.w_up_weight[layer, :, 256 * column : 256 * column + 256])
                wide[column] = both[:256] + both[256:]

            lift(0)
            for column in range(4):
                lanes = slice(256 * column, 256 * column + 256)
                if column < 3:
                    lift(column + 1)
                for piece in range(4):
                    rows = pl.ds(64 * piece, 64)
                    z = wide[column, rows, :] + up_bias[:, lanes]
                    turn = z * turns[:, lanes]
                    turn = turn - jnp.round(turn)
                    square = turn * turn
                    s = z + square * polynomial(SIN_SQUARE, square) * inverse[:, lanes]
                    high, low = split(s)
                    part16[column, rows, :] = high
                    part16[4 + column, rows, :] = low
            both = jnp.concatenate(
                [jnp.concatenate([part16[4 * part + column] for column in range(4)], 1) for part in (0, 1)], 0
            )
            lowered = dot(both, r.w_down_weight[layer])
            out = y + lowered[:256] + lowered[256:] + down_bias
            out = jnp.where(valid_rows(start + 16, 256, layer)[0], out, 0.0)
            if layer == 0:
                for lanes in (0, 1):
                    r.first[lanes, at16(start + 32, 256), :] = out[:, 128 * lanes : 128 * lanes + 128]
            else:
                r.last[at16(start, 256), :] = out

        loop(own // 256, block)

    def shrink_forward_part():
        own = own_rows[0]
        first = r.first
        source = pl.multiple_of((1 - member) * (16 + own) + member * 32, 16)
        target = pl.multiple_of((1 - member) * 16 + member * (32 + own), 16)
        copy = remote(
            first.at[:, pl.ds(source, 16), :],
            first.at[:, pl.ds(target, 16), :],
            r.s_first.at[0],
            r.s_first.at[1],
            there(partner),
        )
        copy.start()
        copy.wait()
        extended = own_rows[1] + 16
        rows = pick(extended, 256)
        bias = inputs.shrink_bias[...].astype(F32).reshape(1, 256)

        def block(index):
            start = rows * index + 8
            total = bias
            for tap in range(3):
                taken = taken_rows(start - 16, rows, tap)
                total = total + dot_weight(taken, r.w_shrink_weight[tap])
            valid = valid_rows(start, rows, 1)[0]
            layers[1].a[at8(start, rows), :] = jnp.where(valid, total, 0.0)

        loop(extended // rows, block, True)

    def taken_rows(row, rows, tap):
        at = 32 + 2 * row - 1 + tap
        return jnp.concatenate([r.first[lanes, pl.ds(at, rows, stride=2), :] for lanes in (0, 1)], 1)

    def clear_layer():
        r.narrow_acc[...] = jnp.zeros((8, 8, 256), F32)
        r.wide_acc[...] = jnp.zeros((3, 8, 1024), F32)

    def later_backward(layer, advances={}):
        own = own_rows[layer]
        base = LATER_AT[layer]
        x, att, qh = layers[layer].x, layers[layer].att, layers[layer].qh
        wide, part16, grads = r.wide, r.half, r.grads
        doh = r.vt
        gain, bias = layer_rows(layer, 1)
        out_bias, up_bias = row_of(inputs.out_bias, layer), row_of(inputs.up_bias, layer)
        alpha, beta, inverse = snake_rows(layer)
        turns = alpha * (1.0 / math.pi)
        slope = alpha * inverse
        r.tall[...] = jnp.zeros((256, 1024), F32)
        clear_layer()
        narrow, broad = r.narrow_acc, r.wide_acc

        def block(index):
            start = 256 * index
            if layer == 0:
                dout = jnp.concatenate([r.first[lanes, at16(start + 32, 256), :] for lanes in (0, 1)], 1)
            else:
                dout = r.cot[at16(start, 256), :]
            joined = att[at16(start, 256), :]
            y = x[at16(start, 256), :] + dot_weight(joined, r.w_out_weight[layer]) + out_bias
            normed, scale = normed_layer(y)
            entered = normed * gain + bias
            entered_parts = jnp.concatenate(split(entered), 0)
            dout_parts = jnp.concatenate(split(dout), 0)
            dout_turned, entered_turned = split(jnp.transpose(dout)), split(jnp.transpose(entered))

            def lift(column):
                lanes = pl.ds(256 * column, 256)
                both = dot(entered_parts, r.w_up_weight[layer, :, lanes])
                wide[column] = both[:256] + both[256:]
                both = dot(dout_parts, r.w_down_weight[layer, lanes, :], NT)
                wide[4 + column] = both[:256] + both[256:]

            def weigh(column):
                lanes = pl.ds(256 * column, 256)
                r.tall[:, lanes] += dot_pair(dout_turned, (part16[column], part16[4 + column]))
                grads[pl.ds(base + UP + 256 * column, 256), :] += dot_pair(
                    entered_turned, (part16[8 + column], part16[12 + column])
                )

            lift(0)
            for column in range(4):
                lanes = slice(256 * column, 256 * column + 256)
                if column < 3:
                    lift(column + 1)
                if column > 0:
                    weigh(column - 1)
                dz_sum = turn_sum = sine_sum = jnp.zeros((8, 256), F32)
                for piece in range(8):
                    rows = pl.ds(32 * piece, 32)
                    z = wide[column, rows, :] + up_bias[:, lanes]
                    ds = wide[4 + column, rows, :]
                    whole = z * turns[:, lanes]
                    turn = whole - jnp.round(whole)
                    square = turn * turn
                    sine2 = square * polynomial(SIN_SQUARE, square)
                    twice = turn * polynomial(SIN_TWICE, square)
                    s = z + sine2 * inverse[:, lanes]
                    dtwice = ds * twice
                    dz = ds + dtwice * slope[:, lanes]
                    dz_sum += fold8(dz)
                    turn_sum += fold8(dtwice * whole)
                    sine_sum += fold8(ds * sine2)
                    high, low = split(s)
                    part16[column, rows, :] = high
                    part16[4 + column, rows, :] = low
                    high, low = split(dz)
                    part16[8 + column, rows, :] = high
                    part16[12 + column, rows, :] = low
                broad[0, :, lanes] += dz_sum
                broad[1, :, lanes] += turn_sum
                broad[2, :, lanes] += sine_sum

            weigh(3)

            def gathered(number):
                return jnp.concatenate([part16[number + column] for column in range(4)], 1)

            both = dot(jnp.concatenate([gathered(8), gathered(12)], 0), r.w_up_weight[layer], NT)
            dentered = both[:256] + both[256:]
            dy = dout + normed_back(dentered * gain, normed, scale)
            r.dy[at16(start, 256), :] = dy
            narrow[0] += fold8(dout)
            narrow[1] += fold8(dy)
            narrow[2] += fold8(dentered * normed)
            narrow[3] += fold8(dentered)
            grads[pl.ds(base + OUT, 128), :] += dot_pair(split(jnp.transpose(joined)), split(dy))
            datt = dot_weight(dy, r.w_out_weight[layer], NT)
            product = datt * joined
            sums = [
                jnp.sum(jnp.where(low_half, product, 0.0), axis=1, keepdims=True),
                jnp.sum(jnp.where(low_half, 0.0, product), axis=1, keepdims=True),
            ]
            aux = [three_lanes(jnp.broadcast_to(-total, (256, 128)), 0.0) for total in sums]
            tiles = query_tiles(datt, aux)
            pairs = key_tiles(datt, aux[0])
            for head in (0, 1):
                doh[head, at16(start, 256), 0:128] = tiles[head][0]
                doh[head, at16(start, 256), 128:256] = tiles[head][1]
                r.dd[head, at16(start, 256), :] = pairs[head][0]
                query = qh[head, at16(start, 256), 0:128].astype(F32)
                rest = pltpu.roll(qh[head, at16(start, 256), 128:256].astype(F32), 64, 1)
                r.qq[head, at16(start, 256), :] = jnp.where(low_half, query, rest).astype(BF)

        loop_with(own // 256, block, advances)

        def turn_down(index):
            taken = r.tall[:, pl.ds(256 * index, 256)]
            grads[at16(base + DOWN + 256 * index, 256), :] = jnp.transpose(taken)

        loop(4, turn_down, True)
        small = base + LATER_SMALL
        for number in range(4):
            grads[pl.ds(small + number, 1), :] = jnp.sum(narrow[number], axis=0, keepdims=True)
        bias_row = jnp.sum(broad[0], axis=0, keepdims=True)
        alpha_row = jnp.sum(broad[1], axis=0, keepdims=True) * (math.pi * inverse)
        beta_row = jnp.sum(broad[2], axis=0, keepdims=True) * (-beta * inverse * inverse)
        for number, row in enumerate((bias_row, alpha_row, beta_row)):
            for column in range(4):
                grads[pl.ds(small + 4 + 4 * number + column, 1), :] = row[:, 256 * column : 256 * column + 256]

    def dk_copy(layer):
        own = own_rows[layer]
        return remote(
            r.kv.at[at16((1 - member) * own, own)],
            r.dkr.at[pl.ds(0, own)],
            r.s_dk.at[2 * layer],
            r.s_dk.at[2 * layer + 1],
            there(partner),
        )

    def attend_backward(layer, advances={}, more={}):
        own = own_rows[layer]
        kh, vh, qh, kt, dkv = layers[layer].kh, layers[layer].vh, layers[layer].qh, layers[layer].kt, r.kv
        doh, dd, qq, part16 = r.vt, r.dd, r.qq, r.half
        blocks, queries = 2 * own // 256, own // 256
        for head in (0, 1):
            r.tall[pl.ds(128 * head, 128), 0:own] = jnp.zeros((128, own), F32)

        def block(index):
            key = lax.rem((1 - member) * queries + index, blocks)
            found = []
            for head in (0, 1):
                keys = kh[head, at16(256 * key, 256), :]
                values = vh[head, at16(256 * key, 256), :]
                for query in range(queries):
                    rows = pl.ds(256 * query, 256)
                    weights = jnp.exp2(dot(keys, qh[head, rows, :], NT))
                    grad = weights * dot(values, doh[head, rows, :], NT)
                    high, low = split(weights)
                    part16[query] = high
                    part16[4 + query] = low
                    high, low = split(grad)
                    part16[8 + query] = high
                    part16[12 + query] = low

                def gathered(number):
                    return jnp.concatenate([part16[number + query] for query in range(queries)], 1)

                dscores, dscores_rest = gathered(8), gathered(12)
                both = dot(jnp.concatenate([gathered(0), gathered(4)], 0), dd[head, 0:own, :])
                dvalue = both[:256] + both[256:]
                both = dot(jnp.concatenate([dscores, dscores_rest], 0), qq[head, 0:own, :])
                dkey = both[:256] + both[256:]
                found.append((dkey, dvalue))
                r.tall[pl.ds(128 * head, 128), 0:own] += dot(kt[head, key], dscores) + dot(kt[head, key], dscores_rest)
            for column, part in ((0, 0), (128, 1)):
                zeroth = found[0][part] + pltpu.roll(found[0][part], 64, 1)
                other = found[1][part] + pltpu.roll(found[1][part], 64, 1)
                joined = jnp.where(low_half, zeroth, other)
                if part == 0:
                    joined = joined * LN2
                dkv[at16(256 * key, 256), column : column + 128] = joined

        loop_with(queries, block, advances)
        copy = dk_copy(layer)
        copy.start()
        loop_with(queries, lambda index: block(index + queries), more)
        copy.wait()

    def qkv_backward(layer, advances={}):
        own = own_rows[layer]
        x, c2, dkv, dkr = layers[layer].x, layers[layer].c2, r.kv, r.dkr
        grads, narrow = r.grads, r.narrow_acc
        gain, bias = layer_rows(layer, 0)
        mean2, scale2, gain2, bias2 = norm_rows(layer, 1)
        number = 4 + 2 * layer
        clear_sums(number)

        def block(index):
            start = 256 * index
            lanes = pl.ds(start, 256)
            dquery = [r.tall[pl.ds(128 * head, 64), lanes] + r.tall[pl.ds(128 * head + 64, 64), lanes] for head in (0, 1)]
            dquery = jnp.transpose(jnp.concatenate(dquery, 0)) * 0.125
            dkeys = dkv[at16(member * own + start, 256), :] + dkr[at16(start, 256), :]
            packed = jnp.concatenate([dquery, dkeys], 1)
            normed, scale = normed_layer(x[at16(start, 256), :])
            entered = normed * gain + bias
            weight = dot_pair(split(jnp.transpose(entered)), split(packed))
            grads[pl.ds(QUERY_KEY_AT[layer], 256), :] += weight[:, :256]
            grads[pl.ds(VALUE_AT[layer], 128), 0:128] += weight[:128, 256:]
            grads[pl.ds(VALUE_AT[layer], 128), 128:256] += weight[128:, 256:]
            dentered = dot_weight(packed, r.w_qkv_weight[layer], NT)
            narrow[4] += fold8(dentered * normed)
            narrow[5] += fold8(dentered)
            dx = r.dy[at16(start, 256), :] + normed_back(dentered * gain, normed, scale)
            r.dx[at16(start + 16, 256), :] = dx
            unit = (c2[at16(start + 16, 256), :] - mean2) * scale2
            dvalue = dx * mish_slope(unit * gain2 + bias2)
            add_sums(number, dvalue, dvalue * unit)

        loop_with(own // 256, block, advances, True)
        for row in (4, 5):
            grads[pl.ds(SMALL_AT[layer] + row, 1), :] = jnp.sum(narrow[row], axis=0, keepdims=True)
        copy = send_sums(number)
        norm_grads(layer, 1)
        source = pl.multiple_of((1 - member) * (8 + own) + member * 16, 8)
        target = pl.multiple_of((1 - member) * 8 + member * (16 + own), 8)
        edge = remote(
            r.dx.at[pl.ds(source, 8)],
            r.dx.at[pl.ds(target, 8)],
            r.s_dx.at[2 * layer],
            r.s_dx.at[2 * layer + 1],
            there(partner),
        )
        edge.start()
        return copy, edge

    def norm_grads(layer, which):
        base, mine = SMALL_AT[layer], r.sums[4 + 2 * layer + (1 - which)]
        r.grads[pl.ds(base + 2 + which, 1), :] = jnp.sum(mine[0:8], axis=0, keepdims=True)
        r.grads[pl.ds(base + which, 1), :] = jnp.sum(mine[8:16], axis=0, keepdims=True)

    def norm_back(layer, which, copy):
        number = 4 + 2 * layer + (1 - which)
        copy.wait()
        mean, scale, gain, bias = norm_rows(layer, which)
        mine = r.sums[number]
        from_bias, from_gain = group_total((mine + r.sums_in[number]) * gain)
        return mean, scale, gain, bias, from_bias / counts[layer], from_gain / counts[layer]

    def weight_rows(at, taken, grad):
        left = [split(jnp.transpose(value)) for value in taken]
        high = jnp.concatenate([pair[0] for pair in left], 0)
        low = jnp.concatenate([pair[1] for pair in left], 0)
        r.grads[pl.ds(at, 256 * len(taken)), :] += dot_pair((high, low), split(grad))

    def conv_weight(source, target, own, at):
        def block(index):
            value = source[at8(256 * index + 8, 272), :]
            grad = target[at16(256 * index + 16, 256), :]
            weight_rows(at, [value[7 + tap : 263 + tap] for tap in range(3)], grad)

        loop(own // 256, block, True)

    def res_backward(layer, copies, advances=((),) * 4):
        own = own_rows[layer]
        extended = own + 16
        rows, small = pick(extended, 256), pick(extended, 256)
        a, c1, h, c2 = layers[layer].a, layers[layer].c1, layers[layer].h, layers[layer].c2
        dx, dv = r.dx, r.kv
        copy, edge = copies

        def res_part(index):
            value = a[at16(256 * index + 16, 256), :]
            weight_rows(RES_AT[layer], [value], dx[at16(256 * index + 16, 256), :])

        loop(own // 256, res_part, True)
        edge.wait()
        zero(dv, 0, 16)
        zero(dv, own + 16, 16)
        mean, scale, gain, bias, from_bias, from_gain = norm_back(layer, 1, copy)
        advance(*advances[0])

        def second(index):
            start = small * index + 8
            unit = (c2[at8(start, small), :] - mean) * scale
            grad = dx[at8(start, small), :] * mish_slope(unit * gain + bias)
            out = scale * (gain * grad - (from_bias + unit * from_gain))
            c2[at8(start, small), :] = jnp.where(valid_rows(start, small, layer)[0], out, 0.0)

        loop(extended // small, second)
        mean1, scale1, gain1, bias1 = norm_rows(layer, 0)
        number = 5 + 2 * layer
        clear_sums(number)
        r.narrow_acc[6] = jnp.zeros((8, 256), F32)

        def hidden(index):
            start = rows * index + 8
            taps = [r.w_conv_two[layer, 2 - tap] for tap in range(3)]
            out = conv_block(c2, rows * index, rows, taps, NT)
            valid, mine = valid_rows(start, rows, layer)
            out = jnp.where(valid, out, 0.0)
            unit = (c1[at8(start, rows), :] - mean1) * scale1
            grad = out * mish_slope(unit * gain1 + bias1)
            dv[at8(start, rows), :] = grad
            r.narrow_acc[6] += fold8(jnp.where(mine, out, 0.0))
            grad = jnp.where(mine, grad, 0.0)
            add_sums(number, grad, grad * unit)

        loop(extended // rows, hidden, True)
        copy = send_sums(number)
        norm_grads(layer, 0)
        summed = jnp.sum(r.narrow_acc[6], axis=0, keepdims=True)
        r.grads[pl.ds(SMALL_AT[layer] + 8, 16), :] = jnp.where(row16 == utterance, summed, 0.0)
        conv_weight(h, c2, own, CONV_TWO_AT[layer])

        advance(*advances[1])
        mean, scale, gain, bias, from_bias, from_gain = norm_back(layer, 0, copy)

        def first_part(index):
            start = small * index + 8
            unit = (c1[at8(start, small), :] - mean) * scale
            out = scale * (gain * dv[at8(start, small), :] - (from_bias + unit * from_gain))
            dv[at8(start, small), :] = jnp.where(valid_rows(start, small, layer)[0], out, 0.0)

        loop(extended // small, first_part)
        taps = [r.w_conv_one[layer, 2 - tap] for tap in range(3)]
        advance(*advances[2])
        conv_weight(a, dv, own, CONV_ONE_AT[layer])
        advance(*advances[3])

        def inputs(start, size):
            out = conv_block(dv, start, size, taps, NT)
            out = out + dot_weight(dx[at8(start + 8, size), :], r.w_res_weight[layer], NT)
            return jnp.where(valid_rows(start + 8, size, layer)[0], out, 0.0)

        if layer == 1:

            def block(index):
                r.da[at8(rows * index + 8, rows), :] = inputs(rows * index, rows)

            loop(extended // rows, block, True)
        else:

            def block(index):
                r.dy[at16(256 * index, 256), :] = inputs(256 * index + 8, 256)

            loop(own // 256, block, True)
            send_blocks(grad_sends[:GRAD_FIRST])

    def shrink_backward_part():
        da, own = r.da, own_rows[1]
        acc = r.narrow_acc
        acc[7] = jnp.zeros((8, 256), F32)

        def weights(index):
            grad = da[at16(256 * index + 16, 256), :]
            weight_rows(SHRINK_AT, [taken_rows(256 * index, 256, tap) for tap in range(3)], grad)

        loop(own // 256, weights, True)

        def block(index):
            value = da[at16(128 * index + 16, 144), :]
            both = jnp.concatenate(split(value), 0)
            parts = [dot(both, r.w_shrink_weight[tap], NT) for tap in range(3)]
            parts = [part[:144] + part[144:] for part in parts]
            even = parts[1][:128]
            odd = parts[2][:128] + parts[0][1:129]
            at = lax.broadcasted_iota(jnp.int32, (128, 256), 0) + 128 * index
            frame = 2 * (at + member * own)
            even = jnp.where(frame < length, even, 0.0)
            odd = jnp.where(frame + 1 < length, odd, 0.0)
            for lanes in (0, 1):
                columns = slice(128 * lanes, 128 * lanes + 128)
                r.first[lanes, pl.ds(32 + 256 * index, 128, stride=2), :] = even[:, columns]
                r.first[lanes, pl.ds(33 + 256 * index, 128, stride=2), :] = odd[:, columns]
            acc[7] += fold8(value[:128])

        loop(own // 128, block, True)

        r.grads[pl.ds(SMALL_AT[1] + 6, 1), :] = jnp.sum(acc[7], axis=0, keepdims=True)

    def block_sends(source, size, target, sems, pieces=1):
        found = []
        rows = size // pieces
        for piece in range(pieces):
            for item in range(half):
                found.append(
                    spread(
                        source.at[pl.ds(size * item + rows * piece, rows)],
                        target.at[place, pl.ds(rows * piece, rows)],
                        sems,
                        pieces * item + piece,
                        half * member + item,
                        pieces * place + piece,
                    )
                )
        return found

    def send_blocks(sends):
        for start, _ in sends:
            start()

    def finish_blocks(sends, size, target, sems, pieces=1):
        for _, wait_sent in sends:
            wait_sent()
        rows = size // pieces
        for item in range(depth):
            for piece in range(pieces):
                part = target.at[item, pl.ds(rows * piece, rows)]
                wait_arrived(part, sems, pieces * item + piece)

    def bucket(number):
        grads, sems, size = r.grads, r.s_total, BUCKET_ROWS[number]
        arrived = arrivals[0 if number > 2 else number]
        skipped = BUCKET_ROWS[3] if number == 4 else 0
        at_once = number > 2
        first = size // 512 * 256
        x, y = lax.rem(dp, 2), lax.div(dp, 2)
        over_x, over_y = (x, {"dp": dp + 1 - 2 * x, "seq": seq}), (y, {"dp": dp + 2 - 4 * y, "seq": seq})
        over_core = (member, there(partner))
        low, high = lax.rem(place, 2), lax.div(place, 2)
        over_z = [] if at_once else [(low, there(seq + 2 - 4 * low)), (high, there(seq + 4 - 8 * high))]
        lanes = []
        for at, count, order in (
            (BUCKET_AT[number], size - first, (over_x, over_y)),
            (BUCKET_AT[number] + size - first, first, (over_y, over_x)),
        ):
            lane = []
            for mine, device in [over_core, *order, *over_z]:
                count = count // 2
                lane.append((at + (1 - mine) * count, at + mine * count, count, device))
                at = at + mine * count
            lanes.append((lane, at, count))
        stages = len(lanes[0][0])

        def rows_at(ref, start, count):
            return ref.at[at8(start, count)]

        def wait_bytes(count, number_of):
            some = rows_at(grads, BUCKET_AT[number], count)
            pltpu.make_async_copy(some, some, sems.at[number, number_of]).wait()

        def total_of(stage):
            return sum(lane[stage][2] for lane, _, _ in lanes)

        def arriving(stage):
            if stage == 0:
                return r.core, CORE_AT[number]
            if stage < 3:
                return (arrived.near, arrived.next)[stage - 1], skipped // (4 * stage)
            return arrived.far, (stage - 3) * (size // 16)

        def pair_out(stage):
            into, at = arriving(stage)
            for lane, _, _ in lanes:
                given, _, count, device = lane[stage]
                remote(
                    rows_at(grads, given, count),
                    into.at[pl.ds(at, count)],
                    sems.at[number, 2 * stage],
                    sems.at[number, 2 * stage + 1],
                    device,
                ).start()
                at += count

        def pair_in(stage):
            wait_bytes(total_of(stage), 2 * stage)
            wait_bytes(total_of(stage), 2 * stage + 1)
            into, at = arriving(stage)
            for lane, _, _ in lanes:
                _, start, count, _ = lane[stage]
                add_all(start, count, [into.at[pl.ds(at, count)]])
                at += count

        def far_peers():
            for step in range(1, depth):
                yield step, lax.rem(place + step, depth)

        far_rows = size // 32

        def far_out():
            at = 3 * (skipped // 32)
            for _, start, count in lanes:
                piece = count // depth
                for step, other in far_peers():
                    remote(
                        rows_at(grads, start + other * piece, piece),
                        arrived.far.at[pl.ds(at + far_rows * (step - 1), piece)],
                        sems.at[number, 6],
                        sems.at[number, 7],
                        there(2 * other + member),
                    ).start()
                at += piece

        def far_in():
            wait_bytes(far_rows * (depth - 1), 6)
            wait_bytes(far_rows * (depth - 1), 7)
            at = 3 * (skipped // 32)
            for _, start, count in lanes:
                piece = count // depth
                parts = [arrived.far.at[pl.ds(at + far_rows * step, piece)] for step in range(depth - 1)]
                add_all(start + place * piece, piece, parts)
                at += piece

        def keep():
            for _, start, count in lanes:
                if at_once:
                    count = count // depth
                    start = start + place * count
                pltpu.make_async_copy(
                    rows_at(grads, start, count),
                    rows_at(grad_total, start, count),
                    sems.at[number, 20],
                ).start()

        def far_back():
            for _, start, count in lanes:
                piece = count // depth
                for _, other in far_peers():
                    remote(
                        rows_at(grads, start + place * piece, piece),
                        rows_at(grad_total, start + place * piece, piece),
                        sems.at[number, 8],
                        sems.at[number, 9],
                        there(2 * other + member),
                    ).start()

        def far_back_in():
            wait_bytes(far_rows * (depth - 1), 8)
            wait_bytes(far_rows * (depth - 1), 9)

        def pair_back(stage):
            source = grads if stage == stages - 1 and not at_once else grad_total
            for lane, _, _ in lanes:
                _, start, count, device = lane[stage]
                remote(
                    rows_at(source, start, count),
                    rows_at(grad_total, start, count),
                    sems.at[number, 18 - 2 * stage],
                    sems.at[number, 19 - 2 * stage],
                    device,
                ).start()

        def pair_back_in(stage):
            wait_bytes(total_of(stage), 18 - 2 * stage)
            wait_bytes(total_of(stage), 19 - 2 * stage)

        def add_all(start, count, parts):
            unit = pick8(count, 256)

            def piece(index):
                rows = at8(start + unit * index, unit)
                value = grads[rows, :]
                for part in parts:
                    value = value + part[at8(unit * index, unit), :]
                grads[rows, :] = value

            loop(count // unit, piece)

        turns = [(None, lambda: pair_out(0))]
        for stage in range(1, stages):
            turns.append((lambda stage=stage: pair_in(stage - 1), lambda stage=stage: pair_out(stage)))
        if at_once:
            turns.append((lambda: pair_in(stages - 1), far_out))
            turns.append((far_in, lambda: (far_back(), keep())))
            turns.append((lambda: (far_back_in(), wait_bytes(far_rows, 20)), lambda: pair_back(stages - 1)))
        else:
            turns.append((lambda: pair_in(stages - 1), lambda: (pair_back(stages - 1), keep())))
        for stage in range(stages - 1, 0, -1):

            def back_in(stage=stage):
                pair_back_in(stage)
                if stage == stages - 1 and not at_once:
                    wait_bytes(total_of(stage), 20)

            turns.append((back_in, lambda stage=stage: pair_back(stage - 1)))
        turns.append((lambda: pair_back_in(0), None))

        def step(which):
            for part in turns[which]:
                if part is not None:
                    part()

        return step

    all_steps = [bucket(number) for number in range(len(BUCKET_ROWS))]

    def advance(*pairs):
        for number, which in pairs:
            all_steps[number](which)

    def loop_with(count, body, advances, unrolled=False):
        if unrolled:
            for index in range(count):
                advance(*advances.get(index, ()))
                body(index)
            return

        def step(index):
            for at, pairs in advances.items():

                @pl.when(index == at)
                def _(pairs=pairs):
                    advance(*pairs)

            body(index)

        loop(count, step)

    last_sends = block_sends(r.last, 128, output, r.s_last)
    grad_sends = block_sends(r.dy, 256, input_grad, r.s_grad, 4)

    for item in range(depth):
        wait_arrived(a0.at[pl.ds(16 + 256 * item, 256)], r.s_frames, item)
    pltpu.make_async_copy(a0.at[pl.ds(8, 8)], a0.at[pl.ds(8, 8)], edge_sems.at[3, 0]).wait()

    def mask_frames(index):
        rows = at8(pick(own_rows[0] + 16, 256) * index + 8, pick(own_rows[0] + 16, 256))
        valid = valid_rows(pick(own_rows[0] + 16, 256) * index + 8, pick(own_rows[0] + 16, 256), 0)[0]
        a0[rows, :] = jnp.where(valid, a0[rows, :], 0.0)

    loop((own_rows[0] + 16) // pick(own_rows[0] + 16, 256), mask_frames)
    cot_sends = [
        spread(
            inputs.cotangent.at[item],
            r.cot.at[at16(128 * block_in_group, 128)],
            r.s_cot,
            item,
            2 * item + group_of_block,
            block_in_group,
        )
        for item in range(depth)
    ]
    for start, _ in cot_sends:
        start()
    res_forward(0)
    qkv_forward(0)
    keys_forward(0)
    later_forward(0)
    shrink_forward_part()
    res_forward(1)
    qkv_forward(1)
    keys_forward(1)
    later_forward(1)
    send_blocks(last_sends)
    for item in range(depth):
        wait_arrived(r.cot.at[pl.ds(128 * item, 128)], r.s_cot, item)

    def mask_cot(index):
        valid = valid_rows(128 * index + 16, 128, 1)[0]
        rows = at16(128 * index, 128)
        r.cot[rows, :] = jnp.where(valid, r.cot[rows, :], 0.0)

    loop(own_rows[1] // 128, mask_cot)
    later_backward(1)
    advance((0, 0))
    attend_backward(1, {}, {0: [(0, 1)]})
    copies = qkv_backward(1)
    res_backward(1, copies, [(), (), [(0, 2)], ()])
    shrink_backward_part()
    advance((1, 0), (0, 3))
    later_backward(0, {1: [(1, 1), (0, 4)], 2: [(0, 5)], 3: [(1, 2), (0, 6)]})
    advance((1, 3), (2, 0), (0, 7))
    attend_backward(0, {1: [(2, 1)], 2: [(1, 4), (0, 8)]}, {0: [(1, 5), (2, 2)], 2: [(1, 6)], 3: [(0, 9)]})
    advance((1, 7), (2, 3), (0, 10))
    copies = qkv_backward(0)
    advance((2, 4))
    res_backward(0, copies, [[(1, 8)], [(2, 5), (3, 0), (3, 1)], (), [(4, 0), (4, 1), (2, 6)]])
    advance((3, 2))
    send_blocks(grad_sends[4:5])
    advance((2, 7), (4, 2))
    send_blocks(grad_sends[5:7])
    advance((3, 3), (1, 9), (4, 3), (2, 8), (3, 4), (4, 4), (3, 5))
    send_blocks(grad_sends[7:9])
    advance((2, 9), (1, 10), (4, 5))
    send_blocks(grad_sends[9:11])
    advance((2, 10))
    send_blocks(grad_sends[11:12])
    advance((3, 6))
    send_blocks(grad_sends[12:13])
    advance((4, 6))
    send_blocks(grad_sends[13:15])
    advance((3, 7))
    send_blocks(grad_sends[15:16])
    advance((4, 7), (3, 8), (4, 8))
    for _, wait_sent in frame_sends + cot_sends:
        wait_sent()
    for after, before, _, _, item in edge_sends:

        @pl.when(sends_after & (seq != 2 * item + 1))
        def _(after=after):
            after.wait_send()

        @pl.when(sends_before & (seq != 2 * item))
        def _(before=before):
            before.wait_send()

    finish_blocks(last_sends, 128, output, r.s_last)
    finish_blocks(grad_sends, 256, input_grad, r.s_grad, 4)


def pick8(total, most):
    best = 8
    for size in range(8, most + 1, 8):
        if total % size == 0:
            best = size
    return best


GRAD_SHAPES = (
    (2, 3, 256, 256),
    (2, 3, 256, 256),
    (2, 256, 256),
    (2, 2, 256),
    (2, 2, 256),
    (2, 1024, 256),
    (2, 256),
    (2, 2, 256),
    (2, 2, 256),
    (2, 256, 384),
    (2, 128, 256),
    (2, 256),
    (2, 256, 1024),
    (2, 1024),
    (2, 1024),
    (2, 1024),
    (2, 1024, 256),
    (2, 256),
    (3, 256, 256),
    (256,),
)

class Gradients(typing.NamedTuple):
    conv_one: Any
    conv_two: Any
    res_weight: Any
    norm_gain: Any
    norm_bias: Any
    time_weight: Any
    time_bias: Any
    layer_gain: Any
    layer_bias: Any
    qkv_weight: Any
    out_weight: Any
    out_bias: Any
    up_weight: Any
    up_bias: Any
    snake_alpha: Any
    snake_beta: Any
    down_weight: Any
    down_bias: Any
    shrink_weight: Any
    shrink_bias: Any


def unpack_kernel(shape, total, last, grad, *refs):
    outs = Gradients(*refs[2:22])
    held, held_last, held_grad, held_time, sems, out_sems = refs[22:]
    loads, stores = [], []

    def rows(start, count):
        return total.at[pl.ds(start, count)], held.at[pl.ds(start, count)]

    def load(start, count):
        source, target = rows(start, count)
        loads.append(pltpu.make_async_copy(source, target, sems.at[len(loads)]))
        loads[-1].start()

    def store(start, count, target, lanes=pl.ds(0, 256)):
        source = held.at[pl.ds(start, count), lanes]
        stores.append((pltpu.make_async_copy(source, target, out_sems.at[len(stores)]), len(loads)))

    def move(start, count, target):
        load(start, count)
        store(start, count, target)

    for source, through, target in ((last, held_last, refs[0]), (grad, held_grad, refs[1])):
        loads.append(pltpu.make_async_copy(source, through, sems.at[len(loads)]))
        loads[-1].start()
        stores.append((pltpu.make_async_copy(through, target, out_sems.at[len(stores)]), len(loads)))
    load(EMBED_AT, 64)
    for layer in (1, 0):
        load(SMALL_AT[layer], 24)
        load(LATER_AT[layer] + LATER_SMALL, 16)
    small_loads = len(loads)
    for layer in (1, 0):
        later = LATER_AT[layer]
        for column in range(4):
            lanes = pl.ds(256 * column, 256)
            move(later + UP + 256 * column, 256, outs.up_weight.at[layer, :, lanes])
        move(later + DOWN, 1024, outs.down_weight.at[layer])
        move(later + OUT, 128, outs.out_weight.at[layer])
        for tap in range(3):
            move(CONV_TWO_AT[layer] + 256 * tap, 256, outs.conv_two.at[layer, tap])
        move(RES_AT[layer], 256, outs.res_weight.at[layer])
        move(QUERY_KEY_AT[layer], 256, outs.qkv_weight.at[layer, :, pl.ds(0, 256)])
        for tap in range(3):
            move(CONV_ONE_AT[layer] + 256 * tap, 256, outs.conv_one.at[layer, tap])
        load(VALUE_AT[layer], 128)
        for part in (0, 1):
            target = outs.qkv_weight.at[layer, pl.ds(128 * part, 128), pl.ds(256, 128)]
            store(VALUE_AT[layer], 128, target, pl.ds(128 * part, 128))
    for tap in range(3):
        move(SHRINK_AT + 256 * tap, 256, outs.shrink_weight.at[tap])
    waited = 0
    for copy, needed in stores:
        for number in range(waited, max(needed, small_loads)):
            loads[number].wait()
        waited = max(needed, small_loads)
        copy.start()
    for number in range(waited, len(loads)):
        loads[number].wait()
    for layer in (0, 1):
        later = held[pl.ds(LATER_AT[layer] + LATER_SMALL, 16), :]
        res = held[pl.ds(SMALL_AT[layer], 24), :]
        outs.norm_gain[layer] = res[0:2]
        outs.norm_bias[layer] = res[2:4]
        outs.layer_gain[layer, 0:1, :] = res[4:5]
        outs.layer_gain[layer, 1:2, :] = later[2:3]
        outs.layer_bias[layer, 0:1, :] = res[5:6]
        outs.layer_bias[layer, 1:2, :] = later[3:4]
        outs.down_bias[layer : layer + 1, :] = later[0:1]
        outs.out_bias[layer : layer + 1, :] = later[1:2]
        for column in range(4):
            lanes = slice(256 * column, 256 * column + 256)
            outs.up_bias[layer : layer + 1, lanes] = later[4 + column : 5 + column]
            outs.snake_alpha[layer : layer + 1, lanes] = later[8 + column : 9 + column]
            outs.snake_beta[layer : layer + 1, lanes] = later[12 + column : 13 + column]
        summed = res[8:24]
        outs.time_bias[layer : layer + 1, :] = jnp.sum(summed, axis=0, keepdims=True)
        right = split(summed)
        blank = jnp.zeros((128 - 16, 256), F32)
        for column in range(4):
            tall = jnp.concatenate([held[pl.ds(EMBED_AT + 16 * column, 16), :], blank], 0)
            left = split(jnp.transpose(tall)[:, 0:16])
            held_time[layer, pl.ds(256 * column, 256), :] = dot_pair(left, right)
        time_copy = pltpu.make_async_copy(held_time.at[layer], outs.time_weight.at[layer], out_sems.at[46 + layer])
        time_copy.start()
        stores.append((time_copy, 0))
    outs.shrink_bias[...] = held[pl.ds(SMALL_AT[1] + 6, 1), :]
    for copy, _ in stores:
        copy.wait()


def fused_local(shape, *args):
    groups = scratch_of(shape)
    given = Arguments(*args)
    specs = Arguments(*(WHOLE,) * 24)._replace(
        frames=ANY,
        lengths=pl.BlockSpec(memory_space=pltpu.SMEM),
        cotangent=ANY,
        conv_one=ANY,
        conv_two=ANY,
        res_weight=ANY,
        time_weight=ANY,
        qkv_weight=ANY,
        out_weight=ANY,
        up_weight=ANY,
        down_weight=ANY,
        shrink_weight=ANY,
    )
    output, input_grad, total = pl.pallas_call(
        lambda *refs: fused_kernel(shape, groups, *refs),
        out_shape=(
            jax.ShapeDtypeStruct(given.cotangent.shape, F32),
            jax.ShapeDtypeStruct(given.frames.shape, F32),
            jax.ShapeDtypeStruct((sum(BUCKET_ROWS), 256), F32),
        ),
        in_specs=list(specs),
        out_specs=(ANY,) * 3,
        scratch_shapes=[one for group in groups for one in group.values()],
        name="layers",
        compiler_params=pltpu.CompilerParams(
            collective_id=0, has_side_effects=True, vmem_limit_bytes=VMEM_BYTES
        ),
    )(*given)
    shapes = [s if len(s) > 1 else (1,) + s for s in GRAD_SHAPES]
    shapes = [output.shape, input_grad.shape] + shapes
    grads = pl.pallas_call(
        lambda *refs: unpack_kernel(shape, *refs),
        out_shape=tuple(jax.ShapeDtypeStruct(s, F32) for s in shapes),
        in_specs=[ANY] * 3,
        out_specs=(ANY, ANY)
        + tuple(
            Gradients(*(WHOLE,) * 20)._replace(
                time_weight=ANY,
                conv_one=ANY,
                conv_two=ANY,
                res_weight=ANY,
                qkv_weight=ANY,
                out_weight=ANY,
                up_weight=ANY,
                down_weight=ANY,
                shrink_weight=ANY,
            )
        ),
        scratch_shapes=[
            pltpu.VMEM((sum(BUCKET_ROWS), 256), F32),
            pltpu.VMEM(output.shape, F32),
            pltpu.VMEM(input_grad.shape, F32),
            pltpu.VMEM((2, 1024, 256), F32),
            pltpu.SemaphoreType.DMA((48,)),
            pltpu.SemaphoreType.DMA((48,)),
        ],
        name="unpack",
        compiler_params=pltpu.CompilerParams(vmem_limit_bytes=VMEM_BYTES),
    )(total, output, input_grad)
    grads = grads[:-1] + (grads[-1].reshape(256),)
    return tuple(grads)


VMEM_BYTES = 64 * 2**20 - 2**18


ARG_SPECS = (P("dp", "seq", None), P("dp", None), P("dp"), P("dp", "seq", None)) + (P(),) * 20
OUT_SPECS = (P("dp", "seq", None), P("dp", "seq", None)) + (P(),) * 20


def solution(mesh):
    shape = dict(mesh.shape)

    def local(*args):
        utterances, frames_in = args[0].shape[:2]
        if fits(shape, utterances, frames_in):
            return fused_local(shape, *args)
        return general_local(*args)

    return jax.shard_map(
        local, mesh=mesh, in_specs=ARG_SPECS, out_specs=OUT_SPECS, check_vma=False
    )
```

```python
import math
import typing
from types import SimpleNamespace
from typing import Any

import jax
import jax.numpy as jnp
from jax import lax
from jax.experimental import pallas as pl
from jax.experimental.pallas import tpu as pltpu
from jax.sharding import PartitionSpec as P

HEADS = 2
GROUPS = 8


precise = lax.Precision.HIGHEST
epsilon = 1e-05


def with_halo(value, sides, width):
    for axis, dim in sides:
        count, length = (lax.axis_size(axis), value.shape[dim])
        up = [(i, (i + 1) % count) for i in range(count - 1)]
        down = [(j, i) for i, j in up]
        last = lax.slice_in_dim(value, length - width, length, axis=dim)
        first = lax.slice_in_dim(value, 0, width, axis=dim)
        before = lax.ppermute(last, axis, up)
        after = lax.ppermute(first, axis, down)
        value = jnp.concatenate([before, value, after], axis=dim)
    return value


def shifted(value, axis, by):
    count = lax.axis_size(axis)
    pairs = [(i, i + by) for i in range(count) if 0 <= i + by < count]
    return lax.ppermute(value, axis, pairs)


def mish_curve(value_in):
    return value_in * jnp.tanh(jax.nn.softplus(value_in))


def conv_piece(padded, weight):
    frames_out = padded.shape[1] - 2
    summed = jnp.einsum("ufc,cd->ufd", padded[:, :frames_out], weight[0], precision=precise)
    summed = summed + jnp.einsum(
        "ufc,cd->ufd", padded[:, 1 : frames_out + 1], weight[1], precision=precise
    )
    return summed + jnp.einsum("ufc,cd->ufd", padded[:, 2:], weight[2], precision=precise)


def shrink_piece(padded, weight, bias_vec):
    span_len = padded.shape[1] - 1
    summed = jnp.einsum("ufc,cd->ufd", padded[:, 0:span_len:2], weight[0], precision=precise)
    summed = summed + jnp.einsum(
        "ufc,cd->ufd", padded[:, 1:span_len:2], weight[1], precision=precise
    )
    summed = summed + jnp.einsum(
        "ufc,cd->ufd", padded[:, 2 : span_len + 1 : 2], weight[2], precision=precise
    )
    return summed + bias_vec


def group_sums(conv_out, mask_row):
    utterances, frames_in, channels = conv_out.shape
    masked = conv_out * mask_row[:, :, None]
    shape_new = (utterances, frames_in, GROUPS, channels // GROUPS)
    first_sum = jnp.sum(masked.reshape(shape_new), axis=(1, 3))
    second_sum = jnp.sum((masked * conv_out).reshape(shape_new), axis=(1, 3))
    return (first_sum, second_sum)


def group_apply(conv_out, first_sum, second_sum, counts, gain_vec, bias_vec, mask_row):
    group_width = conv_out.shape[2] // GROUPS
    mean_val = first_sum / counts[:, None]
    var_val = second_sum / counts[:, None] - mean_val * mean_val
    scale_val = lax.rsqrt(var_val + epsilon)
    mean_full = jnp.repeat(mean_val, group_width, axis=1)[:, None, :]
    scale_full = jnp.repeat(scale_val, group_width, axis=1)[:, None, :]
    normed = (conv_out - mean_full) * scale_full * gain_vec + bias_vec
    return mish_curve(normed) * mask_row[:, :, None]


def time_piece(embedding, weight, bias_vec):
    return jnp.dot(mish_curve(embedding), weight, precision=precise) + bias_vec


def layer_norm(value_in, gain_vec, bias_vec):
    mean_val = jnp.mean(value_in, axis=-1, keepdims=True)
    centered = value_in - mean_val
    var_val = jnp.mean(centered * centered, axis=-1, keepdims=True)
    return centered * lax.rsqrt(var_val + epsilon) * gain_vec + bias_vec


def attend_in(value_in, gain_vec, bias_vec, qkv_weight):
    normed = layer_norm(value_in, gain_vec, bias_vec)
    packed = jnp.einsum("ufc,ce->ufe", normed, qkv_weight, precision=precise)
    inner_dim = packed.shape[2] // 3
    return (
        packed[:, :, :inner_dim],
        packed[:, :, inner_dim : 2 * inner_dim],
        packed[:, :, 2 * inner_dim :],
    )


def attend_out(value_in, queries, key_full, value_full, key_mask, later_weights):
    (
        out_weight,
        out_bias,
        gain_vec,
        bias_vec,
        up_weight,
        up_bias,
        snake_alpha,
        snake_beta,
        down_weight,
        down_bias,
    ) = later_weights
    utterances, frames_in, inner_dim = queries.shape
    head_dim = inner_dim // HEADS
    key_count = key_full.shape[1]
    query_heads = queries.reshape(utterances, frames_in, HEADS, head_dim)
    key_heads = key_full.reshape(utterances, key_count, HEADS, head_dim)
    value_heads = value_full.reshape(utterances, key_count, HEADS, head_dim)
    scores = jnp.einsum("uqhd,ukhd->uhqk", query_heads, key_heads, precision=precise) / math.sqrt(
        head_dim
    )
    scores = jnp.where(key_mask[:, None, None, :] > 0.5, scores, -1e30)
    scores = scores - jnp.max(scores, axis=3, keepdims=True)
    raised = jnp.exp(scores)
    weights_soft = raised / jnp.sum(raised, axis=3, keepdims=True)
    attended = jnp.einsum("uhqk,ukhd->uqhd", weights_soft, value_heads, precision=precise)
    attended = attended.reshape(utterances, frames_in, inner_dim)
    current = (
        value_in + jnp.einsum("ufe,ec->ufc", attended, out_weight, precision=precise) + out_bias
    )
    normed = layer_norm(current, gain_vec, bias_vec)
    raised_up = jnp.einsum("ufc,ce->ufe", normed, up_weight, precision=precise) + up_bias
    snake_out = raised_up + jnp.sin(raised_up * jnp.exp(snake_alpha)) ** 2 / (
        jnp.exp(snake_beta) + 1e-09
    )
    return (
        current + jnp.einsum("ufe,ec->ufc", snake_out, down_weight, precision=precise) + down_bias
    )


def layer_weights(stacked, layer_index):
    (
        conv_one,
        conv_two,
        res_weight,
        norm_gain,
        norm_bias,
        time_weight,
        time_bias,
        layer_gain,
        layer_bias,
        qkv_weight,
        out_weight,
        out_bias,
        up_weight,
        up_bias,
        snake_alpha,
        snake_beta,
        down_weight,
        down_bias,
    ) = stacked
    resnet_part = (
        conv_one[layer_index],
        conv_two[layer_index],
        res_weight[layer_index],
        norm_gain[layer_index],
        norm_bias[layer_index],
        time_weight[layer_index],
        time_bias[layer_index],
    )
    first_part = (layer_gain[layer_index, 0], layer_bias[layer_index, 0], qkv_weight[layer_index])
    later_part = (
        out_weight[layer_index],
        out_bias[layer_index],
        layer_gain[layer_index, 1],
        layer_bias[layer_index, 1],
        up_weight[layer_index],
        up_bias[layer_index],
        snake_alpha[layer_index],
        snake_beta[layer_index],
        down_weight[layer_index],
        down_bias[layer_index],
    )
    return (resnet_part, first_part, later_part)


def layer_grads(resnet_grads, first_grads, later_grads):
    gains = jnp.stack([first_grads[0], later_grads[2]])
    biases = jnp.stack([first_grads[1], later_grads[3]])
    return (
        resnet_grads
        + (gains, biases, first_grads[2], later_grads[0], later_grads[1])
        + later_grads[4:]
    )


def flatten_all(arrays):
    return jnp.concatenate([array_in.reshape(-1) for array_in in arrays])


def unflatten_all(flat, shapes):
    pieces = []
    offset_at = 0
    for shape_in in shapes:
        size_in = math.prod(shape_in)
        pieces.append(flat[offset_at : offset_at + size_in].reshape(shape_in))
        offset_at = offset_at + size_in
    return pieces


def frame_halo(value_in):
    return with_halo(value_in, (("seq", 1),), 1)


def rim_return(grad_padded):
    rim_rows = jnp.concatenate([grad_padded[:, :1], grad_padded[:, -1:]], axis=1)
    arrived = with_halo(rim_rows, (("seq", 1),), 1)
    inner_rows = grad_padded[:, 1:-1]
    inner_rows = inner_rows.at[:, 0].add(arrived[:, 0])
    return inner_rows.at[:, -1].add(arrived[:, 3])


def group_total(conv_out, mask_row):
    first_sum, second_sum = group_sums(conv_out, mask_row)
    return lax.psum((first_sum, second_sum), "seq")


def group_return(conv_out, mask_row, grad_first, grad_second):
    grad_first, grad_second = lax.psum((grad_first, grad_second), "seq")

    def sums_local(conv_in):
        return group_sums(conv_in, mask_row)

    pull_back = jax.vjp(sums_local, conv_out)[1]
    return pull_back((grad_first, grad_second))[0]


def resnet_forward(inputs, mask_row, counts, embedding, weights):
    conv_first, conv_second, res_weight, norm_gain, norm_bias, time_weight, time_bias = weights
    column = mask_row[:, :, None]
    masked = inputs * column
    padded_one = frame_halo(masked)
    first_conv = conv_piece(padded_one, conv_first)
    sums_one = group_total(first_conv, mask_row)
    hidden = group_apply(
        first_conv, sums_one[0], sums_one[1], counts, norm_gain[0], norm_bias[0], mask_row
    )
    hidden = hidden + time_piece(embedding, time_weight, time_bias)[:, None, :]
    padded_two = frame_halo(hidden * column)
    second = conv_piece(padded_two, conv_second)
    sums_two = group_total(second, mask_row)
    result = group_apply(
        second, sums_two[0], sums_two[1], counts, norm_gain[1], norm_bias[1], mask_row
    )
    result = result + jnp.einsum("ufc,cd->ufd", masked, res_weight, precision=precise)
    return (result, (masked, padded_one, first_conv, sums_one, padded_two, second, sums_two))


def resnet_backward(grad_out, saved, mask_row, counts, embedding, weights):
    conv_first, conv_second, res_weight, norm_gain, norm_bias, time_weight, time_bias = weights
    masked, padded_one, first_conv, sums_one, padded_two, second, sums_two = saved
    column = mask_row[:, :, None]

    def norm_local(conv_out, first_sum, second_sum, gain_vec, bias_vec):
        return group_apply(conv_out, first_sum, second_sum, counts, gain_vec, bias_vec, mask_row)

    pull_two = jax.vjp(norm_local, second, sums_two[0], sums_two[1], norm_gain[1], norm_bias[1])[1]
    grad_second, grad_first_sum, grad_second_sum, gain_grad_two, bias_grad_two = pull_two(grad_out)
    grad_second = grad_second + group_return(second, mask_row, grad_first_sum, grad_second_sum)
    grad_res = jnp.einsum("ufc,ufd->cd", masked, grad_out, precision=precise)
    grad_masked = jnp.einsum("ufd,cd->ufc", grad_out, res_weight, precision=precise)
    pull_conv = jax.vjp(conv_piece, padded_two, conv_second)[1]
    grad_padded, grad_conv_second = pull_conv(grad_second)
    grad_hidden = rim_return(grad_padded) * column

    def time_local(weight, bias_vec):
        return time_piece(embedding, weight, bias_vec)

    pull_time = jax.vjp(time_local, time_weight, time_bias)[1]
    grad_time_weight, grad_time_bias = pull_time(jnp.sum(grad_hidden, axis=1))
    pull_one = jax.vjp(
        norm_local, first_conv, sums_one[0], sums_one[1], norm_gain[0], norm_bias[0]
    )[1]
    grad_first, grad_first_sum, grad_second_sum, gain_grad_one, bias_grad_one = pull_one(
        grad_hidden
    )
    grad_first = grad_first + group_return(first_conv, mask_row, grad_first_sum, grad_second_sum)
    pull_conv = jax.vjp(conv_piece, padded_one, conv_first)[1]
    grad_padded, grad_conv_first = pull_conv(grad_first)
    grad_inputs = (rim_return(grad_padded) + grad_masked) * column
    grads = (
        grad_conv_first,
        grad_conv_second,
        grad_res,
        jnp.stack([gain_grad_one, gain_grad_two]),
        jnp.stack([bias_grad_one, bias_grad_two]),
        grad_time_weight,
        grad_time_bias,
    )
    return (grad_inputs, grads)


def block_forward(value_in, key_mask, first_weights, later_weights):
    queries, key_here, value_here = attend_in(
        value_in, first_weights[0], first_weights[1], first_weights[2]
    )
    key_full, value_full = (
        lax.all_gather(key_here, "seq", axis=1, tiled=True),
        lax.all_gather(value_here, "seq", axis=1, tiled=True),
    )
    result = attend_out(value_in, queries, key_full, value_full, key_mask, later_weights)
    kept_pair = (key_full, value_full)
    return (result, (value_in, queries, kept_pair))


def block_backward(grad_out, saved, key_mask, first_weights, later_weights):
    value_in, queries, kept_pair = saved
    key_full, value_full = kept_pair

    def attend_local(current, query_in, key_in, value_full_in, weights_in):
        return attend_out(current, query_in, key_in, value_full_in, key_mask, weights_in)

    pull_out = jax.vjp(attend_local, value_in, queries, key_full, value_full, later_weights)[1]
    grad_value, grad_queries, grad_keys, grad_values, grad_later = pull_out(grad_out)
    grad_keys, grad_values = (
        lax.psum_scatter(grad_keys, "seq", scatter_dimension=1, tiled=True),
        lax.psum_scatter(grad_values, "seq", scatter_dimension=1, tiled=True),
    )
    pull_in = jax.vjp(attend_in, value_in, first_weights[0], first_weights[1], first_weights[2])[1]
    grad_input, grad_gain, grad_bias, grad_qkv = pull_in((grad_queries, grad_keys, grad_values))
    return (grad_value + grad_input, (grad_gain, grad_bias, grad_qkv), grad_later)


def shrink_forward(value_in, mask_row, weight, bias_vec):
    masked = value_in * mask_row[:, :, None]
    carried = shifted(masked[:, -1:], "seq", 1)
    padded = jnp.concatenate([carried, masked], axis=1)
    return (shrink_piece(padded, weight, bias_vec), padded)


def shrink_backward(grad_out, padded, mask_row, weight, bias_vec):
    pull_back = jax.vjp(shrink_piece, padded, weight, bias_vec)[1]
    grad_padded, grad_weight, grad_bias = pull_back(grad_out)
    returned = shifted(grad_padded[:, :1], "seq", -1)
    grad_masked = grad_padded[:, 1:].at[:, -1:].add(returned)
    return (grad_masked * mask_row[:, :, None], grad_weight, grad_bias)


def general_local(
    frames,
    flow_embed,
    lengths,
    cotangent,
    conv_one,
    conv_two,
    res_weight,
    norm_gain,
    norm_bias,
    time_weight,
    time_bias,
    layer_gain,
    layer_bias,
    qkv_weight,
    out_weight,
    out_bias,
    up_weight,
    up_bias,
    snake_alpha,
    snake_beta,
    down_weight,
    down_bias,
    shrink_weight,
    shrink_bias,
):
    stacked = tuple(
        (
            weight_in.astype(jnp.float32)
            for weight_in in (
                conv_one,
                conv_two,
                res_weight,
                norm_gain,
                norm_bias,
                time_weight,
                time_bias,
                layer_gain,
                layer_bias,
                qkv_weight,
                out_weight,
                out_bias,
                up_weight,
                up_bias,
                snake_alpha,
                snake_beta,
                down_weight,
                down_bias,
            )
        )
    )
    shrink_w = shrink_weight.astype(jnp.float32)
    shrink_b = shrink_bias.astype(jnp.float32)
    seq_count = lax.axis_size("seq")
    seq_index = lax.axis_index("seq")
    frames_one = frames.shape[1]
    frames_two = frames_one // 2
    group_width = frames.shape[2] // GROUPS
    place_one = seq_index * frames_one + jnp.arange(frames_one, dtype=jnp.int32)
    place_two = seq_index * frames_two + jnp.arange(frames_two, dtype=jnp.int32)
    mask_one = (place_one[None, :] < lengths[:, None]).astype(jnp.float32)
    mask_two = (2 * place_two[None, :] < lengths[:, None]).astype(jnp.float32)
    keys_one = (
        jnp.arange(frames_one * seq_count, dtype=jnp.int32)[None, :] < lengths[:, None]
    ).astype(jnp.float32)
    keys_two = (
        2 * jnp.arange(frames_two * seq_count, dtype=jnp.int32)[None, :] < lengths[:, None]
    ).astype(jnp.float32)
    counts_one = (lengths * group_width).astype(jnp.float32)
    counts_two = ((lengths + 1) // 2 * group_width).astype(jnp.float32)
    res_zero, first_zero, later_zero = layer_weights(stacked, 0)
    res_one, first_one, later_one = layer_weights(stacked, 1)
    current, saved_first = resnet_forward(frames, mask_one, counts_one, flow_embed, res_zero)
    current, saved_second = block_forward(current, keys_one, first_zero, later_zero)
    current, saved_shrink = shrink_forward(current, mask_one, shrink_w, shrink_b)
    current, saved_third = resnet_forward(current, mask_two, counts_two, flow_embed, res_one)
    current, saved_fourth = block_forward(current, keys_two, first_one, later_one)
    output = current * mask_two[:, :, None]
    grad_now = cotangent * mask_two[:, :, None]
    grad_now, first_grads, later_grads = block_backward(
        grad_now, saved_fourth, keys_two, first_one, later_one
    )
    grad_now, resnet_grads = resnet_backward(
        grad_now, saved_third, mask_two, counts_two, flow_embed, res_one
    )
    grads_top = layer_grads(resnet_grads, first_grads, later_grads)
    shapes = [array_in.shape for array_in in grads_top]
    top_size = sum((math.prod(shape_in) for shape_in in shapes))
    grad_now, grad_shrink_w, grad_shrink_b = shrink_backward(
        grad_now, saved_shrink, mask_one, shrink_w, shrink_b
    )
    grad_now, first_grads, later_grads = block_backward(
        grad_now, saved_second, keys_one, first_zero, later_zero
    )
    grad_now, resnet_grads = resnet_backward(
        grad_now, saved_first, mask_one, counts_one, flow_embed, res_zero
    )
    grads_low = layer_grads(resnet_grads, first_grads, later_grads)
    low_flat = jnp.concatenate([flatten_all(grads_low), grad_shrink_w.reshape(-1), grad_shrink_b])
    summed_all = lax.psum(jnp.concatenate([flatten_all(grads_top), low_flat]), ("dp", "seq"))
    summed_top = summed_all[:top_size]
    summed_low = summed_all[top_size:]
    parts_top = unflatten_all(summed_top, shapes)
    parts_low = unflatten_all(summed_low, shapes + [shrink_w.shape, shrink_b.shape])
    grads_out = tuple(
        (jnp.stack([parts_low[number], parts_top[number]]) for number in range(len(shapes)))
    )
    return (output, grad_now) + grads_out + (parts_low[-2], parts_low[-1])


F32, BF = jnp.float32, jnp.bfloat16
MESH = pl.DeviceIdType.MESH
NN = (((1,), (0,)), ((), ()))
NT = (((1,), (1,)), ((), ()))
LOG2E = math.log2(math.e)
LN2 = math.log(2.0)
ANY = pl.BlockSpec(memory_space=pl.ANY)
WHOLE = pl.BlockSpec(memory_space=pltpu.VMEM)

SIN_SQUARE = (
    9.869604311707743,
    -32.4696711717196,
    42.72719633650352,
    -30.101465841168043,
    13.050098919638232,
    -3.356592620742283,
)
SIN_TWICE = (
    6.283184916495428,
    -41.3415892326883,
    81.59994332977455,
    -76.61447253116356,
    41.34288235420472,
    -12.4712435344911,
)

UP, DOWN, OUT, LATER_SMALL = 0, 1024, 2048, 2176
BUCKET_ROWS = (2304, 1280, 1792, 1280, 1024, 768, 768, 768)
BUCKET_AT = (0, 2304, 3584, 5376, 6656, 8448, 7680, 9216)
GRAD_FIRST = 6
CORE_AT, CORE_ROWS = (0, 1152, 1792, 0, 640, 1152, 1536, 1920), 2688
AT_ONCE = (0, 1, 2, 3, 4)
LATER_AT = (5376, 0)
CONV_TWO_AT = (7680, 2304)
RES_AT = (8448, 3072)
QUERY_KEY_AT = (8704, 3328)
CONV_ONE_AT = (9216, 3584)
VALUE_AT = (8960, 4352)
SMALL_AT = (9088, 4480)
SHRINK_AT, EMBED_AT = 4504, 5272


def pick(total, most):
    best = 16
    for size in range(16, most + 1, 16):
        if total % size == 0:
            best = size
    return best


def fits(shape, utterances, frames_in):
    return shape["seq"] == 2 * utterances and frames_in == 256 and shape["dp"] * utterances == 16


def split(value):
    high = value.astype(BF)
    return high, (value - high.astype(F32)).astype(BF)


def dot(left, right, dims=NN):
    return lax.dot_general(left, right, dims, preferred_element_type=F32)


def dot_weight(value, weight, dims=NN):
    rows = value.shape[0]
    both = dot(jnp.concatenate(split(value), 0), weight, dims)
    return both[:rows] + both[rows:]


def dot_pair(left, right):
    rows = left[0].shape[0]
    both = dot(jnp.concatenate(left, 0), right[0])
    return both[:rows] + both[rows:] + dot(left[0], right[1])


def fold8(value):
    return jnp.sum(value.reshape(value.shape[0] // 8, 8, value.shape[1]), axis=0)


def polynomial(coefficients, at):
    total = jnp.full_like(at, coefficients[-1])
    for number in coefficients[-2::-1]:
        total = total * at + number
    return total


def mish_terms(value):
    raised = jnp.exp(jnp.minimum(value, 20.0))
    top = raised * (raised + 2.0)
    return raised, top, 1.0 / (top + 2.0)


def mish_of(value):
    raised, top, inverse = mish_terms(value)
    return value * (top * inverse)


def mish_slope(value):
    raised, top, inverse = mish_terms(value)
    return inverse * (top + 4.0 * value * (raised * (raised + 1.0)) * inverse)


def loop(count, body, unrolled=False):
    if unrolled:
        for index in range(count):
            body(index)
        return

    def step(index, carry):
        body(index)
        return carry

    lax.fori_loop(0, count, step, 0)


def at8(start, size):
    return pl.ds(start if isinstance(start, int) else pl.multiple_of(start, 8), size)


def at16(start, size):
    return pl.ds(start if isinstance(start, int) else pl.multiple_of(start, 16), size)


class Arguments(typing.NamedTuple):
    frames: Any
    flow_embed: Any
    lengths: Any
    cotangent: Any
    conv_one: Any
    conv_two: Any
    res_weight: Any
    norm_gain: Any
    norm_bias: Any
    time_weight: Any
    time_bias: Any
    layer_gain: Any
    layer_bias: Any
    qkv_weight: Any
    out_weight: Any
    out_bias: Any
    up_weight: Any
    up_bias: Any
    snake_alpha: Any
    snake_beta: Any
    down_weight: Any
    down_bias: Any
    shrink_weight: Any
    shrink_bias: Any


def matrices(found):
    return (
        found.conv_one,
        found.conv_two,
        found.res_weight,
        found.qkv_weight,
        found.out_weight,
        found.up_weight,
        found.down_weight,
        found.shrink_weight,
    )


def scratch_of(shape):
    depth = shape["seq"] // 2
    own_rows = (256 * depth, 128 * depth)

    def array(*size):
        return pltpu.VMEM(size, F32)

    def short(*size):
        return pltpu.VMEM(size, BF)

    def semaphores(*size):
        return pltpu.SemaphoreType.DMA(size)

    shared = dict(
        w_conv_one=short(2, 3, 256, 256),
        w_conv_two=short(2, 3, 256, 256),
        w_res_weight=short(2, 256, 256),
        w_qkv_weight=short(2, 256, 384),
        w_out_weight=short(2, 128, 256),
        w_up_weight=short(2, 256, 1024),
        w_down_weight=short(2, 1024, 256),
        w_shrink_weight=short(3, 256, 256),
        first=array(2, own_rows[0] + 64, 128),
        cot=array(own_rows[1], 256),
        last=array(own_rows[1], 256),
        dy=array(own_rows[0], 256),
        kv=array(2 * own_rows[0], 256),
        dkr=array(own_rows[0], 256),
        dx=array(own_rows[0] + 32, 256),
        da=array(own_rows[1] + 32, 256),
        vt=short(2, own_rows[0], 256),
        dd=short(2, own_rows[0], 128),
        qq=short(2, own_rows[0], 128),
        tall=array(256, 4 * 256),
        wide=array(2 * depth, 256, 256),
        half=short(4 * depth, 256, 256),
        te=array(2, 8, 256),
        sums=array(8, 16, 256),
        sums_in=array(8, 16, 256),
        stat=array(4, 8, 256),
        narrow_acc=array(8, 8, 256),
        wide_acc=array(3, 8, 1024),
        gather=short(256, 256),
        grads=array(sum(BUCKET_ROWS), 256),
        core=array(CORE_ROWS, 256),
        s_weight=semaphores(16),
        s_frames=semaphores(4, depth),
        s_cot=semaphores(2, depth),
        s_last=semaphores(2, depth),
        s_grad=semaphores(2, 4 * depth),
        s_sums=semaphores(2, 8),
        s_kv=semaphores(4, depth),
        s_first=semaphores(2),
        s_dk=semaphores(4),
        s_dx=semaphores(4),
        s_total=semaphores(len(BUCKET_ROWS), 21),
    )
    layers = [
        dict(
            a=array(own + 32, 256),
            c1=array(own + 32, 256),
            h=array(own + 32, 256),
            c2=array(own + 32, 256),
            x=array(own, 256),
            att=array(own, 128),
            qh=short(2, own, 256),
            kh=short(2, 2 * own, 256),
            vh=short(2, 2 * own, 256),
            kt=short(2, own // 128, 128, 256),
        )
        for own in own_rows
    ]
    arrivals = [
        dict(
            near=array(size // 4, 256),
            next=array(size // 8, 256),
            far=array((depth - 1) * size // 32, 256),
        )
        for size in BUCKET_ROWS[:5]
    ]
    return [shared] + layers + arrivals


def named(groups, refs):
    found, at = [], 0
    for group in groups:
        found.append(SimpleNamespace(**dict(zip(group, refs[at : at + len(group)]))))
        at += len(group)
    return found


def fused_kernel(shape, groups, *refs):
    inputs = Arguments(*refs[:24])
    output, input_grad, grad_total = refs[24:27]
    r, *rest = named(groups, refs[27:])
    layers, arrivals = rest[:2], rest[2:]
    dp_count, seq_count = shape["dp"], shape["seq"]
    depth = seq_count // 2
    dp, seq = lax.axis_index("dp"), lax.axis_index("seq")
    member, place = lax.rem(seq, 2), lax.div(seq, 2)
    partner = seq + 1 - 2 * member
    half = depth
    own_rows = (256 * depth, 128 * depth)
    utterance = dp * depth + place
    length = inputs.lengths[place]
    lane128 = lax.broadcasted_iota(jnp.int32, (1, 128), 1)
    low_half = lane128 < 64

    def there(index):
        return {"dp": dp, "seq": index}

    def remote(source, target, sent, arrived, device):
        return pltpu.make_async_remote_copy(
            source, target, sent, arrived, device_id=device, device_id_type=MESH
        )

    held = (
        r.w_conv_one,
        r.w_conv_two,
        r.w_res_weight,
        r.w_qkv_weight,
        r.w_out_weight,
        r.w_up_weight,
        r.w_down_weight,
        r.w_shrink_weight,
    )
    weight_copies = [
        pltpu.make_async_copy(matrix, target, r.s_weight.at[number])
        for number, (matrix, target) in enumerate(zip(matrices(inputs), held))
    ]
    time_copies = []
    for layer in (0, 1):
        for part in range(4):
            time_copies.append(
                pltpu.make_async_copy(
                    inputs.time_weight.at[layer, pl.ds(256 * part, 256)],
                    r.half.at[4 * layer + part],
                    r.s_weight.at[len(held) + 4 * layer + part],
                )
            )

    def zero(ref, start, size):
        ref[pl.ds(start, size), :] = jnp.zeros((size, ref.shape[1]), F32)

    for mine, own in zip(layers, own_rows):
        for ref in (mine.a, mine.h, mine.c2):
            zero(ref, 0, 16)
            zero(ref, own + 16, 16)
    for part in (0, 1):
        zero(r.first.at[part], 0, 32)
        zero(r.first.at[part], own_rows[0] + 32, 32)
    zero(r.da, 0, 16)
    zero(r.da, own_rows[1] + 16, 16)
    for start in (0, own_rows[1] + 16, own_rows[0] + 16):
        zero(r.dx, start, 16)

    barrier = pltpu.get_barrier_semaphore()
    for step in range(1, seq_count):
        pl.semaphore_signal(
            barrier,
            inc=1,
            device_id=there(lax.rem(seq + step, seq_count)),
            device_id_type=MESH,
        )
    for step in range(1, dp_count):
        pl.semaphore_signal(
            barrier,
            inc=1,
            device_id={"dp": lax.rem(dp + step, dp_count), "seq": seq},
            device_id_type=MESH,
        )
    pl.semaphore_wait(barrier, seq_count - 1 + dp_count - 1)

    def spread(source_of, target_of, sems, item, target_seq, arrived_at):
        away = remote(
            source_of, target_of, sems.at[0, item], sems.at[1, arrived_at], there(target_seq)
        )
        here = pltpu.make_async_copy(source_of, target_of, sems.at[1, arrived_at])

        def start():
            @pl.when(target_seq != seq)
            def _():
                away.start()

            @pl.when(target_seq == seq)
            def _():
                here.start()

        def wait_sent():
            @pl.when(target_seq != seq)
            def _():
                away.wait_send()

        return start, wait_sent

    def wait_arrived(target, sems, index):
        pltpu.make_async_copy(target, target, sems.at[1, index]).wait()

    group_of_block = lax.div(seq, half)
    block_in_group = lax.rem(seq, half)
    frame_sends = []
    a0 = layers[0].a
    for turned in (2, 1, 3, 0):
        item = lax.rem(place + turned, depth)
        target = 2 * item + group_of_block
        frame_sends.append(
            spread(
                inputs.frames.at[item],
                a0.at[at16(16 + 256 * block_in_group, 256)],
                r.s_frames,
                item,
                target,
                block_in_group,
            )
        )
    for start, _ in frame_sends:
        start()
    edge_sems = r.s_frames
    edge_sends = []
    for item in range(depth):
        after = remote(
            inputs.frames.at[item, pl.ds(248, 8)],
            a0.at[pl.ds(8, 8)],
            edge_sems.at[2, item],
            edge_sems.at[3, 0],
            there(2 * item + 1),
        )
        before = remote(
            inputs.frames.at[item, pl.ds(0, 8)],
            a0.at[pl.ds(16 + own_rows[0], 8)],
            edge_sems.at[2, item],
            edge_sems.at[3, 0],
            there(2 * item),
        )
        after_here = pltpu.make_async_copy(
            inputs.frames.at[item, pl.ds(248, 8)], a0.at[pl.ds(8, 8)], edge_sems.at[3, 0]
        )
        before_here = pltpu.make_async_copy(
            inputs.frames.at[item, pl.ds(0, 8)],
            a0.at[pl.ds(16 + own_rows[0], 8)],
            edge_sems.at[3, 0],
        )
        edge_sends.append((after, before, after_here, before_here, item))
    sends_after = seq == half - 1
    sends_before = seq == half
    for after, before, after_here, before_here, item in edge_sends:

        @pl.when(sends_after & (seq != 2 * item + 1))
        def _(after=after):
            after.start()

        @pl.when(sends_after & (seq == 2 * item + 1))
        def _(after_here=after_here):
            after_here.start()

        @pl.when(sends_before & (seq != 2 * item))
        def _(before=before):
            before.start()

        @pl.when(sends_before & (seq == 2 * item))
        def _(before_here=before_here):
            before_here.start()

    for copy in time_copies + weight_copies:
        copy.start()
    def zero_grads(index):
        r.grads[at8(64 * index, 64), :] = jnp.zeros((64, 256), F32)

    loop(sum(BUCKET_ROWS) // 64, zero_grads)
    same_group = (
        lax.broadcasted_iota(jnp.int32, (256, 256), 0) // 32
        == lax.broadcasted_iota(jnp.int32, (256, 256), 1) // 32
    )
    r.gather[...] = jnp.where(same_group, 1.0, 0.0).astype(BF)
    for copy in time_copies:
        copy.wait()
    embedded = mish_of(inputs.flow_embed[pl.ds(place, 1), :])
    wide_embed = jnp.broadcast_to(embedded, (16, 1024))
    time_bias = inputs.time_bias[...].astype(F32)
    for layer in (0, 1):
        weight = jnp.concatenate([r.half[4 * layer + part] for part in range(4)], 0)
        projected = dot_weight(wide_embed, weight)
        r.te[layer] = projected[:8] + time_bias[layer : layer + 1]
    row16 = lax.broadcasted_iota(jnp.int32, (16, 256), 0)
    for part in range(4):
        chosen = jnp.where(
            row16 == utterance + 64 * member, embedded[:, 256 * part : 256 * part + 256], 0.0
        )
        r.grads[pl.ds(EMBED_AT + 16 * part, 16), :] = chosen
    for copy in weight_copies:
        copy.wait()

    def valid_rows(start, rows, layer):
        at = lax.broadcasted_iota(jnp.int32, (rows, 256), 0) + (start - 16)
        frame = at + member * own_rows[layer]
        valid = (frame >= 0) & (frame * (1 + layer) < length)
        return valid, valid & (at >= 0) & (at < own_rows[layer])

    def conv_block(source, start, rows, taps, dims=NN):
        value = source[at8(start, rows + 16), :]
        both = jnp.concatenate(split(value), 0)
        total = None
        for tap, weight in enumerate(taps):
            part = dot(both, weight, dims)
            part = part[: rows + 16] + part[rows + 16 :]
            part = part[7 + tap : 7 + tap + rows]
            total = part if total is None else total + part
        return total

    def send_sums(number):
        copy = remote(
            r.sums.at[number],
            r.sums_in.at[number],
            r.s_sums.at[0, number],
            r.s_sums.at[1, number],
            there(partner),
        )
        copy.start()
        return copy

    def group_total(value):
        high = value.astype(BF)
        rest = value - high.astype(F32)
        middle = rest.astype(BF)
        last = (rest - middle.astype(F32)).astype(BF)
        parts = dot(jnp.concatenate([high, middle, last], 0), r.gather[...])
        total = parts[0:16] + parts[16:32] + parts[32:48]
        return (
            jnp.sum(total[0:8], axis=0, keepdims=True),
            jnp.sum(total[8:16], axis=0, keepdims=True),
        )

    counts = (
        (length * 32).astype(F32),
        (lax.div(length + 1, 2) * 32).astype(F32),
    )

    def forward_sums(layer, which, copy):
        number = 2 * layer + which
        copy.wait()
        first_sum, second_sum = group_total(r.sums[number] + r.sums_in[number])
        mean = first_sum / counts[layer]
        variance = second_sum / counts[layer] - mean * mean
        r.stat[number, 0:1, :] = mean
        r.stat[number, 1:2, :] = lax.rsqrt(variance + epsilon)

    def norm_rows(layer, which):
        number = 2 * layer + which
        gain = inputs.norm_gain[...].astype(F32)[layer, which : which + 1]
        bias = inputs.norm_bias[...].astype(F32)[layer, which : which + 1]
        return r.stat[number, 0:1, :], r.stat[number, 1:2, :], gain, bias

    def add_sums(number, first, second):
        r.sums[number, 0:8, :] += fold8(first)
        r.sums[number, 8:16, :] += fold8(second)

    def clear_sums(number):
        r.sums[number] = jnp.zeros((16, 256), F32)

    def normed_layer(value):
        mean = jnp.mean(value, axis=1, keepdims=True)
        centered = value - mean
        variance = jnp.mean(centered * centered, axis=1, keepdims=True)
        scale = lax.rsqrt(variance + epsilon)
        return centered * scale, scale

    def normed_back(grad, normed, scale):
        return scale * (
            grad
            - jnp.mean(grad, axis=1, keepdims=True)
            - normed * jnp.mean(grad * normed, axis=1, keepdims=True)
        )

    def layer_rows(layer, which):
        gain = inputs.layer_gain[...].astype(F32)[layer, which : which + 1]
        bias = inputs.layer_bias[...].astype(F32)[layer, which : which + 1]
        return gain, bias

    def row_of(ref, layer):
        return ref[...].astype(F32)[layer : layer + 1]

    def keys_aux(start, rows, layer):
        lane = lax.broadcasted_iota(jnp.int32, (rows, 128), 1)
        key = lax.broadcasted_iota(jnp.int32, (rows, 128), 0) + start
        masked = jnp.where(key * (1 + layer) < length, 0.0, -1e30)
        ones = jnp.where((lane >= 65) & (lane < 68), 1.0, 0.0)
        return jnp.where(lane == 64, masked, ones)

    def both_heads(value):
        high = value.astype(BF).astype(F32)
        low = value - high
        return high, low, pltpu.roll(high, 64, 1), pltpu.roll(low, 64, 1)

    def key_tiles(value, aux):
        high, low, high_turned, low_turned = both_heads(value)
        tiles = (
            (jnp.where(low_half, high, low_turned), jnp.where(low_half, high, aux)),
            (jnp.where(low_half, high_turned, low), jnp.where(low_half, high_turned, aux)),
        )
        return [(a.astype(BF), b.astype(BF)) for a, b in tiles]

    def query_tiles(value, aux):
        high, low, high_turned, low_turned = both_heads(value)
        tiles = (
            (jnp.where(low_half, high, high_turned), jnp.where(low_half, low, aux[0])),
            (jnp.where(low_half, high_turned, high), jnp.where(low_half, low_turned, aux[1])),
        )
        return [(a.astype(BF), b.astype(BF)) for a, b in tiles]

    def three_lanes(value, first):
        lane = lax.broadcasted_iota(jnp.int32, value.shape, 1)
        high = value.astype(BF).astype(F32)
        rest = value - high
        middle = rest.astype(BF).astype(F32)
        spread_out = jnp.where(lane == 66, middle, rest - middle)
        spread_out = jnp.where(lane == 65, high, spread_out)
        spread_out = jnp.where(lane == 64, first, spread_out)
        return jnp.where((lane >= 64) & (lane < 68), spread_out, 0.0)

    def res_forward(layer):
        own = own_rows[layer]
        extended = own + 16
        rows = pick(extended, 256)
        small = pick(extended, 256)
        a, c1, h, c2 = layers[layer].a, layers[layer].c1, layers[layer].h, layers[layer].c2

        def convolve(source, target, weights, number):
            clear_sums(number)

            def block(index):
                out = conv_block(source, rows * index, rows, [weights[layer, k] for k in range(3)])
                start = rows * index + 8
                target[at8(start, rows), :] = out
                kept = jnp.where(valid_rows(start, rows, layer)[1], out, 0.0)
                add_sums(number, kept, kept * out)

            loop(extended // rows, block, True)
            return send_sums(number)

        copy = convolve(a, c1, r.w_conv_one, 2 * layer)
        forward_sums(layer, 0, copy)
        mean, scale, gain, bias = norm_rows(layer, 0)
        added = r.te[layer, 0:1, :]

        def normed(index):
            start = small * index + 8
            value = (c1[at8(start, small), :] - mean) * scale * gain + bias
            valid = valid_rows(start, small, layer)[0]
            h[at8(start, small), :] = jnp.where(valid, mish_of(value) + added, 0.0)

        loop(extended // small, normed, True)
        copy = convolve(h, c2, r.w_conv_two, 2 * layer + 1)

        def residual(index):
            value = a[at16(256 * index + 16, 256), :]
            layers[layer].x[at16(256 * index, 256), :] = dot_weight(value, r.w_res_weight[layer])

        loop(own // 256, residual, True)
        forward_sums(layer, 1, copy)

    def keys_of(layer):
        return (r.kv, r.dy)[layer]

    def kv_copy(layer, index):
        own = own_rows[layer]
        part = keys_of(layer).at[at16(member * own + 256 * index, 256)]
        return remote(
            part,
            part,
            r.s_kv.at[2 * layer, index],
            r.s_kv.at[2 * layer + 1, index],
            there(partner),
        )

    def qkv_forward(layer):
        own = own_rows[layer]
        c2, x, kv, qh = layers[layer].c2, layers[layer].x, keys_of(layer), layers[layer].qh
        mean, scale, gain, bias = norm_rows(layer, 1)
        layer_gain, layer_bias = layer_rows(layer, 0)
        lane = lax.broadcasted_iota(jnp.int32, (256, 128), 1)
        aux = jnp.where(lane == 64, 1.0, 0.0)

        def block(index):
            start = 256 * index
            value = (c2[at16(start + 16, 256), :] - mean) * scale * gain + bias
            valid = valid_rows(start + 16, 256, layer)[0]
            out = jnp.where(valid, mish_of(value), 0.0) + x[at16(start, 256), :]
            x[at16(start, 256), :] = out
            packed = dot_weight(
                normed_layer(out)[0] * layer_gain + layer_bias, r.w_qkv_weight[layer]
            )
            kv[at16(member * own + start, 256), :] = packed[:, 128:]
            kv_copy(layer, index).start()
            tiles = query_tiles(packed[:, :128] * (LOG2E / 8.0), (aux, aux))
            for head in (0, 1):
                qh[head, at16(start, 256), 0:128] = tiles[head][0]
                qh[head, at16(start, 256), 128:256] = tiles[head][1]

        loop(own // 256, block, True)

    def keys_forward(layer):
        own = own_rows[layer]
        kv, kh, vh, kt, vt = keys_of(layer), layers[layer].kh, layers[layer].vh, layers[layer].kt, r.vt
        mine = own // 256

        def block(number):
            index = lax.rem(member * mine + number, 2 * mine)
            start = 256 * index
            value = kv[at16(start, 256), :]
            aux = keys_aux(start, 256, layer)
            for part, target in ((value[:, :128], kh), (value[:, 128:], vh)):
                tiles = key_tiles(part, aux)
                for head in (0, 1):
                    target[head, at16(start, 256), 0:128] = tiles[head][0]
                    target[head, at16(start, 256), 128:256] = tiles[head][1]
            for column in (0, 128):
                high, low = split(jnp.transpose(value[:, column : column + 128]))
                for head in (0, 1):
                    both = jnp.concatenate([high[64 * head : 64 * head + 64], low[64 * head : 64 * head + 64]], 0)
                    if column == 0:
                        kt[head, index] = both
                    else:
                        vt[head, at16(128 * index, 128), :] = both

        loop(mine, block)
        for index in range(mine):
            kv_copy(layer, index).wait()
        loop(mine, lambda number: block(mine + number))

    def snake_rows(layer):
        alpha = jnp.exp(row_of(inputs.snake_alpha, layer))
        beta = jnp.exp(row_of(inputs.snake_beta, layer))
        return alpha, beta, 1.0 / (beta + 1e-9)

    def later_forward(layer):
        own = own_rows[layer]
        x, att, kh, qh, vt = layers[layer].x, layers[layer].att, layers[layer].kh, layers[layer].qh, r.vt
        wide, part16 = r.wide, r.half
        blocks = 2 * own // 256
        gain, bias = layer_rows(layer, 1)
        out_bias, down_bias, up_bias = row_of(inputs.out_bias, layer), row_of(inputs.down_bias, layer), row_of(inputs.up_bias, layer)
        alpha, beta, inverse = snake_rows(layer)
        turns = alpha * (1.0 / math.pi)

        def block(index):
            start = 256 * index
            parts = [(head, part) for head in (0, 1) for part in (0, 1)]
            keys_in = blocks // 2
            queries = [qh[head, at16(start, 256), :] for head in (0, 1)]
            most, total, found = {}, {}, {}

            def scores(unit):
                head, part = parts[unit]
                highest = jnp.full((8, 256), -3e38, F32)
                for key in range(keys_in):
                    at = 256 * (keys_in * part + key)
                    out = dot(kh[head, at : at + 256, :], queries[head], NT)
                    wide[4 * (unit % 2) + key] = out
                    highest = jnp.maximum(highest, jnp.max(out.reshape(32, 8, 256), axis=0))
                most[unit] = jnp.max(highest, axis=0, keepdims=True)
                if part == 1:
                    most[unit] = jnp.maximum(most[unit], most[unit - 1])

            def exponentials(unit):
                summed = jnp.zeros((8, 256), F32)
                for key in range(keys_in):
                    for piece in range(4):
                        rows = pl.ds(64 * piece, 64)
                        raised = jnp.exp2(wide[4 * (unit % 2) + key, rows, :] - most[unit])
                        summed = summed + fold8(raised)
                        high, low = split(raised)
                        part16[8 * (unit % 2) + key, rows, :] = high
                        part16[8 * (unit % 2) + 4 + key, rows, :] = low
                total[unit] = jnp.sum(summed, axis=0, keepdims=True)

            def weighted(unit):
                head, part = parts[unit]
                first_key = keys_in * part
                values = jnp.concatenate(
                    [vt[head, 128 * key : 128 * key + 128, :] for key in range(first_key, first_key + keys_in)], 1
                )
                out = None
                for which in (0, 4):
                    at = 8 * (unit % 2) + which
                    taken = jnp.concatenate([part16[at + key] for key in range(keys_in)], 0)
                    taken = dot(values, taken)
                    out = taken if out is None else out + taken
                found[unit] = out[:64] + out[64:]

            scores(0)
            for unit in range(4):
                if unit < 3:
                    scores(unit + 1)
                if unit > 0:
                    weighted(unit - 1)
                exponentials(unit)
            weighted(3)
            attended = []
            for head in (0, 1):
                before, after = 2 * head, 2 * head + 1
                lowered = jnp.exp2(most[before] - most[after])
                summed = total[before] * lowered + total[after]
                attended.append((found[before] * lowered + found[after]) * (1.0 / summed))
                level = jnp.transpose(jnp.broadcast_to(most[after] + jnp.log2(summed), (128, 256)))
                aux = three_lanes(-level, 1.0)
                old = qh[head, at16(start, 256), 128:256]
                qh[head, at16(start, 256), 128:256] = jnp.where(low_half, old, aux.astype(BF))
            joined = jnp.transpose(jnp.concatenate(attended, 0))
            att[at16(start, 256), :] = joined
            y = x[at16(start, 256), :] + dot_weight(joined, r.w_out_weight[layer]) + out_bias
            entered = jnp.concatenate(split(normed_layer(y)[0] * gain + bias), 0)

            def lift(column):
                both = dot(entered, r.w_up_weight[layer, :, 256 * column : 256 * column + 256])
                wide[column] = both[:256] + both[256:]

            lift(0)
            for column in range(4):
                lanes = slice(256 * column, 256 * column + 256)
                if column < 3:
                    lift(column + 1)
                for piece in range(4):
                    rows = pl.ds(64 * piece, 64)
                    z = wide[column, rows, :] + up_bias[:, lanes]
                    turn = z * turns[:, lanes]
                    turn = turn - jnp.round(turn)
                    square = turn * turn
                    s = z + square * polynomial(SIN_SQUARE, square) * inverse[:, lanes]
                    high, low = split(s)
                    part16[column, rows, :] = high
                    part16[4 + column, rows, :] = low
            both = jnp.concatenate(
                [jnp.concatenate([part16[4 * part + column] for column in range(4)], 1) for part in (0, 1)], 0
            )
            lowered = dot(both, r.w_down_weight[layer])
            out = y + lowered[:256] + lowered[256:] + down_bias
            out = jnp.where(valid_rows(start + 16, 256, layer)[0], out, 0.0)
            if layer == 0:
                for lanes in (0, 1):
                    r.first[lanes, at16(start + 32, 256), :] = out[:, 128 * lanes : 128 * lanes + 128]
            else:
                r.last[at16(start, 256), :] = out

        loop(own // 256, block)

    def shrink_forward_part():
        own = own_rows[0]
        first = r.first
        source = pl.multiple_of((1 - member) * (16 + own) + member * 32, 16)
        target = pl.multiple_of((1 - member) * 16 + member * (32 + own), 16)
        copy = remote(
            first.at[:, pl.ds(source, 16), :],
            first.at[:, pl.ds(target, 16), :],
            r.s_first.at[0],
            r.s_first.at[1],
            there(partner),
        )
        copy.start()
        copy.wait()
        extended = own_rows[1] + 16
        rows = pick(extended, 256)
        bias = inputs.shrink_bias[...].astype(F32).reshape(1, 256)

        def block(index):
            start = rows * index + 8
            total = bias
            for tap in range(3):
                taken = taken_rows(start - 16, rows, tap)
                total = total + dot_weight(taken, r.w_shrink_weight[tap])
            valid = valid_rows(start, rows, 1)[0]
            layers[1].a[at8(start, rows), :] = jnp.where(valid, total, 0.0)

        loop(extended // rows, block, True)

    def taken_rows(row, rows, tap):
        at = 32 + 2 * row - 1 + tap
        return jnp.concatenate([r.first[lanes, pl.ds(at, rows, stride=2), :] for lanes in (0, 1)], 1)

    def clear_layer():
        r.narrow_acc[...] = jnp.zeros((8, 8, 256), F32)
        r.wide_acc[...] = jnp.zeros((3, 8, 1024), F32)

    def later_backward(layer, advances={}):
        own = own_rows[layer]
        base = LATER_AT[layer]
        x, att, qh = layers[layer].x, layers[layer].att, layers[layer].qh
        wide, part16, grads = r.wide, r.half, r.grads
        doh = r.vt
        gain, bias = layer_rows(layer, 1)
        out_bias, up_bias = row_of(inputs.out_bias, layer), row_of(inputs.up_bias, layer)
        alpha, beta, inverse = snake_rows(layer)
        turns = alpha * (1.0 / math.pi)
        slope = alpha * inverse
        r.tall[...] = jnp.zeros((256, 1024), F32)
        clear_layer()
        narrow, broad = r.narrow_acc, r.wide_acc

        def block(index):
            start = 256 * index
            if layer == 0:
                dout = jnp.concatenate([r.first[lanes, at16(start + 32, 256), :] for lanes in (0, 1)], 1)
            else:
                dout = r.cot[at16(start, 256), :]
            joined = att[at16(start, 256), :]
            y = x[at16(start, 256), :] + dot_weight(joined, r.w_out_weight[layer]) + out_bias
            normed, scale = normed_layer(y)
            entered = normed * gain + bias
            entered_parts = jnp.concatenate(split(entered), 0)
            dout_parts = jnp.concatenate(split(dout), 0)
            dout_turned, entered_turned = split(jnp.transpose(dout)), split(jnp.transpose(entered))

            def lift(column):
                lanes = pl.ds(256 * column, 256)
                both = dot(entered_parts, r.w_up_weight[layer, :, lanes])
                wide[column] = both[:256] + both[256:]
                both = dot(dout_parts, r.w_down_weight[layer, lanes, :], NT)
                wide[4 + column] = both[:256] + both[256:]

            def weigh(column):
                lanes = pl.ds(256 * column, 256)
                r.tall[:, lanes] += dot_pair(dout_turned, (part16[column], part16[4 + column]))
                grads[pl.ds(base + UP + 256 * column, 256), :] += dot_pair(
                    entered_turned, (part16[8 + column], part16[12 + column])
                )

            lift(0)
            for column in range(4):
                lanes = slice(256 * column, 256 * column + 256)
                if column < 3:
                    lift(column + 1)
                if column > 0:
                    weigh(column - 1)
                dz_sum = turn_sum = sine_sum = jnp.zeros((8, 256), F32)
                for piece in range(8):
                    rows = pl.ds(32 * piece, 32)
                    z = wide[column, rows, :] + up_bias[:, lanes]
                    ds = wide[4 + column, rows, :]
                    whole = z * turns[:, lanes]
                    turn = whole - jnp.round(whole)
                    square = turn * turn
                    sine2 = square * polynomial(SIN_SQUARE, square)
                    twice = turn * polynomial(SIN_TWICE, square)
                    s = z + sine2 * inverse[:, lanes]
                    dtwice = ds * twice
                    dz = ds + dtwice * slope[:, lanes]
                    dz_sum += fold8(dz)
                    turn_sum += fold8(dtwice * whole)
                    sine_sum += fold8(ds * sine2)
                    high, low = split(s)
                    part16[column, rows, :] = high
                    part16[4 + column, rows, :] = low
                    high, low = split(dz)
                    part16[8 + column, rows, :] = high
                    part16[12 + column, rows, :] = low
                broad[0, :, lanes] += dz_sum
                broad[1, :, lanes] += turn_sum
                broad[2, :, lanes] += sine_sum

            weigh(3)

            def gathered(number):
                return jnp.concatenate([part16[number + column] for column in range(4)], 1)

            both = dot(jnp.concatenate([gathered(8), gathered(12)], 0), r.w_up_weight[layer], NT)
            dentered = both[:256] + both[256:]
            dy = dout + normed_back(dentered * gain, normed, scale)
            r.dy[at16(start, 256), :] = dy
            narrow[0] += fold8(dout)
            narrow[1] += fold8(dy)
            narrow[2] += fold8(dentered * normed)
            narrow[3] += fold8(dentered)
            grads[pl.ds(base + OUT, 128), :] += dot_pair(split(jnp.transpose(joined)), split(dy))
            datt = dot_weight(dy, r.w_out_weight[layer], NT)
            product = datt * joined
            sums = [
                jnp.sum(jnp.where(low_half, product, 0.0), axis=1, keepdims=True),
                jnp.sum(jnp.where(low_half, 0.0, product), axis=1, keepdims=True),
            ]
            aux = [three_lanes(jnp.broadcast_to(-total, (256, 128)), 0.0) for total in sums]
            tiles = query_tiles(datt, aux)
            pairs = key_tiles(datt, aux[0])
            for head in (0, 1):
                doh[head, at16(start, 256), 0:128] = tiles[head][0]
                doh[head, at16(start, 256), 128:256] = tiles[head][1]
                r.dd[head, at16(start, 256), :] = pairs[head][0]
                query = qh[head, at16(start, 256), 0:128].astype(F32)
                rest = pltpu.roll(qh[head, at16(start, 256), 128:256].astype(F32), 64, 1)
                r.qq[head, at16(start, 256), :] = jnp.where(low_half, query, rest).astype(BF)

        loop_with(own // 256, block, advances)

        def turn_down(index):
            taken = r.tall[:, pl.ds(256 * index, 256)]
            grads[at16(base + DOWN + 256 * index, 256), :] = jnp.transpose(taken)

        loop(4, turn_down, True)
        small = base + LATER_SMALL
        for number in range(4):
            grads[pl.ds(small + number, 1), :] = jnp.sum(narrow[number], axis=0, keepdims=True)
        bias_row = jnp.sum(broad[0], axis=0, keepdims=True)
        alpha_row = jnp.sum(broad[1], axis=0, keepdims=True) * (math.pi * inverse)
        beta_row = jnp.sum(broad[2], axis=0, keepdims=True) * (-beta * inverse * inverse)
        for number, row in enumerate((bias_row, alpha_row, beta_row)):
            for column in range(4):
                grads[pl.ds(small + 4 + 4 * number + column, 1), :] = row[:, 256 * column : 256 * column + 256]

    def dk_copy(layer):
        own = own_rows[layer]
        return remote(
            r.kv.at[at16((1 - member) * own, own)],
            r.dkr.at[pl.ds(0, own)],
            r.s_dk.at[2 * layer],
            r.s_dk.at[2 * layer + 1],
            there(partner),
        )

    def attend_backward(layer, advances={}, more={}):
        own = own_rows[layer]
        kh, vh, qh, kt, dkv = layers[layer].kh, layers[layer].vh, layers[layer].qh, layers[layer].kt, r.kv
        doh, dd, qq, part16 = r.vt, r.dd, r.qq, r.half
        blocks, queries = 2 * own // 256, own // 256
        for head in (0, 1):
            r.tall[pl.ds(128 * head, 128), 0:own] = jnp.zeros((128, own), F32)

        def block(index):
            key = lax.rem((1 - member) * queries + index, blocks)
            found = []
            for head in (0, 1):
                keys = kh[head, at16(256 * key, 256), :]
                values = vh[head, at16(256 * key, 256), :]
                for query in range(queries):
                    rows = pl.ds(256 * query, 256)
                    weights = jnp.exp2(dot(keys, qh[head, rows, :], NT))
                    grad = weights * dot(values, doh[head, rows, :], NT)
                    high, low = split(weights)
                    part16[query] = high
                    part16[4 + query] = low
                    high, low = split(grad)
                    part16[8 + query] = high
                    part16[12 + query] = low

                def gathered(number):
                    return jnp.concatenate([part16[number + query] for query in range(queries)], 1)

                dscores, dscores_rest = gathered(8), gathered(12)
                both = dot(jnp.concatenate([gathered(0), gathered(4)], 0), dd[head, 0:own, :])
                dvalue = both[:256] + both[256:]
                both = dot(jnp.concatenate([dscores, dscores_rest], 0), qq[head, 0:own, :])
                dkey = both[:256] + both[256:]
                found.append((dkey, dvalue))
                r.tall[pl.ds(128 * head, 128), 0:own] += dot(kt[head, key], dscores) + dot(kt[head, key], dscores_rest)
            for column, part in ((0, 0), (128, 1)):
                zeroth = found[0][part] + pltpu.roll(found[0][part], 64, 1)
                other = found[1][part] + pltpu.roll(found[1][part], 64, 1)
                joined = jnp.where(low_half, zeroth, other)
                if part == 0:
                    joined = joined * LN2
                dkv[at16(256 * key, 256), column : column + 128] = joined

        loop_with(queries, block, advances)
        copy = dk_copy(layer)
        copy.start()
        loop_with(queries, lambda index: block(index + queries), more)
        copy.wait()

    def qkv_backward(layer, advances={}):
        own = own_rows[layer]
        x, c2, dkv, dkr = layers[layer].x, layers[layer].c2, r.kv, r.dkr
        grads, narrow = r.grads, r.narrow_acc
        gain, bias = layer_rows(layer, 0)
        mean2, scale2, gain2, bias2 = norm_rows(layer, 1)
        number = 4 + 2 * layer
        clear_sums(number)

        def block(index):
            start = 256 * index
            lanes = pl.ds(start, 256)
            dquery = [r.tall[pl.ds(128 * head, 64), lanes] + r.tall[pl.ds(128 * head + 64, 64), lanes] for head in (0, 1)]
            dquery = jnp.transpose(jnp.concatenate(dquery, 0)) * 0.125
            dkeys = dkv[at16(member * own + start, 256), :] + dkr[at16(start, 256), :]
            packed = jnp.concatenate([dquery, dkeys], 1)
            normed, scale = normed_layer(x[at16(start, 256), :])
            entered = normed * gain + bias
            weight = dot_pair(split(jnp.transpose(entered)), split(packed))
            grads[pl.ds(QUERY_KEY_AT[layer], 256), :] += weight[:, :256]
            grads[pl.ds(VALUE_AT[layer], 128), 0:128] += weight[:128, 256:]
            grads[pl.ds(VALUE_AT[layer], 128), 128:256] += weight[128:, 256:]
            dentered = dot_weight(packed, r.w_qkv_weight[layer], NT)
            narrow[4] += fold8(dentered * normed)
            narrow[5] += fold8(dentered)
            dx = r.dy[at16(start, 256), :] + normed_back(dentered * gain, normed, scale)
            r.dx[at16(start + 16, 256), :] = dx
            unit = (c2[at16(start + 16, 256), :] - mean2) * scale2
            dvalue = dx * mish_slope(unit * gain2 + bias2)
            add_sums(number, dvalue, dvalue * unit)

        loop_with(own // 256, block, advances, True)
        for row in (4, 5):
            grads[pl.ds(SMALL_AT[layer] + row, 1), :] = jnp.sum(narrow[row], axis=0, keepdims=True)
        copy = send_sums(number)
        norm_grads(layer, 1)
        source = pl.multiple_of((1 - member) * (8 + own) + member * 16, 8)
        target = pl.multiple_of((1 - member) * 8 + member * (16 + own), 8)
        edge = remote(
            r.dx.at[pl.ds(source, 8)],
            r.dx.at[pl.ds(target, 8)],
            r.s_dx.at[2 * layer],
            r.s_dx.at[2 * layer + 1],
            there(partner),
        )
        edge.start()
        return copy, edge

    def norm_grads(layer, which):
        base, mine = SMALL_AT[layer], r.sums[4 + 2 * layer + (1 - which)]
        r.grads[pl.ds(base + 2 + which, 1), :] = jnp.sum(mine[0:8], axis=0, keepdims=True)
        r.grads[pl.ds(base + which, 1), :] = jnp.sum(mine[8:16], axis=0, keepdims=True)

    def norm_back(layer, which, copy):
        number = 4 + 2 * layer + (1 - which)
        copy.wait()
        mean, scale, gain, bias = norm_rows(layer, which)
        mine = r.sums[number]
        from_bias, from_gain = group_total((mine + r.sums_in[number]) * gain)
        return mean, scale, gain, bias, from_bias / counts[layer], from_gain / counts[layer]

    def weight_rows(at, taken, grad):
        left = [split(jnp.transpose(value)) for value in taken]
        high = jnp.concatenate([pair[0] for pair in left], 0)
        low = jnp.concatenate([pair[1] for pair in left], 0)
        r.grads[pl.ds(at, 256 * len(taken)), :] += dot_pair((high, low), split(grad))

    def conv_weight(source, target, own, at):
        def block(index):
            value = source[at8(256 * index + 8, 272), :]
            grad = target[at16(256 * index + 16, 256), :]
            weight_rows(at, [value[7 + tap : 263 + tap] for tap in range(3)], grad)

        loop(own // 256, block, True)

    def res_backward(layer, copies, advances=((),) * 5):
        own = own_rows[layer]
        extended = own + 16
        rows, small = pick(extended, 256), pick(extended, 256)
        a, c1, h, c2 = layers[layer].a, layers[layer].c1, layers[layer].h, layers[layer].c2
        dx, dv = r.dx, r.kv
        copy, edge = copies

        def res_part(index):
            value = a[at16(256 * index + 16, 256), :]
            weight_rows(RES_AT[layer], [value], dx[at16(256 * index + 16, 256), :])

        loop(own // 256, res_part, True)
        edge.wait()
        zero(dv, 0, 16)
        zero(dv, own + 16, 16)
        mean, scale, gain, bias, from_bias, from_gain = norm_back(layer, 1, copy)
        advance(*advances[0])

        def second(index):
            start = small * index + 8
            unit = (c2[at8(start, small), :] - mean) * scale
            grad = dx[at8(start, small), :] * mish_slope(unit * gain + bias)
            out = scale * (gain * grad - (from_bias + unit * from_gain))
            c2[at8(start, small), :] = jnp.where(valid_rows(start, small, layer)[0], out, 0.0)

        loop(extended // small, second)
        mean1, scale1, gain1, bias1 = norm_rows(layer, 0)
        number = 5 + 2 * layer
        clear_sums(number)
        r.narrow_acc[6] = jnp.zeros((8, 256), F32)

        def hidden(index):
            start = rows * index + 8
            taps = [r.w_conv_two[layer, 2 - tap] for tap in range(3)]
            out = conv_block(c2, rows * index, rows, taps, NT)
            valid, mine = valid_rows(start, rows, layer)
            out = jnp.where(valid, out, 0.0)
            unit = (c1[at8(start, rows), :] - mean1) * scale1
            grad = out * mish_slope(unit * gain1 + bias1)
            dv[at8(start, rows), :] = grad
            r.narrow_acc[6] += fold8(jnp.where(mine, out, 0.0))
            grad = jnp.where(mine, grad, 0.0)
            add_sums(number, grad, grad * unit)

        loop(extended // rows, hidden, True)
        copy = send_sums(number)
        norm_grads(layer, 0)
        summed = jnp.sum(r.narrow_acc[6], axis=0, keepdims=True)
        r.grads[pl.ds(SMALL_AT[layer] + 8, 16), :] = jnp.where(row16 == utterance, summed, 0.0)
        advance(*advances[1])
        conv_weight(h, c2, own, CONV_TWO_AT[layer])
        advance(*advances[2])
        mean, scale, gain, bias, from_bias, from_gain = norm_back(layer, 0, copy)

        def first_part(index):
            start = small * index + 8
            unit = (c1[at8(start, small), :] - mean) * scale
            out = scale * (gain * dv[at8(start, small), :] - (from_bias + unit * from_gain))
            dv[at8(start, small), :] = jnp.where(valid_rows(start, small, layer)[0], out, 0.0)

        loop(extended // small, first_part)
        taps = [r.w_conv_one[layer, 2 - tap] for tap in range(3)]
        advance(*advances[3])
        conv_weight(a, dv, own, CONV_ONE_AT[layer])
        advance(*advances[4])

        def inputs(start, size):
            out = conv_block(dv, start, size, taps, NT)
            out = out + dot_weight(dx[at8(start + 8, size), :], r.w_res_weight[layer], NT)
            return jnp.where(valid_rows(start + 8, size, layer)[0], out, 0.0)

        if layer == 1:

            def block(index):
                r.da[at8(rows * index + 8, rows), :] = inputs(rows * index, rows)

            loop(extended // rows, block, True)
        else:

            def block(index):
                r.dy[at16(256 * index, 256), :] = inputs(256 * index + 8, 256)

            loop(own // 256, block, True)
            send_blocks(grad_sends[:GRAD_FIRST])

    def shrink_backward_part():
        da, own = r.da, own_rows[1]
        acc = r.narrow_acc
        acc[7] = jnp.zeros((8, 256), F32)

        def weights(index):
            grad = da[at16(256 * index + 16, 256), :]
            weight_rows(SHRINK_AT, [taken_rows(256 * index, 256, tap) for tap in range(3)], grad)

        loop(own // 256, weights, True)

        def block(index):
            value = da[at16(128 * index + 16, 144), :]
            both = jnp.concatenate(split(value), 0)
            parts = [dot(both, r.w_shrink_weight[tap], NT) for tap in range(3)]
            parts = [part[:144] + part[144:] for part in parts]
            even = parts[1][:128]
            odd = parts[2][:128] + parts[0][1:129]
            at = lax.broadcasted_iota(jnp.int32, (128, 256), 0) + 128 * index
            frame = 2 * (at + member * own)
            even = jnp.where(frame < length, even, 0.0)
            odd = jnp.where(frame + 1 < length, odd, 0.0)
            for lanes in (0, 1):
                columns = slice(128 * lanes, 128 * lanes + 128)
                r.first[lanes, pl.ds(32 + 256 * index, 128, stride=2), :] = even[:, columns]
                r.first[lanes, pl.ds(33 + 256 * index, 128, stride=2), :] = odd[:, columns]
            acc[7] += fold8(value[:128])

        loop(own // 128, block, True)

        r.grads[pl.ds(SMALL_AT[1] + 6, 1), :] = jnp.sum(acc[7], axis=0, keepdims=True)

    def block_sends(source, size, target, sems, pieces=1):
        found = []
        rows = size // pieces
        for piece in range(pieces):
            for item in range(half):
                found.append(
                    spread(
                        source.at[pl.ds(size * item + rows * piece, rows)],
                        target.at[place, pl.ds(rows * piece, rows)],
                        sems,
                        pieces * item + piece,
                        half * member + item,
                        pieces * place + piece,
                    )
                )
        return found

    def send_blocks(sends):
        for start, _ in sends:
            start()

    def finish_blocks(sends, size, target, sems, pieces=1):
        for _, wait_sent in sends:
            wait_sent()
        rows = size // pieces
        for item in range(depth):
            for piece in range(pieces):
                part = target.at[item, pl.ds(rows * piece, rows)]
                wait_arrived(part, sems, pieces * item + piece)

    def bucket(number):
        grads, sems, size = r.grads, r.s_total, BUCKET_ROWS[number]
        arrived = arrivals[number]
        at_once = number in AT_ONCE
        first = size // 512 * 256
        x, y = lax.rem(dp, 2), lax.div(dp, 2)
        over_x, over_y = (x, {"dp": dp + 1 - 2 * x, "seq": seq}), (y, {"dp": dp + 2 - 4 * y, "seq": seq})
        over_core = (member, there(partner))
        low, high = lax.rem(place, 2), lax.div(place, 2)
        over_z = [] if at_once else [(low, there(seq + 2 - 4 * low)), (high, there(seq + 4 - 8 * high))]
        lanes = []
        for at, count, order in (
            (BUCKET_AT[number], size - first, (over_x, over_y)),
            (BUCKET_AT[number] + size - first, first, (over_y, over_x)),
        ):
            lane = []
            for mine, device in [over_core, *order, *over_z]:
                count = count // 2
                lane.append((at + (1 - mine) * count, at + mine * count, count, device))
                at = at + mine * count
            lanes.append((lane, at, count))
        stages = len(lanes[0][0])

        def rows_at(ref, start, count):
            return ref.at[at8(start, count)]

        def wait_bytes(count, number_of):
            some = rows_at(grads, BUCKET_AT[number], count)
            pltpu.make_async_copy(some, some, sems.at[number, number_of]).wait()

        def total_of(stage):
            return sum(lane[stage][2] for lane, _, _ in lanes)

        def arriving(stage):
            if stage == 0:
                return r.core, CORE_AT[number]
            if stage < 3:
                return (arrived.near, arrived.next)[stage - 1], 0
            return arrived.far, (stage - 3) * (size // 16)

        def pair_out(stage):
            into, at = arriving(stage)
            for lane, _, _ in lanes:
                given, _, count, device = lane[stage]
                remote(
                    rows_at(grads, given, count),
                    into.at[pl.ds(at, count)],
                    sems.at[number, 2 * stage],
                    sems.at[number, 2 * stage + 1],
                    device,
                ).start()
                at += count

        def pair_in(stage):
            wait_bytes(total_of(stage), 2 * stage)
            wait_bytes(total_of(stage), 2 * stage + 1)
            into, at = arriving(stage)
            for lane, _, _ in lanes:
                _, start, count, _ = lane[stage]
                add_all(start, count, [into.at[pl.ds(at, count)]])
                at += count

        def far_peers():
            for step in range(1, depth):
                yield step, lax.rem(place + step, depth)

        far_rows = size // 32

        def far_out():
            at = 0
            for _, start, count in lanes:
                piece = count // depth
                for step, other in far_peers():
                    remote(
                        rows_at(grads, start + other * piece, piece),
                        arrived.far.at[pl.ds(at + far_rows * (step - 1), piece)],
                        sems.at[number, 6],
                        sems.at[number, 7],
                        there(2 * other + member),
                    ).start()
                at += piece

        def far_in():
            wait_bytes(far_rows * (depth - 1), 6)
            wait_bytes(far_rows * (depth - 1), 7)
            at = 0
            for _, start, count in lanes:
                piece = count // depth
                parts = [arrived.far.at[pl.ds(at + far_rows * step, piece)] for step in range(depth - 1)]
                add_all(start + place * piece, piece, parts)
                at += piece

        def keep():
            for _, start, count in lanes:
                if at_once:
                    count = count // depth
                    start = start + place * count
                pltpu.make_async_copy(
                    rows_at(grads, start, count),
                    rows_at(grad_total, start, count),
                    sems.at[number, 20],
                ).start()

        def far_back():
            for _, start, count in lanes:
                piece = count // depth
                for _, other in far_peers():
                    remote(
                        rows_at(grads, start + place * piece, piece),
                        rows_at(grad_total, start + place * piece, piece),
                        sems.at[number, 8],
                        sems.at[number, 9],
                        there(2 * other + member),
                    ).start()

        def far_back_in():
            wait_bytes(far_rows * (depth - 1), 8)
            wait_bytes(far_rows * (depth - 1), 9)

        def pair_back(stage):
            source = grads if stage == stages - 1 and not at_once else grad_total
            for lane, _, _ in lanes:
                _, start, count, device = lane[stage]
                remote(
                    rows_at(source, start, count),
                    rows_at(grad_total, start, count),
                    sems.at[number, 18 - 2 * stage],
                    sems.at[number, 19 - 2 * stage],
                    device,
                ).start()

        def pair_back_in(stage):
            wait_bytes(total_of(stage), 18 - 2 * stage)
            wait_bytes(total_of(stage), 19 - 2 * stage)

        def add_all(start, count, parts):
            unit = pick8(count, 256)

            def piece(index):
                rows = at8(start + unit * index, unit)
                value = grads[rows, :]
                for part in parts:
                    value = value + part[at8(unit * index, unit), :]
                grads[rows, :] = value

            loop(count // unit, piece)

        turns = [(None, lambda: pair_out(0))]
        for stage in range(1, stages):
            turns.append((lambda stage=stage: pair_in(stage - 1), lambda stage=stage: pair_out(stage)))
        if at_once:
            turns.append((lambda: pair_in(stages - 1), far_out))
            turns.append((far_in, lambda: (far_back(), keep())))
            turns.append((lambda: (far_back_in(), wait_bytes(far_rows, 20)), lambda: pair_back(stages - 1)))
        else:
            turns.append((lambda: pair_in(stages - 1), lambda: (pair_back(stages - 1), keep())))
        for stage in range(stages - 1, 0, -1):

            def back_in(stage=stage):
                pair_back_in(stage)
                if stage == stages - 1 and not at_once:
                    wait_bytes(total_of(stage), 20)

            turns.append((back_in, lambda stage=stage: pair_back(stage - 1)))
        turns.append((lambda: pair_back_in(0), None))

        def step(which):
            for part in turns[which]:
                if part is not None:
                    part()

        return step

    def short_bucket(number):
        grads, sems, size = r.grads, r.s_total, BUCKET_ROWS[number]
        skipped = sum(BUCKET_ROWS[5:number])
        at, count1, count2, count3 = BUCKET_AT[number], size // 2, size // 8, size // 32
        at1 = at + member * count1
        at2 = at1 + dp * count2
        at3 = at2 + place * count3
        near = (arrivals[0].near, arrivals[0].near, arrivals[0].next)[number - 5]
        near_at, far_at = 3 * count2 * (number == 6), 3 * (skipped // 32)
        near_peers = [(step, lax.rem(dp + step, dp_count)) for step in range(1, dp_count)]
        far_peers = [(step, lax.rem(place + step, depth)) for step in range(1, depth)]

        def rows_at(ref, start, count):
            return ref.at[at8(start, count)]

        def send(source, target, stage, device):
            remote(
                source, target, sems.at[number, 2 * stage], sems.at[number, 2 * stage + 1], device
            ).start()

        def arrive(count, stage):
            some = rows_at(grads, at, count)
            for side in (0, 1):
                pltpu.make_async_copy(some, some, sems.at[number, 2 * stage + side]).wait()

        def add(start, count, ref, from_at, parts):
            rows = at8(start, count)
            value = grads[rows, :]
            for part in range(parts):
                value = value + ref[pl.ds(from_at + part * count, count), :]
            grads[rows, :] = value

        def chip(index):
            return {"dp": index, "seq": seq}

        def step(which):
            if which == 0:
                given = rows_at(grads, at + (1 - member) * count1, count1)
                send(given, r.core.at[pl.ds(CORE_AT[number], count1)], 0, there(partner))
            if which == 1:
                arrive(count1, 0)
                add(at1, count1, r.core, CORE_AT[number], 1)
                for turn, other in near_peers:
                    target = near.at[pl.ds(near_at + (turn - 1) * count2, count2)]
                    send(rows_at(grads, at1 + other * count2, count2), target, 1, chip(other))
            if which == 2:
                arrive(3 * count2, 1)
                add(at2, count2, near, near_at, 3)
                for turn, other in far_peers:
                    target = arrivals[0].far.at[pl.ds(far_at + (turn - 1) * count3, count3)]
                    device = there(2 * other + member)
                    send(rows_at(grads, at2 + other * count3, count3), target, 2, device)
            if which == 3:
                arrive(3 * count3, 2)
                add(at3, count3, arrivals[0].far, far_at, 3)
                mine, result = rows_at(grads, at3, count3), rows_at(grad_total, at3, count3)
                for _, other in far_peers:
                    send(mine, result, 3, there(2 * other + member))
                pltpu.make_async_copy(mine, result, sems.at[number, 20]).start()
            if which == 4:
                arrive(3 * count3, 3)
                mine = rows_at(grads, at3, count3)
                pltpu.make_async_copy(mine, mine, sems.at[number, 20]).wait()
                result = rows_at(grad_total, at2, count2)
                for _, other in near_peers:
                    send(result, result, 4, chip(other))
            if which == 5:
                arrive(3 * count2, 4)
                result = rows_at(grad_total, at1, count1)
                send(result, result, 5, there(partner))
            if which == 6:
                arrive(count1, 5)

        return step

    all_steps = [bucket(number) if number < 5 else short_bucket(number) for number in range(len(BUCKET_ROWS))]

    def advance(*pairs):
        for number, which in pairs:
            all_steps[number](which)

    def loop_with(count, body, advances, unrolled=False):
        if unrolled:
            for index in range(count):
                advance(*advances.get(index, ()))
                body(index)
            return

        def step(index):
            for at, pairs in advances.items():

                @pl.when(index == at)
                def _(pairs=pairs):
                    advance(*pairs)

            body(index)

        loop(count, step)

    last_sends = block_sends(r.last, 128, output, r.s_last)
    grad_sends = block_sends(r.dy, 256, input_grad, r.s_grad, 4)

    for item in range(depth):
        wait_arrived(a0.at[pl.ds(16 + 256 * item, 256)], r.s_frames, item)
    pltpu.make_async_copy(a0.at[pl.ds(8, 8)], a0.at[pl.ds(8, 8)], edge_sems.at[3, 0]).wait()

    def mask_frames(index):
        rows = at8(pick(own_rows[0] + 16, 256) * index + 8, pick(own_rows[0] + 16, 256))
        valid = valid_rows(pick(own_rows[0] + 16, 256) * index + 8, pick(own_rows[0] + 16, 256), 0)[0]
        a0[rows, :] = jnp.where(valid, a0[rows, :], 0.0)

    loop((own_rows[0] + 16) // pick(own_rows[0] + 16, 256), mask_frames)
    cot_sends = [
        spread(
            inputs.cotangent.at[item],
            r.cot.at[at16(128 * block_in_group, 128)],
            r.s_cot,
            item,
            2 * item + group_of_block,
            block_in_group,
        )
        for item in range(depth)
    ]
    for start, _ in cot_sends:
        start()
    res_forward(0)
    qkv_forward(0)
    keys_forward(0)
    later_forward(0)
    shrink_forward_part()
    res_forward(1)
    qkv_forward(1)
    keys_forward(1)
    later_forward(1)
    send_blocks(last_sends)
    for item in range(depth):
        wait_arrived(r.cot.at[pl.ds(128 * item, 128)], r.s_cot, item)

    def mask_cot(index):
        valid = valid_rows(128 * index + 16, 128, 1)[0]
        rows = at16(128 * index, 128)
        r.cot[rows, :] = jnp.where(valid, r.cot[rows, :], 0.0)

    loop(own_rows[1] // 128, mask_cot)
    later_backward(1)
    advance((0, 0))
    attend_backward(1, {}, {})
    advance((0, 1))
    copies = qkv_backward(1)
    res_backward(1, copies, [(), (), [(1, 0)], [(1, 1)], ()])
    shrink_backward_part()
    advance((0, 2), (2, 0))
    later_backward(0, {1: [(2, 1), (1, 2)], 2: [(0, 3)], 3: [(2, 2), (1, 3)]})
    advance((0, 4), (2, 3), (4, 0), (3, 0))
    attend_backward(0, {1: [(1, 4), (4, 1), (3, 1)], 3: [(4, 2)]}, {0: [(0, 5)], 1: [(2, 4), (4, 3), (3, 2)], 2: [(0, 6)], 3: [(1, 5), (3, 3)]})
    advance((2, 5))
    copies = qkv_backward(0)
    advance((0, 7), (4, 4))
    res_backward(0, copies, [[(1, 6), (3, 4)], [(5, 0), (0, 8), (2, 6)], [(6, 0), (5, 1), (4, 5)], [(6, 1), (1, 7)], [(7, 0), (1, 8), (3, 5)]])
    advance((7, 1), (2, 7), (5, 2), (2, 8), (4, 6), (6, 2), (3, 6))
    send_blocks(grad_sends[6:7])
    advance((5, 3), (7, 2), (6, 3), (5, 4))
    send_blocks(grad_sends[7:9])
    advance((4, 7), (7, 3), (3, 7), (6, 4))
    send_blocks(grad_sends[9:10])
    advance((4, 8), (3, 8))
    send_blocks(grad_sends[10:11])
    advance((5, 5))
    send_blocks(grad_sends[11:13])
    advance((7, 4), (5, 6))
    send_blocks(grad_sends[13:14])
    advance((6, 5))
    send_blocks(grad_sends[14:16])
    advance((6, 6), (7, 5), (7, 6))
    for _, wait_sent in frame_sends + cot_sends:
        wait_sent()
    for after, before, _, _, item in edge_sends:

        @pl.when(sends_after & (seq != 2 * item + 1))
        def _(after=after):
            after.wait_send()

        @pl.when(sends_before & (seq != 2 * item))
        def _(before=before):
            before.wait_send()

    finish_blocks(last_sends, 128, output, r.s_last)
    finish_blocks(grad_sends, 256, input_grad, r.s_grad, 4)


def pick8(total, most):
    best = 8
    for size in range(8, most + 1, 8):
        if total % size == 0:
            best = size
    return best


GRAD_SHAPES = (
    (2, 3, 256, 256),
    (2, 3, 256, 256),
    (2, 256, 256),
    (2, 2, 256),
    (2, 2, 256),
    (2, 1024, 256),
    (2, 256),
    (2, 2, 256),
    (2, 2, 256),
    (2, 256, 384),
    (2, 128, 256),
    (2, 256),
    (2, 256, 1024),
    (2, 1024),
    (2, 1024),
    (2, 1024),
    (2, 1024, 256),
    (2, 256),
    (3, 256, 256),
    (256,),
)

class Gradients(typing.NamedTuple):
    conv_one: Any
    conv_two: Any
    res_weight: Any
    norm_gain: Any
    norm_bias: Any
    time_weight: Any
    time_bias: Any
    layer_gain: Any
    layer_bias: Any
    qkv_weight: Any
    out_weight: Any
    out_bias: Any
    up_weight: Any
    up_bias: Any
    snake_alpha: Any
    snake_beta: Any
    down_weight: Any
    down_bias: Any
    shrink_weight: Any
    shrink_bias: Any


def unpack_kernel(shape, total, last, grad, *refs):
    outs = Gradients(*refs[2:22])
    held, held_last, held_grad, held_time, sems, out_sems = refs[22:]
    loads, stores = [], []

    def rows(start, count):
        return total.at[pl.ds(start, count)], held.at[pl.ds(start, count)]

    def load(start, count):
        source, target = rows(start, count)
        loads.append(pltpu.make_async_copy(source, target, sems.at[len(loads)]))
        loads[-1].start()

    def store(start, count, target, lanes=pl.ds(0, 256)):
        source = held.at[pl.ds(start, count), lanes]
        stores.append((pltpu.make_async_copy(source, target, out_sems.at[len(stores)]), len(loads)))

    def move(start, count, target):
        load(start, count)
        store(start, count, target)

    for source, through, target in ((last, held_last, refs[0]), (grad, held_grad, refs[1])):
        loads.append(pltpu.make_async_copy(source, through, sems.at[len(loads)]))
        loads[-1].start()
        stores.append((pltpu.make_async_copy(through, target, out_sems.at[len(stores)]), len(loads)))
    load(EMBED_AT, 64)
    for layer in (1, 0):
        load(SMALL_AT[layer], 24)
        load(LATER_AT[layer] + LATER_SMALL, 16)
    small_loads = len(loads)
    for layer in (1, 0):
        later = LATER_AT[layer]
        for column in range(4):
            lanes = pl.ds(256 * column, 256)
            move(later + UP + 256 * column, 256, outs.up_weight.at[layer, :, lanes])
        move(later + DOWN, 1024, outs.down_weight.at[layer])
        move(later + OUT, 128, outs.out_weight.at[layer])
        for tap in range(3):
            move(CONV_TWO_AT[layer] + 256 * tap, 256, outs.conv_two.at[layer, tap])
        move(RES_AT[layer], 256, outs.res_weight.at[layer])
        move(QUERY_KEY_AT[layer], 256, outs.qkv_weight.at[layer, :, pl.ds(0, 256)])
        for tap in range(3):
            move(CONV_ONE_AT[layer] + 256 * tap, 256, outs.conv_one.at[layer, tap])
        load(VALUE_AT[layer], 128)
        for part in (0, 1):
            target = outs.qkv_weight.at[layer, pl.ds(128 * part, 128), pl.ds(256, 128)]
            store(VALUE_AT[layer], 128, target, pl.ds(128 * part, 128))
    for tap in range(3):
        move(SHRINK_AT + 256 * tap, 256, outs.shrink_weight.at[tap])
    for number in range(small_loads):
        loads[number].wait()
    for layer in (0, 1):
        later = held[pl.ds(LATER_AT[layer] + LATER_SMALL, 16), :]
        res = held[pl.ds(SMALL_AT[layer], 24), :]
        outs.norm_gain[layer] = res[0:2]
        outs.norm_bias[layer] = res[2:4]
        outs.layer_gain[layer, 0:1, :] = res[4:5]
        outs.layer_gain[layer, 1:2, :] = later[2:3]
        outs.layer_bias[layer, 0:1, :] = res[5:6]
        outs.layer_bias[layer, 1:2, :] = later[3:4]
        outs.down_bias[layer : layer + 1, :] = later[0:1]
        outs.out_bias[layer : layer + 1, :] = later[1:2]
        for column in range(4):
            lanes = slice(256 * column, 256 * column + 256)
            outs.up_bias[layer : layer + 1, lanes] = later[4 + column : 5 + column]
            outs.snake_alpha[layer : layer + 1, lanes] = later[8 + column : 9 + column]
            outs.snake_beta[layer : layer + 1, lanes] = later[12 + column : 13 + column]
        summed = res[8:24]
        outs.time_bias[layer : layer + 1, :] = jnp.sum(summed, axis=0, keepdims=True)
        right = split(summed)
        blank = jnp.zeros((128 - 16, 256), F32)
        for column in range(4):
            tall = jnp.concatenate([held[pl.ds(EMBED_AT + 16 * column, 16), :], blank], 0)
            left = split(jnp.transpose(tall)[:, 0:16])
            held_time[layer, pl.ds(256 * column, 256), :] = dot_pair(left, right)
        time_copy = pltpu.make_async_copy(held_time.at[layer], outs.time_weight.at[layer], out_sems.at[46 + layer])
        stores.insert(0, (time_copy, 0))
    outs.shrink_bias[...] = held[pl.ds(SMALL_AT[1] + 6, 1), :]
    waited = small_loads
    for copy, needed in stores:
        for number in range(waited, needed):
            loads[number].wait()
        waited = max(waited, needed)
        copy.start()
    for copy, _ in stores:
        copy.wait()


def fused_local(shape, *args):
    groups = scratch_of(shape)
    given = Arguments(*args)
    specs = Arguments(*(WHOLE,) * 24)._replace(
        frames=ANY,
        lengths=pl.BlockSpec(memory_space=pltpu.SMEM),
        cotangent=ANY,
        conv_one=ANY,
        conv_two=ANY,
        res_weight=ANY,
        time_weight=ANY,
        qkv_weight=ANY,
        out_weight=ANY,
        up_weight=ANY,
        down_weight=ANY,
        shrink_weight=ANY,
    )
    output, input_grad, total = pl.pallas_call(
        lambda *refs: fused_kernel(shape, groups, *refs),
        out_shape=(
            jax.ShapeDtypeStruct(given.cotangent.shape, F32),
            jax.ShapeDtypeStruct(given.frames.shape, F32),
            jax.ShapeDtypeStruct((sum(BUCKET_ROWS), 256), F32),
        ),
        in_specs=list(specs),
        out_specs=(ANY,) * 3,
        scratch_shapes=[one for group in groups for one in group.values()],
        name="layers",
        compiler_params=pltpu.CompilerParams(
            collective_id=0, has_side_effects=True, vmem_limit_bytes=VMEM_BYTES
        ),
    )(*given)
    shapes = [s if len(s) > 1 else (1,) + s for s in GRAD_SHAPES]
    shapes = [output.shape, input_grad.shape] + shapes
    grads = pl.pallas_call(
        lambda *refs: unpack_kernel(shape, *refs),
        out_shape=tuple(jax.ShapeDtypeStruct(s, F32) for s in shapes),
        in_specs=[ANY] * 3,
        out_specs=(ANY, ANY)
        + tuple(
            Gradients(*(WHOLE,) * 20)._replace(
                time_weight=ANY,
                conv_one=ANY,
                conv_two=ANY,
                res_weight=ANY,
                qkv_weight=ANY,
                out_weight=ANY,
                up_weight=ANY,
                down_weight=ANY,
                shrink_weight=ANY,
            )
        ),
        scratch_shapes=[
            pltpu.VMEM((sum(BUCKET_ROWS), 256), F32),
            pltpu.VMEM(output.shape, F32),
            pltpu.VMEM(input_grad.shape, F32),
            pltpu.VMEM((2, 1024, 256), F32),
            pltpu.SemaphoreType.DMA((48,)),
            pltpu.SemaphoreType.DMA((48,)),
        ],
        name="unpack",
        compiler_params=pltpu.CompilerParams(vmem_limit_bytes=VMEM_BYTES),
    )(total, output, input_grad)
    grads = grads[:-1] + (grads[-1].reshape(256),)
    return tuple(grads)


VMEM_BYTES = 64 * 2**20 - 2**18


ARG_SPECS = (P("dp", "seq", None), P("dp", None), P("dp"), P("dp", "seq", None)) + (P(),) * 20
OUT_SPECS = (P("dp", "seq", None), P("dp", "seq", None)) + (P(),) * 20


def solution(mesh):
    shape = dict(mesh.shape)

    def local(*args):
        utterances, frames_in = args[0].shape[:2]
        if fits(shape, utterances, frames_in):
            return fused_local(shape, *args)
        return general_local(*args)

    return jax.shard_map(
        local, mesh=mesh, in_specs=ARG_SPECS, out_specs=OUT_SPECS, check_vma=False
    )
```

```python
import math
import typing
from types import SimpleNamespace
from typing import Any

import jax
import jax.numpy as jnp
from jax import lax
from jax.experimental import pallas as pl
from jax.experimental.pallas import tpu as pltpu
from jax.sharding import PartitionSpec as P

HEADS = 2
GROUPS = 8


precise = lax.Precision.HIGHEST
epsilon = 1e-05


def with_halo(value, sides, width):
    for axis, dim in sides:
        count, length = (lax.axis_size(axis), value.shape[dim])
        up = [(i, (i + 1) % count) for i in range(count - 1)]
        down = [(j, i) for i, j in up]
        last = lax.slice_in_dim(value, length - width, length, axis=dim)
        first = lax.slice_in_dim(value, 0, width, axis=dim)
        before = lax.ppermute(last, axis, up)
        after = lax.ppermute(first, axis, down)
        value = jnp.concatenate([before, value, after], axis=dim)
    return value


def shifted(value, axis, by):
    count = lax.axis_size(axis)
    pairs = [(i, i + by) for i in range(count) if 0 <= i + by < count]
    return lax.ppermute(value, axis, pairs)


def mish_curve(value_in):
    return value_in * jnp.tanh(jax.nn.softplus(value_in))


def conv_piece(padded, weight):
    frames_out = padded.shape[1] - 2
    summed = jnp.einsum("ufc,cd->ufd", padded[:, :frames_out], weight[0], precision=precise)
    summed = summed + jnp.einsum(
        "ufc,cd->ufd", padded[:, 1 : frames_out + 1], weight[1], precision=precise
    )
    return summed + jnp.einsum("ufc,cd->ufd", padded[:, 2:], weight[2], precision=precise)


def shrink_piece(padded, weight, bias_vec):
    span_len = padded.shape[1] - 1
    summed = jnp.einsum("ufc,cd->ufd", padded[:, 0:span_len:2], weight[0], precision=precise)
    summed = summed + jnp.einsum(
        "ufc,cd->ufd", padded[:, 1:span_len:2], weight[1], precision=precise
    )
    summed = summed + jnp.einsum(
        "ufc,cd->ufd", padded[:, 2 : span_len + 1 : 2], weight[2], precision=precise
    )
    return summed + bias_vec


def group_sums(conv_out, mask_row):
    utterances, frames_in, channels = conv_out.shape
    masked = conv_out * mask_row[:, :, None]
    shape_new = (utterances, frames_in, GROUPS, channels // GROUPS)
    first_sum = jnp.sum(masked.reshape(shape_new), axis=(1, 3))
    second_sum = jnp.sum((masked * conv_out).reshape(shape_new), axis=(1, 3))
    return (first_sum, second_sum)


def group_apply(conv_out, first_sum, second_sum, counts, gain_vec, bias_vec, mask_row):
    group_width = conv_out.shape[2] // GROUPS
    mean_val = first_sum / counts[:, None]
    var_val = second_sum / counts[:, None] - mean_val * mean_val
    scale_val = lax.rsqrt(var_val + epsilon)
    mean_full = jnp.repeat(mean_val, group_width, axis=1)[:, None, :]
    scale_full = jnp.repeat(scale_val, group_width, axis=1)[:, None, :]
    normed = (conv_out - mean_full) * scale_full * gain_vec + bias_vec
    return mish_curve(normed) * mask_row[:, :, None]


def time_piece(embedding, weight, bias_vec):
    return jnp.dot(mish_curve(embedding), weight, precision=precise) + bias_vec


def layer_norm(value_in, gain_vec, bias_vec):
    mean_val = jnp.mean(value_in, axis=-1, keepdims=True)
    centered = value_in - mean_val
    var_val = jnp.mean(centered * centered, axis=-1, keepdims=True)
    return centered * lax.rsqrt(var_val + epsilon) * gain_vec + bias_vec


def attend_in(value_in, gain_vec, bias_vec, qkv_weight):
    normed = layer_norm(value_in, gain_vec, bias_vec)
    packed = jnp.einsum("ufc,ce->ufe", normed, qkv_weight, precision=precise)
    inner_dim = packed.shape[2] // 3
    return (
        packed[:, :, :inner_dim],
        packed[:, :, inner_dim : 2 * inner_dim],
        packed[:, :, 2 * inner_dim :],
    )


def attend_out(value_in, queries, key_full, value_full, key_mask, later_weights):
    (
        out_weight,
        out_bias,
        gain_vec,
        bias_vec,
        up_weight,
        up_bias,
        snake_alpha,
        snake_beta,
        down_weight,
        down_bias,
    ) = later_weights
    utterances, frames_in, inner_dim = queries.shape
    head_dim = inner_dim // HEADS
    key_count = key_full.shape[1]
    query_heads = queries.reshape(utterances, frames_in, HEADS, head_dim)
    key_heads = key_full.reshape(utterances, key_count, HEADS, head_dim)
    value_heads = value_full.reshape(utterances, key_count, HEADS, head_dim)
    scores = jnp.einsum("uqhd,ukhd->uhqk", query_heads, key_heads, precision=precise) / math.sqrt(
        head_dim
    )
    scores = jnp.where(key_mask[:, None, None, :] > 0.5, scores, -1e30)
    scores = scores - jnp.max(scores, axis=3, keepdims=True)
    raised = jnp.exp(scores)
    weights_soft = raised / jnp.sum(raised, axis=3, keepdims=True)
    attended = jnp.einsum("uhqk,ukhd->uqhd", weights_soft, value_heads, precision=precise)
    attended = attended.reshape(utterances, frames_in, inner_dim)
    current = (
        value_in + jnp.einsum("ufe,ec->ufc", attended, out_weight, precision=precise) + out_bias
    )
    normed = layer_norm(current, gain_vec, bias_vec)
    raised_up = jnp.einsum("ufc,ce->ufe", normed, up_weight, precision=precise) + up_bias
    snake_out = raised_up + jnp.sin(raised_up * jnp.exp(snake_alpha)) ** 2 / (
        jnp.exp(snake_beta) + 1e-09
    )
    return (
        current + jnp.einsum("ufe,ec->ufc", snake_out, down_weight, precision=precise) + down_bias
    )


def layer_weights(stacked, layer_index):
    (
        conv_one,
        conv_two,
        res_weight,
        norm_gain,
        norm_bias,
        time_weight,
        time_bias,
        layer_gain,
        layer_bias,
        qkv_weight,
        out_weight,
        out_bias,
        up_weight,
        up_bias,
        snake_alpha,
        snake_beta,
        down_weight,
        down_bias,
    ) = stacked
    resnet_part = (
        conv_one[layer_index],
        conv_two[layer_index],
        res_weight[layer_index],
        norm_gain[layer_index],
        norm_bias[layer_index],
        time_weight[layer_index],
        time_bias[layer_index],
    )
    first_part = (layer_gain[layer_index, 0], layer_bias[layer_index, 0], qkv_weight[layer_index])
    later_part = (
        out_weight[layer_index],
        out_bias[layer_index],
        layer_gain[layer_index, 1],
        layer_bias[layer_index, 1],
        up_weight[layer_index],
        up_bias[layer_index],
        snake_alpha[layer_index],
        snake_beta[layer_index],
        down_weight[layer_index],
        down_bias[layer_index],
    )
    return (resnet_part, first_part, later_part)


def layer_grads(resnet_grads, first_grads, later_grads):
    gains = jnp.stack([first_grads[0], later_grads[2]])
    biases = jnp.stack([first_grads[1], later_grads[3]])
    return (
        resnet_grads
        + (gains, biases, first_grads[2], later_grads[0], later_grads[1])
        + later_grads[4:]
    )


def flatten_all(arrays):
    return jnp.concatenate([array_in.reshape(-1) for array_in in arrays])


def unflatten_all(flat, shapes):
    pieces = []
    offset_at = 0
    for shape_in in shapes:
        size_in = math.prod(shape_in)
        pieces.append(flat[offset_at : offset_at + size_in].reshape(shape_in))
        offset_at = offset_at + size_in
    return pieces


def frame_halo(value_in):
    return with_halo(value_in, (("seq", 1),), 1)


def rim_return(grad_padded):
    rim_rows = jnp.concatenate([grad_padded[:, :1], grad_padded[:, -1:]], axis=1)
    arrived = with_halo(rim_rows, (("seq", 1),), 1)
    inner_rows = grad_padded[:, 1:-1]
    inner_rows = inner_rows.at[:, 0].add(arrived[:, 0])
    return inner_rows.at[:, -1].add(arrived[:, 3])


def group_total(conv_out, mask_row):
    first_sum, second_sum = group_sums(conv_out, mask_row)
    return lax.psum((first_sum, second_sum), "seq")


def group_return(conv_out, mask_row, grad_first, grad_second):
    grad_first, grad_second = lax.psum((grad_first, grad_second), "seq")

    def sums_local(conv_in):
        return group_sums(conv_in, mask_row)

    pull_back = jax.vjp(sums_local, conv_out)[1]
    return pull_back((grad_first, grad_second))[0]


def resnet_forward(inputs, mask_row, counts, embedding, weights):
    conv_first, conv_second, res_weight, norm_gain, norm_bias, time_weight, time_bias = weights
    column = mask_row[:, :, None]
    masked = inputs * column
    padded_one = frame_halo(masked)
    first_conv = conv_piece(padded_one, conv_first)
    sums_one = group_total(first_conv, mask_row)
    hidden = group_apply(
        first_conv, sums_one[0], sums_one[1], counts, norm_gain[0], norm_bias[0], mask_row
    )
    hidden = hidden + time_piece(embedding, time_weight, time_bias)[:, None, :]
    padded_two = frame_halo(hidden * column)
    second = conv_piece(padded_two, conv_second)
    sums_two = group_total(second, mask_row)
    result = group_apply(
        second, sums_two[0], sums_two[1], counts, norm_gain[1], norm_bias[1], mask_row
    )
    result = result + jnp.einsum("ufc,cd->ufd", masked, res_weight, precision=precise)
    return (result, (masked, padded_one, first_conv, sums_one, padded_two, second, sums_two))


def resnet_backward(grad_out, saved, mask_row, counts, embedding, weights):
    conv_first, conv_second, res_weight, norm_gain, norm_bias, time_weight, time_bias = weights
    masked, padded_one, first_conv, sums_one, padded_two, second, sums_two = saved
    column = mask_row[:, :, None]

    def norm_local(conv_out, first_sum, second_sum, gain_vec, bias_vec):
        return group_apply(conv_out, first_sum, second_sum, counts, gain_vec, bias_vec, mask_row)

    pull_two = jax.vjp(norm_local, second, sums_two[0], sums_two[1], norm_gain[1], norm_bias[1])[1]
    grad_second, grad_first_sum, grad_second_sum, gain_grad_two, bias_grad_two = pull_two(grad_out)
    grad_second = grad_second + group_return(second, mask_row, grad_first_sum, grad_second_sum)
    grad_res = jnp.einsum("ufc,ufd->cd", masked, grad_out, precision=precise)
    grad_masked = jnp.einsum("ufd,cd->ufc", grad_out, res_weight, precision=precise)
    pull_conv = jax.vjp(conv_piece, padded_two, conv_second)[1]
    grad_padded, grad_conv_second = pull_conv(grad_second)
    grad_hidden = rim_return(grad_padded) * column

    def time_local(weight, bias_vec):
        return time_piece(embedding, weight, bias_vec)

    pull_time = jax.vjp(time_local, time_weight, time_bias)[1]
    grad_time_weight, grad_time_bias = pull_time(jnp.sum(grad_hidden, axis=1))
    pull_one = jax.vjp(
        norm_local, first_conv, sums_one[0], sums_one[1], norm_gain[0], norm_bias[0]
    )[1]
    grad_first, grad_first_sum, grad_second_sum, gain_grad_one, bias_grad_one = pull_one(
        grad_hidden
    )
    grad_first = grad_first + group_return(first_conv, mask_row, grad_first_sum, grad_second_sum)
    pull_conv = jax.vjp(conv_piece, padded_one, conv_first)[1]
    grad_padded, grad_conv_first = pull_conv(grad_first)
    grad_inputs = (rim_return(grad_padded) + grad_masked) * column
    grads = (
        grad_conv_first,
        grad_conv_second,
        grad_res,
        jnp.stack([gain_grad_one, gain_grad_two]),
        jnp.stack([bias_grad_one, bias_grad_two]),
        grad_time_weight,
        grad_time_bias,
    )
    return (grad_inputs, grads)


def block_forward(value_in, key_mask, first_weights, later_weights):
    queries, key_here, value_here = attend_in(
        value_in, first_weights[0], first_weights[1], first_weights[2]
    )
    key_full, value_full = (
        lax.all_gather(key_here, "seq", axis=1, tiled=True),
        lax.all_gather(value_here, "seq", axis=1, tiled=True),
    )
    result = attend_out(value_in, queries, key_full, value_full, key_mask, later_weights)
    kept_pair = (key_full, value_full)
    return (result, (value_in, queries, kept_pair))


def block_backward(grad_out, saved, key_mask, first_weights, later_weights):
    value_in, queries, kept_pair = saved
    key_full, value_full = kept_pair

    def attend_local(current, query_in, key_in, value_full_in, weights_in):
        return attend_out(current, query_in, key_in, value_full_in, key_mask, weights_in)

    pull_out = jax.vjp(attend_local, value_in, queries, key_full, value_full, later_weights)[1]
    grad_value, grad_queries, grad_keys, grad_values, grad_later = pull_out(grad_out)
    grad_keys, grad_values = (
        lax.psum_scatter(grad_keys, "seq", scatter_dimension=1, tiled=True),
        lax.psum_scatter(grad_values, "seq", scatter_dimension=1, tiled=True),
    )
    pull_in = jax.vjp(attend_in, value_in, first_weights[0], first_weights[1], first_weights[2])[1]
    grad_input, grad_gain, grad_bias, grad_qkv = pull_in((grad_queries, grad_keys, grad_values))
    return (grad_value + grad_input, (grad_gain, grad_bias, grad_qkv), grad_later)


def shrink_forward(value_in, mask_row, weight, bias_vec):
    masked = value_in * mask_row[:, :, None]
    carried = shifted(masked[:, -1:], "seq", 1)
    padded = jnp.concatenate([carried, masked], axis=1)
    return (shrink_piece(padded, weight, bias_vec), padded)


def shrink_backward(grad_out, padded, mask_row, weight, bias_vec):
    pull_back = jax.vjp(shrink_piece, padded, weight, bias_vec)[1]
    grad_padded, grad_weight, grad_bias = pull_back(grad_out)
    returned = shifted(grad_padded[:, :1], "seq", -1)
    grad_masked = grad_padded[:, 1:].at[:, -1:].add(returned)
    return (grad_masked * mask_row[:, :, None], grad_weight, grad_bias)


def general_local(
    frames,
    flow_embed,
    lengths,
    cotangent,
    conv_one,
    conv_two,
    res_weight,
    norm_gain,
    norm_bias,
    time_weight,
    time_bias,
    layer_gain,
    layer_bias,
    qkv_weight,
    out_weight,
    out_bias,
    up_weight,
    up_bias,
    snake_alpha,
    snake_beta,
    down_weight,
    down_bias,
    shrink_weight,
    shrink_bias,
):
    stacked = tuple(
        (
            weight_in.astype(jnp.float32)
            for weight_in in (
                conv_one,
                conv_two,
                res_weight,
                norm_gain,
                norm_bias,
                time_weight,
                time_bias,
                layer_gain,
                layer_bias,
                qkv_weight,
                out_weight,
                out_bias,
                up_weight,
                up_bias,
                snake_alpha,
                snake_beta,
                down_weight,
                down_bias,
            )
        )
    )
    shrink_w = shrink_weight.astype(jnp.float32)
    shrink_b = shrink_bias.astype(jnp.float32)
    seq_count = lax.axis_size("seq")
    seq_index = lax.axis_index("seq")
    frames_one = frames.shape[1]
    frames_two = frames_one // 2
    group_width = frames.shape[2] // GROUPS
    place_one = seq_index * frames_one + jnp.arange(frames_one, dtype=jnp.int32)
    place_two = seq_index * frames_two + jnp.arange(frames_two, dtype=jnp.int32)
    mask_one = (place_one[None, :] < lengths[:, None]).astype(jnp.float32)
    mask_two = (2 * place_two[None, :] < lengths[:, None]).astype(jnp.float32)
    keys_one = (
        jnp.arange(frames_one * seq_count, dtype=jnp.int32)[None, :] < lengths[:, None]
    ).astype(jnp.float32)
    keys_two = (
        2 * jnp.arange(frames_two * seq_count, dtype=jnp.int32)[None, :] < lengths[:, None]
    ).astype(jnp.float32)
    counts_one = (lengths * group_width).astype(jnp.float32)
    counts_two = ((lengths + 1) // 2 * group_width).astype(jnp.float32)
    res_zero, first_zero, later_zero = layer_weights(stacked, 0)
    res_one, first_one, later_one = layer_weights(stacked, 1)
    current, saved_first = resnet_forward(frames, mask_one, counts_one, flow_embed, res_zero)
    current, saved_second = block_forward(current, keys_one, first_zero, later_zero)
    current, saved_shrink = shrink_forward(current, mask_one, shrink_w, shrink_b)
    current, saved_third = resnet_forward(current, mask_two, counts_two, flow_embed, res_one)
    current, saved_fourth = block_forward(current, keys_two, first_one, later_one)
    output = current * mask_two[:, :, None]
    grad_now = cotangent * mask_two[:, :, None]
    grad_now, first_grads, later_grads = block_backward(
        grad_now, saved_fourth, keys_two, first_one, later_one
    )
    grad_now, resnet_grads = resnet_backward(
        grad_now, saved_third, mask_two, counts_two, flow_embed, res_one
    )
    grads_top = layer_grads(resnet_grads, first_grads, later_grads)
    shapes = [array_in.shape for array_in in grads_top]
    top_size = sum((math.prod(shape_in) for shape_in in shapes))
    grad_now, grad_shrink_w, grad_shrink_b = shrink_backward(
        grad_now, saved_shrink, mask_one, shrink_w, shrink_b
    )
    grad_now, first_grads, later_grads = block_backward(
        grad_now, saved_second, keys_one, first_zero, later_zero
    )
    grad_now, resnet_grads = resnet_backward(
        grad_now, saved_first, mask_one, counts_one, flow_embed, res_zero
    )
    grads_low = layer_grads(resnet_grads, first_grads, later_grads)
    low_flat = jnp.concatenate([flatten_all(grads_low), grad_shrink_w.reshape(-1), grad_shrink_b])
    summed_all = lax.psum(jnp.concatenate([flatten_all(grads_top), low_flat]), ("dp", "seq"))
    summed_top = summed_all[:top_size]
    summed_low = summed_all[top_size:]
    parts_top = unflatten_all(summed_top, shapes)
    parts_low = unflatten_all(summed_low, shapes + [shrink_w.shape, shrink_b.shape])
    grads_out = tuple(
        (jnp.stack([parts_low[number], parts_top[number]]) for number in range(len(shapes)))
    )
    return (output, grad_now) + grads_out + (parts_low[-2], parts_low[-1])


F32, BF = jnp.float32, jnp.bfloat16
MESH = pl.DeviceIdType.MESH
NN = (((1,), (0,)), ((), ()))
NT = (((1,), (1,)), ((), ()))
LOG2E = math.log2(math.e)
LN2 = math.log(2.0)
ANY = pl.BlockSpec(memory_space=pl.ANY)
WHOLE = pl.BlockSpec(memory_space=pltpu.VMEM)

SIN_SQUARE = (
    9.869604311707743,
    -32.4696711717196,
    42.72719633650352,
    -30.101465841168043,
    13.050098919638232,
    -3.356592620742283,
)
SIN_TWICE = (
    6.283184916495428,
    -41.3415892326883,
    81.59994332977455,
    -76.61447253116356,
    41.34288235420472,
    -12.4712435344911,
)

UP, DOWN, OUT, LATER_SMALL = 0, 1024, 2048, 2176
BUCKET_ROWS = (2304, 1280, 1792, 1280, 1024, 768, 768, 768)
BUCKET_AT = (0, 2304, 3584, 5376, 6656, 8448, 7680, 9216)
GRAD_FIRST = 6
CORE_AT, CORE_ROWS = (0, 1152, 1792, 0, 640, 1152, 1536, 1920), 2688
AT_ONCE = (0, 1, 2, 3, 4)
LATER_AT = (5376, 0)
CONV_TWO_AT = (7680, 2304)
RES_AT = (8448, 3072)
QUERY_KEY_AT = (8704, 3328)
CONV_ONE_AT = (9216, 3584)
VALUE_AT = (8960, 4352)
SMALL_AT = (9088, 4480)
SHRINK_AT, EMBED_AT = 4504, 5272


def pick(total, most):
    best = 16
    for size in range(16, most + 1, 16):
        if total % size == 0:
            best = size
    return best


def fits(shape, utterances, frames_in):
    return shape["seq"] == 2 * utterances and frames_in == 256 and shape["dp"] * utterances == 16


def split(value):
    high = value.astype(BF)
    return high, (value - high.astype(F32)).astype(BF)


def dot(left, right, dims=NN):
    return lax.dot_general(left, right, dims, preferred_element_type=F32)


def dot_weight(value, weight, dims=NN):
    rows = value.shape[0]
    both = dot(jnp.concatenate(split(value), 0), weight, dims)
    return both[:rows] + both[rows:]


def dot_pair(left, right):
    rows = left[0].shape[0]
    both = dot(jnp.concatenate(left, 0), right[0])
    return both[:rows] + both[rows:] + dot(left[0], right[1])


def fold8(value):
    return jnp.sum(value.reshape(value.shape[0] // 8, 8, value.shape[1]), axis=0)


def polynomial(coefficients, at):
    total = jnp.full_like(at, coefficients[-1])
    for number in coefficients[-2::-1]:
        total = total * at + number
    return total


def mish_terms(value):
    raised = jnp.exp(jnp.minimum(value, 20.0))
    top = raised * (raised + 2.0)
    return raised, top, 1.0 / (top + 2.0)


def mish_of(value):
    raised, top, inverse = mish_terms(value)
    return value * (top * inverse)


def mish_slope(value):
    raised, top, inverse = mish_terms(value)
    return inverse * (top + 4.0 * value * (raised * (raised + 1.0)) * inverse)


def loop(count, body, unrolled=False):
    if unrolled:
        for index in range(count):
            body(index)
        return

    def step(index, carry):
        body(index)
        return carry

    lax.fori_loop(0, count, step, 0)


def at8(start, size):
    return pl.ds(start if isinstance(start, int) else pl.multiple_of(start, 8), size)


def at16(start, size):
    return pl.ds(start if isinstance(start, int) else pl.multiple_of(start, 16), size)


class Arguments(typing.NamedTuple):
    frames: Any
    flow_embed: Any
    lengths: Any
    cotangent: Any
    conv_one: Any
    conv_two: Any
    res_weight: Any
    norm_gain: Any
    norm_bias: Any
    time_weight: Any
    time_bias: Any
    layer_gain: Any
    layer_bias: Any
    qkv_weight: Any
    out_weight: Any
    out_bias: Any
    up_weight: Any
    up_bias: Any
    snake_alpha: Any
    snake_beta: Any
    down_weight: Any
    down_bias: Any
    shrink_weight: Any
    shrink_bias: Any


def matrices(found):
    return (
        found.conv_one,
        found.conv_two,
        found.res_weight,
        found.qkv_weight,
        found.out_weight,
        found.up_weight,
        found.down_weight,
        found.shrink_weight,
    )


def scratch_of(shape):
    depth = shape["seq"] // 2
    own_rows = (256 * depth, 128 * depth)

    def array(*size):
        return pltpu.VMEM(size, F32)

    def short(*size):
        return pltpu.VMEM(size, BF)

    def semaphores(*size):
        return pltpu.SemaphoreType.DMA(size)

    shared = dict(
        w_conv_one=short(2, 3, 256, 256),
        w_conv_two=short(2, 3, 256, 256),
        w_res_weight=short(2, 256, 256),
        w_qkv_weight=short(2, 256, 384),
        w_out_weight=short(2, 128, 256),
        w_up_weight=short(2, 256, 1024),
        w_down_weight=short(2, 1024, 256),
        w_shrink_weight=short(3, 256, 256),
        first=array(2, own_rows[0] + 64, 128),
        cot=array(own_rows[1], 256),
        last=array(own_rows[1], 256),
        dy=array(own_rows[0], 256),
        kv=array(2 * own_rows[0], 256),
        dkr=array(own_rows[0], 256),
        dx=array(own_rows[0] + 32, 256),
        da=array(own_rows[1] + 32, 256),
        vt=short(2, own_rows[0], 256),
        dd=short(2, own_rows[0], 128),
        qq=short(2, own_rows[0], 128),
        tall=array(256, 4 * 256),
        wide=array(2 * depth, 256, 256),
        half=short(4 * depth, 256, 256),
        te=array(2, 8, 256),
        sums=array(8, 16, 256),
        sums_in=array(8, 16, 256),
        stat=array(4, 8, 256),
        narrow_acc=array(8, 8, 256),
        wide_acc=array(3, 8, 1024),
        gather=short(256, 256),
        grads=array(sum(BUCKET_ROWS), 256),
        core=array(CORE_ROWS, 256),
        s_weight=semaphores(16),
        s_frames=semaphores(4, depth),
        s_cot=semaphores(2, depth),
        s_last=semaphores(2, depth),
        s_grad=semaphores(2, 4 * depth),
        s_sums=semaphores(2, 8),
        s_kv=semaphores(4, depth),
        s_first=semaphores(2),
        s_dk=semaphores(4),
        s_dx=semaphores(4),
        s_total=semaphores(len(BUCKET_ROWS), 21),
    )
    layers = [
        dict(
            a=array(own + 32, 256),
            c1=array(own + 32, 256),
            h=array(own + 32, 256),
            c2=array(own + 32, 256),
            x=array(own, 256),
            att=array(own, 128),
            qh=short(2, own, 256),
            kh=short(2, 2 * own, 256),
            vh=short(2, 2 * own, 256),
            kt=short(2, own // 128, 128, 256),
        )
        for own in own_rows
    ]
    arrivals = [
        dict(
            near=array(size // 4, 256),
            next=array(size // 8, 256),
            far=array((depth - 1) * size // 32, 256),
        )
        for size in BUCKET_ROWS[:5]
    ]
    return [shared] + layers + arrivals


def named(groups, refs):
    found, at = [], 0
    for group in groups:
        found.append(SimpleNamespace(**dict(zip(group, refs[at : at + len(group)]))))
        at += len(group)
    return found


def fused_kernel(shape, groups, *refs):
    inputs = Arguments(*refs[:24])
    output, input_grad, grad_total = refs[24:27]
    r, *rest = named(groups, refs[27:])
    layers, arrivals = rest[:2], rest[2:]
    dp_count, seq_count = shape["dp"], shape["seq"]
    depth = seq_count // 2
    dp, seq = lax.axis_index("dp"), lax.axis_index("seq")
    member, place = lax.rem(seq, 2), lax.div(seq, 2)
    partner = seq + 1 - 2 * member
    half = depth
    own_rows = (256 * depth, 128 * depth)
    utterance = dp * depth + place
    length = inputs.lengths[place]
    lane128 = lax.broadcasted_iota(jnp.int32, (1, 128), 1)
    low_half = lane128 < 64

    def there(index):
        return {"dp": dp, "seq": index}

    def remote(source, target, sent, arrived, device):
        return pltpu.make_async_remote_copy(
            source, target, sent, arrived, device_id=device, device_id_type=MESH
        )

    held = (
        r.w_conv_one,
        r.w_conv_two,
        r.w_res_weight,
        r.w_qkv_weight,
        r.w_out_weight,
        r.w_up_weight,
        r.w_down_weight,
        r.w_shrink_weight,
    )
    weight_copies = [
        pltpu.make_async_copy(matrix, target, r.s_weight.at[number])
        for number, (matrix, target) in enumerate(zip(matrices(inputs), held))
    ]
    time_copies = []
    for layer in (0, 1):
        for part in range(4):
            time_copies.append(
                pltpu.make_async_copy(
                    inputs.time_weight.at[layer, pl.ds(256 * part, 256)],
                    r.half.at[4 * layer + part],
                    r.s_weight.at[len(held) + 4 * layer + part],
                )
            )

    def zero(ref, start, size):
        ref[pl.ds(start, size), :] = jnp.zeros((size, ref.shape[1]), F32)

    for mine, own in zip(layers, own_rows):
        for ref in (mine.a, mine.h, mine.c2):
            zero(ref, 0, 16)
            zero(ref, own + 16, 16)
    for part in (0, 1):
        zero(r.first.at[part], 0, 32)
        zero(r.first.at[part], own_rows[0] + 32, 32)
    zero(r.da, 0, 16)
    zero(r.da, own_rows[1] + 16, 16)
    for start in (0, own_rows[1] + 16, own_rows[0] + 16):
        zero(r.dx, start, 16)

    barrier = pltpu.get_barrier_semaphore()
    for step in range(1, seq_count):
        pl.semaphore_signal(
            barrier,
            inc=1,
            device_id=there(lax.rem(seq + step, seq_count)),
            device_id_type=MESH,
        )
    for step in range(1, dp_count):
        pl.semaphore_signal(
            barrier,
            inc=1,
            device_id={"dp": lax.rem(dp + step, dp_count), "seq": seq},
            device_id_type=MESH,
        )
    pl.semaphore_wait(barrier, seq_count - 1 + dp_count - 1)

    def spread(source_of, target_of, sems, item, target_seq, arrived_at):
        away = remote(
            source_of, target_of, sems.at[0, item], sems.at[1, arrived_at], there(target_seq)
        )
        here = pltpu.make_async_copy(source_of, target_of, sems.at[1, arrived_at])

        def start():
            @pl.when(target_seq != seq)
            def _():
                away.start()

            @pl.when(target_seq == seq)
            def _():
                here.start()

        def wait_sent():
            @pl.when(target_seq != seq)
            def _():
                away.wait_send()

        return start, wait_sent

    def wait_arrived(target, sems, index):
        pltpu.make_async_copy(target, target, sems.at[1, index]).wait()

    group_of_block = lax.div(seq, half)
    block_in_group = lax.rem(seq, half)
    frame_sends = []
    a0 = layers[0].a
    for turned in (2, 1, 3, 0):
        item = lax.rem(place + turned, depth)
        target = 2 * item + group_of_block
        frame_sends.append(
            spread(
                inputs.frames.at[item],
                a0.at[at16(16 + 256 * block_in_group, 256)],
                r.s_frames,
                item,
                target,
                block_in_group,
            )
        )
    for start, _ in frame_sends:
        start()
    edge_sems = r.s_frames
    edge_sends = []
    for item in range(depth):
        after = remote(
            inputs.frames.at[item, pl.ds(248, 8)],
            a0.at[pl.ds(8, 8)],
            edge_sems.at[2, item],
            edge_sems.at[3, 0],
            there(2 * item + 1),
        )
        before = remote(
            inputs.frames.at[item, pl.ds(0, 8)],
            a0.at[pl.ds(16 + own_rows[0], 8)],
            edge_sems.at[2, item],
            edge_sems.at[3, 0],
            there(2 * item),
        )
        after_here = pltpu.make_async_copy(
            inputs.frames.at[item, pl.ds(248, 8)], a0.at[pl.ds(8, 8)], edge_sems.at[3, 0]
        )
        before_here = pltpu.make_async_copy(
            inputs.frames.at[item, pl.ds(0, 8)],
            a0.at[pl.ds(16 + own_rows[0], 8)],
            edge_sems.at[3, 0],
        )
        edge_sends.append((after, before, after_here, before_here, item))
    sends_after = seq == half - 1
    sends_before = seq == half
    for after, before, after_here, before_here, item in edge_sends:

        @pl.when(sends_after & (seq != 2 * item + 1))
        def _(after=after):
            after.start()

        @pl.when(sends_after & (seq == 2 * item + 1))
        def _(after_here=after_here):
            after_here.start()

        @pl.when(sends_before & (seq != 2 * item))
        def _(before=before):
            before.start()

        @pl.when(sends_before & (seq == 2 * item))
        def _(before_here=before_here):
            before_here.start()

    for copy in time_copies + weight_copies:
        copy.start()
    def zero_grads(index):
        r.grads[at8(64 * index, 64), :] = jnp.zeros((64, 256), F32)

    loop(sum(BUCKET_ROWS) // 64, zero_grads)
    same_group = (
        lax.broadcasted_iota(jnp.int32, (256, 256), 0) // 32
        == lax.broadcasted_iota(jnp.int32, (256, 256), 1) // 32
    )
    r.gather[...] = jnp.where(same_group, 1.0, 0.0).astype(BF)
    for copy in time_copies:
        copy.wait()
    embedded = mish_of(inputs.flow_embed[pl.ds(place, 1), :])
    wide_embed = jnp.broadcast_to(embedded, (16, 1024))
    time_bias = inputs.time_bias[...].astype(F32)
    for layer in (0, 1):
        weight = jnp.concatenate([r.half[4 * layer + part] for part in range(4)], 0)
        projected = dot_weight(wide_embed, weight)
        r.te[layer] = projected[:8] + time_bias[layer : layer + 1]
    row16 = lax.broadcasted_iota(jnp.int32, (16, 256), 0)
    for part in range(4):
        chosen = jnp.where(
            row16 == utterance + 64 * member, embedded[:, 256 * part : 256 * part + 256], 0.0
        )
        r.grads[pl.ds(EMBED_AT + 16 * part, 16), :] = chosen
    for copy in weight_copies:
        copy.wait()

    def valid_rows(start, rows, layer):
        at = lax.broadcasted_iota(jnp.int32, (rows, 256), 0) + (start - 16)
        frame = at + member * own_rows[layer]
        valid = (frame >= 0) & (frame * (1 + layer) < length)
        return valid, valid & (at >= 0) & (at < own_rows[layer])

    def conv_block(source, start, rows, taps, dims=NN):
        value = source[at8(start, rows + 16), :]
        both = jnp.concatenate(split(value), 0)
        total = None
        for tap, weight in enumerate(taps):
            part = dot(both, weight, dims)
            part = part[: rows + 16] + part[rows + 16 :]
            part = part[7 + tap : 7 + tap + rows]
            total = part if total is None else total + part
        return total

    def send_sums(number):
        copy = remote(
            r.sums.at[number],
            r.sums_in.at[number],
            r.s_sums.at[0, number],
            r.s_sums.at[1, number],
            there(partner),
        )
        copy.start()
        return copy

    def group_total(value):
        high = value.astype(BF)
        rest = value - high.astype(F32)
        middle = rest.astype(BF)
        last = (rest - middle.astype(F32)).astype(BF)
        parts = dot(jnp.concatenate([high, middle, last], 0), r.gather[...])
        total = parts[0:16] + parts[16:32] + parts[32:48]
        return (
            jnp.sum(total[0:8], axis=0, keepdims=True),
            jnp.sum(total[8:16], axis=0, keepdims=True),
        )

    counts = (
        (length * 32).astype(F32),
        (lax.div(length + 1, 2) * 32).astype(F32),
    )

    def forward_sums(layer, which, copy):
        number = 2 * layer + which
        copy.wait()
        first_sum, second_sum = group_total(r.sums[number] + r.sums_in[number])
        mean = first_sum / counts[layer]
        variance = second_sum / counts[layer] - mean * mean
        r.stat[number, 0:1, :] = mean
        r.stat[number, 1:2, :] = lax.rsqrt(variance + epsilon)

    def norm_rows(layer, which):
        number = 2 * layer + which
        gain = inputs.norm_gain[...].astype(F32)[layer, which : which + 1]
        bias = inputs.norm_bias[...].astype(F32)[layer, which : which + 1]
        return r.stat[number, 0:1, :], r.stat[number, 1:2, :], gain, bias

    def add_sums(number, first, second):
        r.sums[number, 0:8, :] += fold8(first)
        r.sums[number, 8:16, :] += fold8(second)

    def clear_sums(number):
        r.sums[number] = jnp.zeros((16, 256), F32)

    def normed_layer(value):
        mean = jnp.mean(value, axis=1, keepdims=True)
        centered = value - mean
        variance = jnp.mean(centered * centered, axis=1, keepdims=True)
        scale = lax.rsqrt(variance + epsilon)
        return centered * scale, scale

    def normed_back(grad, normed, scale):
        return scale * (
            grad
            - jnp.mean(grad, axis=1, keepdims=True)
            - normed * jnp.mean(grad * normed, axis=1, keepdims=True)
        )

    def layer_rows(layer, which):
        gain = inputs.layer_gain[...].astype(F32)[layer, which : which + 1]
        bias = inputs.layer_bias[...].astype(F32)[layer, which : which + 1]
        return gain, bias

    def row_of(ref, layer):
        return ref[...].astype(F32)[layer : layer + 1]

    def keys_aux(start, rows, layer):
        lane = lax.broadcasted_iota(jnp.int32, (rows, 128), 1)
        key = lax.broadcasted_iota(jnp.int32, (rows, 128), 0) + start
        masked = jnp.where(key * (1 + layer) < length, 0.0, -1e30)
        ones = jnp.where((lane >= 65) & (lane < 68), 1.0, 0.0)
        return jnp.where(lane == 64, masked, ones)

    def both_heads(value):
        high = value.astype(BF).astype(F32)
        low = value - high
        return high, low, pltpu.roll(high, 64, 1), pltpu.roll(low, 64, 1)

    def key_tiles(value, aux):
        high, low, high_turned, low_turned = both_heads(value)
        tiles = (
            (jnp.where(low_half, high, low_turned), jnp.where(low_half, high, aux)),
            (jnp.where(low_half, high_turned, low), jnp.where(low_half, high_turned, aux)),
        )
        return [(a.astype(BF), b.astype(BF)) for a, b in tiles]

    def query_tiles(value, aux):
        high, low, high_turned, low_turned = both_heads(value)
        tiles = (
            (jnp.where(low_half, high, high_turned), jnp.where(low_half, low, aux[0])),
            (jnp.where(low_half, high_turned, high), jnp.where(low_half, low_turned, aux[1])),
        )
        return [(a.astype(BF), b.astype(BF)) for a, b in tiles]

    def three_lanes(value, first):
        lane = lax.broadcasted_iota(jnp.int32, value.shape, 1)
        high = value.astype(BF).astype(F32)
        rest = value - high
        middle = rest.astype(BF).astype(F32)
        spread_out = jnp.where(lane == 66, middle, rest - middle)
        spread_out = jnp.where(lane == 65, high, spread_out)
        spread_out = jnp.where(lane == 64, first, spread_out)
        return jnp.where((lane >= 64) & (lane < 68), spread_out, 0.0)

    def turned_rows(value):
        row = lax.broadcasted_iota(jnp.int32, (8, 256), 0)
        high = value.astype(BF).astype(F32)
        rest = value - high
        middle = rest.astype(BF).astype(F32)
        rows = jnp.where(row == 0, 1.0, 0.0)
        rows = jnp.where(row == 1, high, rows)
        rows = jnp.where(row == 2, middle, rows)
        rows = jnp.where(row == 3, rest - middle, rows)
        return jnp.transpose(jnp.concatenate([jnp.zeros((64, 256), F32), rows, jnp.zeros((56, 256), F32)], 0))

    def res_forward(layer):
        own = own_rows[layer]
        extended = own + 16
        rows = pick(extended, 256)
        small = pick(extended, 256)
        a, c1, h, c2 = layers[layer].a, layers[layer].c1, layers[layer].h, layers[layer].c2

        def convolve(source, target, weights, number):
            clear_sums(number)

            def block(index):
                out = conv_block(source, rows * index, rows, [weights[layer, k] for k in range(3)])
                start = rows * index + 8
                target[at8(start, rows), :] = out
                kept = jnp.where(valid_rows(start, rows, layer)[1], out, 0.0)
                add_sums(number, kept, kept * out)

            loop(extended // rows, block, True)
            return send_sums(number)

        copy = convolve(a, c1, r.w_conv_one, 2 * layer)
        forward_sums(layer, 0, copy)
        mean, scale, gain, bias = norm_rows(layer, 0)
        added = r.te[layer, 0:1, :]

        def normed(index):
            start = small * index + 8
            value = (c1[at8(start, small), :] - mean) * scale * gain + bias
            valid = valid_rows(start, small, layer)[0]
            h[at8(start, small), :] = jnp.where(valid, mish_of(value) + added, 0.0)

        loop(extended // small, normed, True)
        copy = convolve(h, c2, r.w_conv_two, 2 * layer + 1)

        def residual(index):
            value = a[at16(256 * index + 16, 256), :]
            layers[layer].x[at16(256 * index, 256), :] = dot_weight(value, r.w_res_weight[layer])

        loop(own // 256, residual, True)
        forward_sums(layer, 1, copy)

    def keys_of(layer):
        return (r.kv, r.dy)[layer]

    def kv_copy(layer, index):
        own = own_rows[layer]
        part = keys_of(layer).at[at16(member * own + 256 * index, 256)]
        return remote(
            part,
            part,
            r.s_kv.at[2 * layer, index],
            r.s_kv.at[2 * layer + 1, index],
            there(partner),
        )

    def qkv_forward(layer):
        own = own_rows[layer]
        c2, x, kv, qh = layers[layer].c2, layers[layer].x, keys_of(layer), layers[layer].qh
        mean, scale, gain, bias = norm_rows(layer, 1)
        layer_gain, layer_bias = layer_rows(layer, 0)
        lane = lax.broadcasted_iota(jnp.int32, (256, 128), 1)
        aux = jnp.where(lane == 64, 1.0, 0.0)

        def block(index):
            start = 256 * index
            value = (c2[at16(start + 16, 256), :] - mean) * scale * gain + bias
            valid = valid_rows(start + 16, 256, layer)[0]
            out = jnp.where(valid, mish_of(value), 0.0) + x[at16(start, 256), :]
            x[at16(start, 256), :] = out
            packed = dot_weight(
                normed_layer(out)[0] * layer_gain + layer_bias, r.w_qkv_weight[layer]
            )
            kv[at16(member * own + start, 256), :] = packed[:, 128:]
            kv_copy(layer, index).start()
            tiles = query_tiles(packed[:, :128] * (LOG2E / 8.0), (aux, aux))
            for head in (0, 1):
                qh[head, at16(start, 256), 0:128] = tiles[head][0]
                qh[head, at16(start, 256), 128:256] = tiles[head][1]

        loop(own // 256, block, True)

    def keys_forward(layer):
        own = own_rows[layer]
        kv, kh, vh, kt, vt = keys_of(layer), layers[layer].kh, layers[layer].vh, layers[layer].kt, r.vt
        mine = own // 256

        def block(number):
            index = lax.rem(member * mine + number, 2 * mine)
            start = 256 * index
            value = kv[at16(start, 256), :]
            aux = keys_aux(start, 256, layer)
            for part, target in ((value[:, :128], kh), (value[:, 128:], vh)):
                tiles = key_tiles(part, aux)
                for head in (0, 1):
                    target[head, at16(start, 256), 0:128] = tiles[head][0]
                    target[head, at16(start, 256), 128:256] = tiles[head][1]
            for column in (0, 128):
                high, low = split(jnp.transpose(value[:, column : column + 128]))
                for head in (0, 1):
                    both = jnp.concatenate([high[64 * head : 64 * head + 64], low[64 * head : 64 * head + 64]], 0)
                    if column == 0:
                        kt[head, index] = both
                    else:
                        vt[head, at16(128 * index, 128), :] = both

        loop(mine, block)
        for index in range(mine):
            kv_copy(layer, index).wait()
        loop(mine, lambda number: block(mine + number))

    def snake_rows(layer):
        alpha = jnp.exp(row_of(inputs.snake_alpha, layer))
        beta = jnp.exp(row_of(inputs.snake_beta, layer))
        return alpha, beta, 1.0 / (beta + 1e-9)

    def later_forward(layer):
        own = own_rows[layer]
        x, att, kh, qh, vt = layers[layer].x, layers[layer].att, layers[layer].kh, layers[layer].qh, r.vt
        wide, part16 = r.wide, r.half
        blocks = 2 * own // 256
        gain, bias = layer_rows(layer, 1)
        out_bias, down_bias, up_bias = row_of(inputs.out_bias, layer), row_of(inputs.down_bias, layer), row_of(inputs.up_bias, layer)
        alpha, beta, inverse = snake_rows(layer)
        turns = alpha * (1.0 / math.pi)

        def block(index):
            start = 256 * index
            parts = [(head, part) for head in (0, 1) for part in (0, 1)]
            keys_in = blocks // 2
            queries = [qh[head, at16(start, 256), :] for head in (0, 1)]
            most, total, found = {}, {}, {}

            def scores(unit):
                head, part = parts[unit]
                highest = jnp.full((8, 256), -3e38, F32)
                for key in range(keys_in):
                    at = 256 * (keys_in * part + key)
                    out = dot(kh[head, at : at + 256, :], queries[head], NT)
                    wide[4 * (unit % 2) + key] = out
                    highest = jnp.maximum(highest, jnp.max(out.reshape(32, 8, 256), axis=0))
                most[unit] = jnp.max(highest, axis=0, keepdims=True)
                if part == 1:
                    most[unit] = jnp.maximum(most[unit], most[unit - 1])

            def exponentials(unit):
                summed = jnp.zeros((8, 256), F32)
                for key in range(keys_in):
                    for piece in range(4):
                        rows = pl.ds(64 * piece, 64)
                        raised = jnp.exp2(wide[4 * (unit % 2) + key, rows, :] - most[unit])
                        summed = summed + fold8(raised)
                        high, low = split(raised)
                        part16[8 * (unit % 2) + key, rows, :] = high
                        part16[8 * (unit % 2) + 4 + key, rows, :] = low
                total[unit] = jnp.sum(summed, axis=0, keepdims=True)

            def weighted(unit):
                head, part = parts[unit]
                first_key = keys_in * part
                values = jnp.concatenate(
                    [vt[head, 128 * key : 128 * key + 128, :] for key in range(first_key, first_key + keys_in)], 1
                )
                out = None
                for which in (0, 4):
                    at = 8 * (unit % 2) + which
                    taken = jnp.concatenate([part16[at + key] for key in range(keys_in)], 0)
                    taken = dot(values, taken)
                    out = taken if out is None else out + taken
                found[unit] = out[:64] + out[64:]

            scores(0)
            for unit in range(4):
                if unit < 3:
                    scores(unit + 1)
                if unit > 0:
                    weighted(unit - 1)
                exponentials(unit)
            weighted(3)
            attended = []
            for head in (0, 1):
                before, after = 2 * head, 2 * head + 1
                lowered = jnp.exp2(most[before] - most[after])
                summed = total[before] * lowered + total[after]
                attended.append((found[before] * lowered + found[after]) * (1.0 / summed))
                aux = turned_rows(-(most[after] + jnp.log2(summed)))
                old = qh[head, at16(start, 256), 128:256]
                qh[head, at16(start, 256), 128:256] = jnp.where(low_half, old, aux.astype(BF))
            joined = jnp.transpose(jnp.concatenate(attended, 0))
            att[at16(start, 256), :] = joined
            y = x[at16(start, 256), :] + dot_weight(joined, r.w_out_weight[layer]) + out_bias
            entered = jnp.concatenate(split(normed_layer(y)[0] * gain + bias), 0)

            def lift(column):
                both = dot(entered, r.w_up_weight[layer, :, 256 * column : 256 * column + 256])
                wide[column] = both[:256] + both[256:]

            lift(0)
            for column in range(4):
                lanes = slice(256 * column, 256 * column + 256)
                if column < 3:
                    lift(column + 1)
                for piece in range(4):
                    rows = pl.ds(64 * piece, 64)
                    z = wide[column, rows, :] + up_bias[:, lanes]
                    turn = z * turns[:, lanes]
                    turn = turn - jnp.round(turn)
                    square = turn * turn
                    s = z + square * polynomial(SIN_SQUARE, square) * inverse[:, lanes]
                    high, low = split(s)
                    part16[column, rows, :] = high
                    part16[4 + column, rows, :] = low
            both = jnp.concatenate(
                [jnp.concatenate([part16[4 * part + column] for column in range(4)], 1) for part in (0, 1)], 0
            )
            lowered = dot(both, r.w_down_weight[layer])
            out = y + lowered[:256] + lowered[256:] + down_bias
            out = jnp.where(valid_rows(start + 16, 256, layer)[0], out, 0.0)
            if layer == 0:
                for lanes in (0, 1):
                    r.first[lanes, at16(start + 32, 256), :] = out[:, 128 * lanes : 128 * lanes + 128]
            else:
                r.last[at16(start, 256), :] = out

        loop(own // 256, block)

    def shrink_forward_part():
        own = own_rows[0]
        first = r.first
        source = pl.multiple_of((1 - member) * (16 + own) + member * 32, 16)
        target = pl.multiple_of((1 - member) * 16 + member * (32 + own), 16)
        copy = remote(
            first.at[:, pl.ds(source, 16), :],
            first.at[:, pl.ds(target, 16), :],
            r.s_first.at[0],
            r.s_first.at[1],
            there(partner),
        )
        copy.start()
        copy.wait()
        extended = own_rows[1] + 16
        rows = pick(extended, 256)
        bias = inputs.shrink_bias[...].astype(F32).reshape(1, 256)

        def block(index):
            start = rows * index + 8
            total = bias
            for tap in range(3):
                taken = taken_rows(start - 16, rows, tap)
                total = total + dot_weight(taken, r.w_shrink_weight[tap])
            valid = valid_rows(start, rows, 1)[0]
            layers[1].a[at8(start, rows), :] = jnp.where(valid, total, 0.0)

        loop(extended // rows, block, True)

    def taken_rows(row, rows, tap):
        at = 32 + 2 * row - 1 + tap
        return jnp.concatenate([r.first[lanes, pl.ds(at, rows, stride=2), :] for lanes in (0, 1)], 1)

    def clear_layer():
        r.narrow_acc[...] = jnp.zeros((8, 8, 256), F32)
        r.wide_acc[...] = jnp.zeros((3, 8, 1024), F32)

    def later_backward(layer, advances={}):
        own = own_rows[layer]
        base = LATER_AT[layer]
        x, att, qh = layers[layer].x, layers[layer].att, layers[layer].qh
        wide, part16, grads = r.wide, r.half, r.grads
        doh = r.vt
        gain, bias = layer_rows(layer, 1)
        out_bias, up_bias = row_of(inputs.out_bias, layer), row_of(inputs.up_bias, layer)
        alpha, beta, inverse = snake_rows(layer)
        turns = alpha * (1.0 / math.pi)
        slope = alpha * inverse
        r.tall[...] = jnp.zeros((256, 1024), F32)
        clear_layer()
        narrow, broad = r.narrow_acc, r.wide_acc

        def block(index):
            start = 256 * index
            if layer == 0:
                dout = jnp.concatenate([r.first[lanes, at16(start + 32, 256), :] for lanes in (0, 1)], 1)
            else:
                dout = r.cot[at16(start, 256), :]
            joined = att[at16(start, 256), :]
            y = x[at16(start, 256), :] + dot_weight(joined, r.w_out_weight[layer]) + out_bias
            normed, scale = normed_layer(y)
            entered = normed * gain + bias
            entered_parts = jnp.concatenate(split(entered), 0)
            dout_parts = jnp.concatenate(split(dout), 0)
            dout_turned, entered_turned = split(jnp.transpose(dout)), split(jnp.transpose(entered))

            def lift(column):
                lanes = pl.ds(256 * column, 256)
                both = dot(entered_parts, r.w_up_weight[layer, :, lanes])
                wide[column] = both[:256] + both[256:]
                both = dot(dout_parts, r.w_down_weight[layer, lanes, :], NT)
                wide[4 + column] = both[:256] + both[256:]

            def weigh(column):
                lanes = pl.ds(256 * column, 256)
                r.tall[:, lanes] += dot_pair(dout_turned, (part16[column], part16[4 + column]))
                grads[pl.ds(base + UP + 256 * column, 256), :] += dot_pair(
                    entered_turned, (part16[8 + column], part16[12 + column])
                )

            lift(0)
            for column in range(4):
                lanes = slice(256 * column, 256 * column + 256)
                if column < 3:
                    lift(column + 1)
                if column > 0:
                    weigh(column - 1)
                dz_sum = turn_sum = sine_sum = jnp.zeros((8, 256), F32)
                for piece in range(8):
                    rows = pl.ds(32 * piece, 32)
                    z = wide[column, rows, :] + up_bias[:, lanes]
                    ds = wide[4 + column, rows, :]
                    whole = z * turns[:, lanes]
                    turn = whole - jnp.round(whole)
                    square = turn * turn
                    sine2 = square * polynomial(SIN_SQUARE, square)
                    twice = turn * polynomial(SIN_TWICE, square)
                    s = z + sine2 * inverse[:, lanes]
                    dtwice = ds * twice
                    dz = ds + dtwice * slope[:, lanes]
                    dz_sum += fold8(dz)
                    turn_sum += fold8(dtwice * whole)
                    sine_sum += fold8(ds * sine2)
                    high, low = split(s)
                    part16[column, rows, :] = high
                    part16[4 + column, rows, :] = low
                    high, low = split(dz)
                    part16[8 + column, rows, :] = high
                    part16[12 + column, rows, :] = low
                broad[0, :, lanes] += dz_sum
                broad[1, :, lanes] += turn_sum
                broad[2, :, lanes] += sine_sum

            weigh(3)

            def gathered(number):
                return jnp.concatenate([part16[number + column] for column in range(4)], 1)

            both = dot(jnp.concatenate([gathered(8), gathered(12)], 0), r.w_up_weight[layer], NT)
            dentered = both[:256] + both[256:]
            dy = dout + normed_back(dentered * gain, normed, scale)
            r.dy[at16(start, 256), :] = dy
            narrow[0] += fold8(dout)
            narrow[1] += fold8(dy)
            narrow[2] += fold8(dentered * normed)
            narrow[3] += fold8(dentered)
            grads[pl.ds(base + OUT, 128), :] += dot_pair(split(jnp.transpose(joined)), split(dy))
            datt = dot_weight(dy, r.w_out_weight[layer], NT)
            product = datt * joined
            sums = [
                jnp.sum(jnp.where(low_half, product, 0.0), axis=1, keepdims=True),
                jnp.sum(jnp.where(low_half, 0.0, product), axis=1, keepdims=True),
            ]
            aux = [three_lanes(jnp.broadcast_to(-total, (256, 128)), 0.0) for total in sums]
            tiles = query_tiles(datt, aux)
            pairs = key_tiles(datt, aux[0])
            for head in (0, 1):
                doh[head, at16(start, 256), 0:128] = tiles[head][0]
                doh[head, at16(start, 256), 128:256] = tiles[head][1]
                r.dd[head, at16(start, 256), :] = pairs[head][0]
                query = qh[head, at16(start, 256), 0:128].astype(F32)
                rest = pltpu.roll(qh[head, at16(start, 256), 128:256].astype(F32), 64, 1)
                r.qq[head, at16(start, 256), :] = jnp.where(low_half, query, rest).astype(BF)

        loop_with(own // 256, block, advances)

        def turn_down(index):
            taken = r.tall[:, pl.ds(256 * index, 256)]
            grads[at16(base + DOWN + 256 * index, 256), :] = jnp.transpose(taken)

        loop(4, turn_down, True)
        small = base + LATER_SMALL
        for number in range(4):
            grads[pl.ds(small + number, 1), :] = jnp.sum(narrow[number], axis=0, keepdims=True)
        bias_row = jnp.sum(broad[0], axis=0, keepdims=True)
        alpha_row = jnp.sum(broad[1], axis=0, keepdims=True) * (math.pi * inverse)
        beta_row = jnp.sum(broad[2], axis=0, keepdims=True) * (-beta * inverse * inverse)
        for number, row in enumerate((bias_row, alpha_row, beta_row)):
            for column in range(4):
                grads[pl.ds(small + 4 + 4 * number + column, 1), :] = row[:, 256 * column : 256 * column + 256]

    def dk_copy(layer):
        own = own_rows[layer]
        return remote(
            r.kv.at[at16((1 - member) * own, own)],
            r.dkr.at[pl.ds(0, own)],
            r.s_dk.at[2 * layer],
            r.s_dk.at[2 * layer + 1],
            there(partner),
        )

    def attend_backward(layer, advances={}, more={}):
        own = own_rows[layer]
        kh, vh, qh, kt, dkv = layers[layer].kh, layers[layer].vh, layers[layer].qh, layers[layer].kt, r.kv
        doh, dd, qq, part16 = r.vt, r.dd, r.qq, r.half
        blocks, queries = 2 * own // 256, own // 256
        for head in (0, 1):
            r.tall[pl.ds(128 * head, 128), 0:own] = jnp.zeros((128, own), F32)

        def block(index):
            key = lax.rem((1 - member) * queries + index, blocks)
            found = []
            for head in (0, 1):
                keys = kh[head, at16(256 * key, 256), :]
                values = vh[head, at16(256 * key, 256), :]
                for query in range(queries):
                    rows = pl.ds(256 * query, 256)
                    weights = jnp.exp2(dot(keys, qh[head, rows, :], NT))
                    grad = weights * dot(values, doh[head, rows, :], NT)
                    high, low = split(weights)
                    part16[query] = high
                    part16[4 + query] = low
                    high, low = split(grad)
                    part16[8 + query] = high
                    part16[12 + query] = low

                def gathered(number):
                    return jnp.concatenate([part16[number + query] for query in range(queries)], 1)

                dscores, dscores_rest = gathered(8), gathered(12)
                both = dot(jnp.concatenate([gathered(0), gathered(4)], 0), dd[head, 0:own, :])
                dvalue = both[:256] + both[256:]
                both = dot(jnp.concatenate([dscores, dscores_rest], 0), qq[head, 0:own, :])
                dkey = both[:256] + both[256:]
                found.append((dkey, dvalue))
                r.tall[pl.ds(128 * head, 128), 0:own] += dot(kt[head, key], dscores) + dot(kt[head, key], dscores_rest)
            for column, part in ((0, 0), (128, 1)):
                zeroth = found[0][part] + pltpu.roll(found[0][part], 64, 1)
                other = found[1][part] + pltpu.roll(found[1][part], 64, 1)
                joined = jnp.where(low_half, zeroth, other)
                if part == 0:
                    joined = joined * LN2
                dkv[at16(256 * key, 256), column : column + 128] = joined

        loop_with(queries, block, advances)
        copy = dk_copy(layer)
        copy.start()
        loop_with(queries, lambda index: block(index + queries), more)
        copy.wait()

    def qkv_backward(layer, advances={}):
        own = own_rows[layer]
        x, c2, dkv, dkr = layers[layer].x, layers[layer].c2, r.kv, r.dkr
        grads, narrow = r.grads, r.narrow_acc
        gain, bias = layer_rows(layer, 0)
        mean2, scale2, gain2, bias2 = norm_rows(layer, 1)
        number = 4 + 2 * layer
        clear_sums(number)

        def block(index):
            start = 256 * index
            lanes = pl.ds(start, 256)
            dquery = [r.tall[pl.ds(128 * head, 64), lanes] + r.tall[pl.ds(128 * head + 64, 64), lanes] for head in (0, 1)]
            dquery = jnp.transpose(jnp.concatenate(dquery, 0)) * 0.125
            dkeys = dkv[at16(member * own + start, 256), :] + dkr[at16(start, 256), :]
            packed = jnp.concatenate([dquery, dkeys], 1)
            normed, scale = normed_layer(x[at16(start, 256), :])
            entered = normed * gain + bias
            weight = dot_pair(split(jnp.transpose(entered)), split(packed))
            grads[pl.ds(QUERY_KEY_AT[layer], 256), :] += weight[:, :256]
            grads[pl.ds(VALUE_AT[layer], 128), 0:128] += weight[:128, 256:]
            grads[pl.ds(VALUE_AT[layer], 128), 128:256] += weight[128:, 256:]
            dentered = dot_weight(packed, r.w_qkv_weight[layer], NT)
            narrow[4] += fold8(dentered * normed)
            narrow[5] += fold8(dentered)
            dx = r.dy[at16(start, 256), :] + normed_back(dentered * gain, normed, scale)
            r.dx[at16(start + 16, 256), :] = dx
            unit = (c2[at16(start + 16, 256), :] - mean2) * scale2
            dvalue = dx * mish_slope(unit * gain2 + bias2)
            add_sums(number, dvalue, dvalue * unit)

        loop_with(own // 256, block, advances, True)
        for row in (4, 5):
            grads[pl.ds(SMALL_AT[layer] + row, 1), :] = jnp.sum(narrow[row], axis=0, keepdims=True)
        copy = send_sums(number)
        norm_grads(layer, 1)
        source = pl.multiple_of((1 - member) * (8 + own) + member * 16, 8)
        target = pl.multiple_of((1 - member) * 8 + member * (16 + own), 8)
        edge = remote(
            r.dx.at[pl.ds(source, 8)],
            r.dx.at[pl.ds(target, 8)],
            r.s_dx.at[2 * layer],
            r.s_dx.at[2 * layer + 1],
            there(partner),
        )
        edge.start()
        return copy, edge

    def norm_grads(layer, which):
        base, mine = SMALL_AT[layer], r.sums[4 + 2 * layer + (1 - which)]
        r.grads[pl.ds(base + 2 + which, 1), :] = jnp.sum(mine[0:8], axis=0, keepdims=True)
        r.grads[pl.ds(base + which, 1), :] = jnp.sum(mine[8:16], axis=0, keepdims=True)

    def norm_back(layer, which, copy):
        number = 4 + 2 * layer + (1 - which)
        copy.wait()
        mean, scale, gain, bias = norm_rows(layer, which)
        mine = r.sums[number]
        from_bias, from_gain = group_total((mine + r.sums_in[number]) * gain)
        return mean, scale, gain, bias, from_bias / counts[layer], from_gain / counts[layer]

    def weight_rows(at, taken, grad):
        left = [split(jnp.transpose(value)) for value in taken]
        high = jnp.concatenate([pair[0] for pair in left], 0)
        low = jnp.concatenate([pair[1] for pair in left], 0)
        r.grads[pl.ds(at, 256 * len(taken)), :] += dot_pair((high, low), split(grad))

    def conv_weight(source, target, own, at):
        def block(index):
            value = source[at8(256 * index + 8, 272), :]
            grad = target[at16(256 * index + 16, 256), :]
            weight_rows(at, [value[7 + tap : 263 + tap] for tap in range(3)], grad)

        loop(own // 256, block, True)

    def res_backward(layer, copies, advances=((),) * 5):
        own = own_rows[layer]
        extended = own + 16
        rows, small = pick(extended, 256), pick(extended, 256)
        a, c1, h, c2 = layers[layer].a, layers[layer].c1, layers[layer].h, layers[layer].c2
        dx, dv = r.dx, r.kv
        copy, edge = copies

        def res_part(index):
            value = a[at16(256 * index + 16, 256), :]
            weight_rows(RES_AT[layer], [value], dx[at16(256 * index + 16, 256), :])

        loop(own // 256, res_part, True)
        edge.wait()
        zero(dv, 0, 16)
        zero(dv, own + 16, 16)
        mean, scale, gain, bias, from_bias, from_gain = norm_back(layer, 1, copy)
        advance(*advances[0])

        def second(index):
            start = small * index + 8
            unit = (c2[at8(start, small), :] - mean) * scale
            grad = dx[at8(start, small), :] * mish_slope(unit * gain + bias)
            out = scale * (gain * grad - (from_bias + unit * from_gain))
            c2[at8(start, small), :] = jnp.where(valid_rows(start, small, layer)[0], out, 0.0)

        loop(extended // small, second)
        mean1, scale1, gain1, bias1 = norm_rows(layer, 0)
        number = 5 + 2 * layer
        clear_sums(number)
        r.narrow_acc[6] = jnp.zeros((8, 256), F32)

        def hidden(index):
            start = rows * index + 8
            taps = [r.w_conv_two[layer, 2 - tap] for tap in range(3)]
            out = conv_block(c2, rows * index, rows, taps, NT)
            valid, mine = valid_rows(start, rows, layer)
            out = jnp.where(valid, out, 0.0)
            unit = (c1[at8(start, rows), :] - mean1) * scale1
            grad = out * mish_slope(unit * gain1 + bias1)
            dv[at8(start, rows), :] = grad
            r.narrow_acc[6] += fold8(jnp.where(mine, out, 0.0))
            grad = jnp.where(mine, grad, 0.0)
            add_sums(number, grad, grad * unit)

        loop(extended // rows, hidden, True)
        copy = send_sums(number)
        norm_grads(layer, 0)
        summed = jnp.sum(r.narrow_acc[6], axis=0, keepdims=True)
        r.grads[pl.ds(SMALL_AT[layer] + 8, 16), :] = jnp.where(row16 == utterance, summed, 0.0)
        advance(*advances[1])
        conv_weight(h, c2, own, CONV_TWO_AT[layer])
        advance(*advances[2])
        mean, scale, gain, bias, from_bias, from_gain = norm_back(layer, 0, copy)

        def first_part(index):
            start = small * index + 8
            unit = (c1[at8(start, small), :] - mean) * scale
            out = scale * (gain * dv[at8(start, small), :] - (from_bias + unit * from_gain))
            dv[at8(start, small), :] = jnp.where(valid_rows(start, small, layer)[0], out, 0.0)

        loop(extended // small, first_part)
        taps = [r.w_conv_one[layer, 2 - tap] for tap in range(3)]
        advance(*advances[3])

        def inputs(start, size):
            out = conv_block(dv, start, size, taps, NT)
            out = out + dot_weight(dx[at8(start + 8, size), :], r.w_res_weight[layer], NT)
            return jnp.where(valid_rows(start + 8, size, layer)[0], out, 0.0)

        if layer == 1:

            def block(index):
                r.da[at8(rows * index + 8, rows), :] = inputs(rows * index, rows)

            loop(extended // rows, block, True)
            conv_weight(a, dv, own, CONV_ONE_AT[layer])
            advance(*advances[4])
        else:

            def block(index):
                r.dy[at16(256 * index, 256), :] = inputs(256 * index + 8, 256)

            loop(own // 256, block, True)
            send_blocks(grad_sends[:GRAD_FIRST])
            conv_weight(a, dv, own, CONV_ONE_AT[layer])
            advance(*advances[4])

    def shrink_backward_part():
        da, own = r.da, own_rows[1]
        acc = r.narrow_acc
        acc[7] = jnp.zeros((8, 256), F32)

        def weights(index):
            grad = da[at16(256 * index + 16, 256), :]
            weight_rows(SHRINK_AT, [taken_rows(256 * index, 256, tap) for tap in range(3)], grad)

        loop(own // 256, weights, True)

        def block(index):
            value = da[at16(128 * index + 16, 144), :]
            both = jnp.concatenate(split(value), 0)
            parts = [dot(both, r.w_shrink_weight[tap], NT) for tap in range(3)]
            parts = [part[:144] + part[144:] for part in parts]
            even = parts[1][:128]
            odd = parts[2][:128] + parts[0][1:129]
            at = lax.broadcasted_iota(jnp.int32, (128, 256), 0) + 128 * index
            frame = 2 * (at + member * own)
            even = jnp.where(frame < length, even, 0.0)
            odd = jnp.where(frame + 1 < length, odd, 0.0)
            for lanes in (0, 1):
                columns = slice(128 * lanes, 128 * lanes + 128)
                r.first[lanes, pl.ds(32 + 256 * index, 128, stride=2), :] = even[:, columns]
                r.first[lanes, pl.ds(33 + 256 * index, 128, stride=2), :] = odd[:, columns]
            acc[7] += fold8(value[:128])

        loop(own // 128, block, True)

        r.grads[pl.ds(SMALL_AT[1] + 6, 1), :] = jnp.sum(acc[7], axis=0, keepdims=True)

    def block_sends(source, size, target, sems, pieces=1):
        found = []
        rows = size // pieces
        for piece in range(pieces):
            for item in range(half):
                found.append(
                    spread(
                        source.at[pl.ds(size * item + rows * piece, rows)],
                        target.at[place, pl.ds(rows * piece, rows)],
                        sems,
                        pieces * item + piece,
                        half * member + item,
                        pieces * place + piece,
                    )
                )
        return found

    def send_blocks(sends):
        for start, _ in sends:
            start()

    def finish_blocks(sends, size, target, sems, pieces=1):
        for _, wait_sent in sends:
            wait_sent()
        rows = size // pieces
        for item in range(depth):
            for piece in range(pieces):
                part = target.at[item, pl.ds(rows * piece, rows)]
                wait_arrived(part, sems, pieces * item + piece)

    def bucket(number):
        grads, sems, size = r.grads, r.s_total, BUCKET_ROWS[number]
        arrived = arrivals[number]
        at_once = number in AT_ONCE
        first = size // 512 * 256
        x, y = lax.rem(dp, 2), lax.div(dp, 2)
        over_x, over_y = (x, {"dp": dp + 1 - 2 * x, "seq": seq}), (y, {"dp": dp + 2 - 4 * y, "seq": seq})
        over_core = (member, there(partner))
        low, high = lax.rem(place, 2), lax.div(place, 2)
        over_z = [] if at_once else [(low, there(seq + 2 - 4 * low)), (high, there(seq + 4 - 8 * high))]
        lanes = []
        for at, count, order in (
            (BUCKET_AT[number], size - first, (over_x, over_y)),
            (BUCKET_AT[number] + size - first, first, (over_y, over_x)),
        ):
            lane = []
            for mine, device in [over_core, *order, *over_z]:
                count = count // 2
                lane.append((at + (1 - mine) * count, at + mine * count, count, device))
                at = at + mine * count
            lanes.append((lane, at, count))
        stages = len(lanes[0][0])

        def rows_at(ref, start, count):
            return ref.at[at8(start, count)]

        def wait_bytes(count, number_of):
            some = rows_at(grads, BUCKET_AT[number], count)
            pltpu.make_async_copy(some, some, sems.at[number, number_of]).wait()

        def total_of(stage):
            return sum(lane[stage][2] for lane, _, _ in lanes)

        def arriving(stage):
            if stage == 0:
                return r.core, CORE_AT[number]
            if stage < 3:
                return (arrived.near, arrived.next)[stage - 1], 0
            return arrived.far, (stage - 3) * (size // 16)

        def pair_out(stage):
            into, at = arriving(stage)
            for lane, _, _ in lanes:
                given, _, count, device = lane[stage]
                remote(
                    rows_at(grads, given, count),
                    into.at[pl.ds(at, count)],
                    sems.at[number, 2 * stage],
                    sems.at[number, 2 * stage + 1],
                    device,
                ).start()
                at += count

        def pair_in(stage):
            wait_bytes(total_of(stage), 2 * stage)
            wait_bytes(total_of(stage), 2 * stage + 1)
            into, at = arriving(stage)
            for lane, _, _ in lanes:
                _, start, count, _ = lane[stage]
                add_all(start, count, [into.at[pl.ds(at, count)]])
                at += count

        def far_peers():
            for step in range(1, depth):
                yield step, lax.rem(place + step, depth)

        far_rows = size // 32

        def far_out():
            at = 0
            for _, start, count in lanes:
                piece = count // depth
                for step, other in far_peers():
                    remote(
                        rows_at(grads, start + other * piece, piece),
                        arrived.far.at[pl.ds(at + far_rows * (step - 1), piece)],
                        sems.at[number, 6],
                        sems.at[number, 7],
                        there(2 * other + member),
                    ).start()
                at += piece

        def far_in():
            wait_bytes(far_rows * (depth - 1), 6)
            wait_bytes(far_rows * (depth - 1), 7)
            at = 0
            for _, start, count in lanes:
                piece = count // depth
                parts = [arrived.far.at[pl.ds(at + far_rows * step, piece)] for step in range(depth - 1)]
                add_all(start + place * piece, piece, parts)
                at += piece

        def keep():
            for _, start, count in lanes:
                if at_once:
                    count = count // depth
                    start = start + place * count
                pltpu.make_async_copy(
                    rows_at(grads, start, count),
                    rows_at(grad_total, start, count),
                    sems.at[number, 20],
                ).start()

        def far_back():
            for _, start, count in lanes:
                piece = count // depth
                for _, other in far_peers():
                    remote(
                        rows_at(grads, start + place * piece, piece),
                        rows_at(grad_total, start + place * piece, piece),
                        sems.at[number, 8],
                        sems.at[number, 9],
                        there(2 * other + member),
                    ).start()

        def far_back_in():
            wait_bytes(far_rows * (depth - 1), 8)
            wait_bytes(far_rows * (depth - 1), 9)

        def pair_back(stage):
            source = grads if stage == stages - 1 and not at_once else grad_total
            for lane, _, _ in lanes:
                _, start, count, device = lane[stage]
                remote(
                    rows_at(source, start, count),
                    rows_at(grad_total, start, count),
                    sems.at[number, 18 - 2 * stage],
                    sems.at[number, 19 - 2 * stage],
                    device,
                ).start()

        def pair_back_in(stage):
            wait_bytes(total_of(stage), 18 - 2 * stage)
            wait_bytes(total_of(stage), 19 - 2 * stage)

        def add_all(start, count, parts):
            unit = pick8(count, 256)

            def piece(index):
                rows = at8(start + unit * index, unit)
                value = grads[rows, :]
                for part in parts:
                    value = value + part[at8(unit * index, unit), :]
                grads[rows, :] = value

            loop(count // unit, piece)

        turns = [(None, lambda: pair_out(0))]
        for stage in range(1, stages):
            turns.append((lambda stage=stage: pair_in(stage - 1), lambda stage=stage: pair_out(stage)))
        if at_once:
            turns.append((lambda: pair_in(stages - 1), far_out))
            turns.append((far_in, lambda: (far_back(), keep())))
            turns.append((lambda: (far_back_in(), wait_bytes(far_rows, 20)), lambda: pair_back(stages - 1)))
        else:
            turns.append((lambda: pair_in(stages - 1), lambda: (pair_back(stages - 1), keep())))
        for stage in range(stages - 1, 0, -1):

            def back_in(stage=stage):
                pair_back_in(stage)
                if stage == stages - 1 and not at_once:
                    wait_bytes(total_of(stage), 20)

            turns.append((back_in, lambda stage=stage: pair_back(stage - 1)))
        turns.append((lambda: pair_back_in(0), None))

        def step(which):
            for part in turns[which]:
                if part is not None:
                    part()

        return step

    def short_bucket(number):
        grads, sems, size = r.grads, r.s_total, BUCKET_ROWS[number]
        skipped = sum(BUCKET_ROWS[5:number])
        at, count1, count2, count3 = BUCKET_AT[number], size // 2, size // 8, size // 32
        at1 = at + member * count1
        at2 = at1 + dp * count2
        at3 = at2 + place * count3
        near = (arrivals[0].near, arrivals[0].near, arrivals[0].next)[number - 5]
        near_at, far_at = 3 * count2 * (number == 6), 3 * (skipped // 32)
        near_peers = [(step, lax.rem(dp + step, dp_count)) for step in range(1, dp_count)]
        far_peers = [(step, lax.rem(place + step, depth)) for step in range(1, depth)]

        def rows_at(ref, start, count):
            return ref.at[at8(start, count)]

        def send(source, target, stage, device):
            remote(
                source, target, sems.at[number, 2 * stage], sems.at[number, 2 * stage + 1], device
            ).start()

        def arrive(count, stage):
            some = rows_at(grads, at, count)
            for side in (0, 1):
                pltpu.make_async_copy(some, some, sems.at[number, 2 * stage + side]).wait()

        def add(start, count, ref, from_at, parts):
            rows = at8(start, count)
            value = grads[rows, :]
            for part in range(parts):
                value = value + ref[pl.ds(from_at + part * count, count), :]
            grads[rows, :] = value

        def chip(index):
            return {"dp": index, "seq": seq}

        def step(which):
            if which == 0:
                given = rows_at(grads, at + (1 - member) * count1, count1)
                send(given, r.core.at[pl.ds(CORE_AT[number], count1)], 0, there(partner))
            if which == 1:
                arrive(count1, 0)
                add(at1, count1, r.core, CORE_AT[number], 1)
                for turn, other in near_peers:
                    target = near.at[pl.ds(near_at + (turn - 1) * count2, count2)]
                    send(rows_at(grads, at1 + other * count2, count2), target, 1, chip(other))
            if which == 2:
                arrive(3 * count2, 1)
                add(at2, count2, near, near_at, 3)
                for turn, other in far_peers:
                    target = arrivals[0].far.at[pl.ds(far_at + (turn - 1) * count3, count3)]
                    device = there(2 * other + member)
                    send(rows_at(grads, at2 + other * count3, count3), target, 2, device)
            if which == 3:
                arrive(3 * count3, 2)
                add(at3, count3, arrivals[0].far, far_at, 3)
                mine, result = rows_at(grads, at3, count3), rows_at(grad_total, at3, count3)
                for _, other in far_peers:
                    send(mine, result, 3, there(2 * other + member))
                pltpu.make_async_copy(mine, result, sems.at[number, 20]).start()
            if which == 4:
                arrive(3 * count3, 3)
                mine = rows_at(grads, at3, count3)
                pltpu.make_async_copy(mine, mine, sems.at[number, 20]).wait()
                result = rows_at(grad_total, at2, count2)
                for _, other in near_peers:
                    send(result, result, 4, chip(other))
            if which == 5:
                arrive(3 * count2, 4)
                result = rows_at(grad_total, at1, count1)
                send(result, result, 5, there(partner))
            if which == 6:
                arrive(count1, 5)

        return step

    all_steps = [bucket(number) if number < 5 else short_bucket(number) for number in range(len(BUCKET_ROWS))]

    def advance(*pairs):
        for number, which in pairs:
            all_steps[number](which)

    def loop_with(count, body, advances, unrolled=False):
        if unrolled:
            for index in range(count):
                advance(*advances.get(index, ()))
                body(index)
            return

        def step(index):
            for at, pairs in advances.items():

                @pl.when(index == at)
                def _(pairs=pairs):
                    advance(*pairs)

            body(index)

        loop(count, step)

    last_sends = block_sends(r.last, 128, output, r.s_last)
    grad_sends = block_sends(r.dy, 256, input_grad, r.s_grad, 4)

    for item in range(depth):
        wait_arrived(a0.at[pl.ds(16 + 256 * item, 256)], r.s_frames, item)
    pltpu.make_async_copy(a0.at[pl.ds(8, 8)], a0.at[pl.ds(8, 8)], edge_sems.at[3, 0]).wait()

    def mask_frames(index):
        rows = at8(pick(own_rows[0] + 16, 256) * index + 8, pick(own_rows[0] + 16, 256))
        valid = valid_rows(pick(own_rows[0] + 16, 256) * index + 8, pick(own_rows[0] + 16, 256), 0)[0]
        a0[rows, :] = jnp.where(valid, a0[rows, :], 0.0)

    loop((own_rows[0] + 16) // pick(own_rows[0] + 16, 256), mask_frames)
    cot_sends = [
        spread(
            inputs.cotangent.at[item],
            r.cot.at[at16(128 * block_in_group, 128)],
            r.s_cot,
            item,
            2 * item + group_of_block,
            block_in_group,
        )
        for item in range(depth)
    ]
    for start, _ in cot_sends:
        start()
    res_forward(0)
    qkv_forward(0)
    keys_forward(0)
    later_forward(0)
    shrink_forward_part()
    res_forward(1)
    qkv_forward(1)
    keys_forward(1)
    later_forward(1)
    send_blocks(last_sends)
    for item in range(depth):
        wait_arrived(r.cot.at[pl.ds(128 * item, 128)], r.s_cot, item)

    def mask_cot(index):
        valid = valid_rows(128 * index + 16, 128, 1)[0]
        rows = at16(128 * index, 128)
        r.cot[rows, :] = jnp.where(valid, r.cot[rows, :], 0.0)

    loop(own_rows[1] // 128, mask_cot)
    later_backward(1)
    advance((0, 0))
    attend_backward(1, {}, {})
    advance((0, 1))
    copies = qkv_backward(1)
    res_backward(1, copies, [(), (), [(1, 0)], [(1, 1)], ()])
    shrink_backward_part()
    advance((0, 2), (2, 0))
    later_backward(0, {1: [(2, 1), (1, 2)], 2: [(0, 3)], 3: [(2, 2), (1, 3)]})
    advance((0, 4), (2, 3), (4, 0), (3, 0))
    attend_backward(0, {1: [(1, 4), (4, 1), (3, 1)], 3: [(4, 2)]}, {0: [(0, 5)], 1: [(2, 4), (4, 3), (3, 2)], 2: [(0, 6)], 3: [(1, 5), (3, 3)]})
    advance((2, 5))
    copies = qkv_backward(0)
    advance((0, 7), (4, 4))
    res_backward(0, copies, [[(1, 6), (3, 4)], [(5, 0), (0, 8), (2, 6)], [(6, 0), (5, 1), (4, 5)], [(6, 1), (1, 7)], [(7, 0), (1, 8), (3, 5)]])
    advance((7, 1), (2, 7), (5, 2), (2, 8), (4, 6), (6, 2), (3, 6))
    send_blocks(grad_sends[6:7])
    advance((5, 3), (7, 2), (6, 3), (5, 4))
    send_blocks(grad_sends[7:9])
    advance((4, 7), (7, 3), (3, 7), (6, 4))
    send_blocks(grad_sends[9:10])
    advance((4, 8), (3, 8))
    send_blocks(grad_sends[10:11])
    advance((5, 5))
    send_blocks(grad_sends[11:13])
    advance((7, 4), (5, 6))
    send_blocks(grad_sends[13:14])
    advance((6, 5))
    send_blocks(grad_sends[14:16])
    advance((6, 6), (7, 5), (7, 6))
    for _, wait_sent in frame_sends + cot_sends:
        wait_sent()
    for after, before, _, _, item in edge_sends:

        @pl.when(sends_after & (seq != 2 * item + 1))
        def _(after=after):
            after.wait_send()

        @pl.when(sends_before & (seq != 2 * item))
        def _(before=before):
            before.wait_send()

    finish_blocks(last_sends, 128, output, r.s_last)
    finish_blocks(grad_sends, 256, input_grad, r.s_grad, 4)


def pick8(total, most):
    best = 8
    for size in range(8, most + 1, 8):
        if total % size == 0:
            best = size
    return best


GRAD_SHAPES = (
    (2, 3, 256, 256),
    (2, 3, 256, 256),
    (2, 256, 256),
    (2, 2, 256),
    (2, 2, 256),
    (2, 1024, 256),
    (2, 256),
    (2, 2, 256),
    (2, 2, 256),
    (2, 256, 384),
    (2, 128, 256),
    (2, 256),
    (2, 256, 1024),
    (2, 1024),
    (2, 1024),
    (2, 1024),
    (2, 1024, 256),
    (2, 256),
    (3, 256, 256),
    (256,),
)

class Gradients(typing.NamedTuple):
    conv_one: Any
    conv_two: Any
    res_weight: Any
    norm_gain: Any
    norm_bias: Any
    time_weight: Any
    time_bias: Any
    layer_gain: Any
    layer_bias: Any
    qkv_weight: Any
    out_weight: Any
    out_bias: Any
    up_weight: Any
    up_bias: Any
    snake_alpha: Any
    snake_beta: Any
    down_weight: Any
    down_bias: Any
    shrink_weight: Any
    shrink_bias: Any


def unpack_kernel(shape, total, last, grad, *refs):
    outs = Gradients(*refs[2:22])
    held, held_last, held_grad, held_time, sems, out_sems = refs[22:]
    loads, stores = [], []

    def rows(start, count):
        return total.at[pl.ds(start, count)], held.at[pl.ds(start, count)]

    def load(start, count):
        source, target = rows(start, count)
        loads.append(pltpu.make_async_copy(source, target, sems.at[len(loads)]))
        loads[-1].start()

    def store(start, count, target, lanes=pl.ds(0, 256)):
        source = held.at[pl.ds(start, count), lanes]
        stores.append((pltpu.make_async_copy(source, target, out_sems.at[len(stores)]), len(loads)))

    def move(start, count, target):
        load(start, count)
        store(start, count, target)

    for source, through, target in ((last, held_last, refs[0]), (grad, held_grad, refs[1])):
        loads.append(pltpu.make_async_copy(source, through, sems.at[len(loads)]))
        loads[-1].start()
        stores.append((pltpu.make_async_copy(through, target, out_sems.at[len(stores)]), len(loads)))
    load(EMBED_AT, 64)
    for layer in (1, 0):
        load(SMALL_AT[layer], 24)
        load(LATER_AT[layer] + LATER_SMALL, 16)
    small_loads = len(loads)
    for layer in (1, 0):
        later = LATER_AT[layer]
        for column in range(4):
            lanes = pl.ds(256 * column, 256)
            move(later + UP + 256 * column, 256, outs.up_weight.at[layer, :, lanes])
        move(later + DOWN, 1024, outs.down_weight.at[layer])
        move(later + OUT, 128, outs.out_weight.at[layer])
        for tap in range(3):
            move(CONV_TWO_AT[layer] + 256 * tap, 256, outs.conv_two.at[layer, tap])
        move(RES_AT[layer], 256, outs.res_weight.at[layer])
        move(QUERY_KEY_AT[layer], 256, outs.qkv_weight.at[layer, :, pl.ds(0, 256)])
        for tap in range(3):
            move(CONV_ONE_AT[layer] + 256 * tap, 256, outs.conv_one.at[layer, tap])
        load(VALUE_AT[layer], 128)
        for part in (0, 1):
            target = outs.qkv_weight.at[layer, pl.ds(128 * part, 128), pl.ds(256, 128)]
            store(VALUE_AT[layer], 128, target, pl.ds(128 * part, 128))
    for tap in range(3):
        move(SHRINK_AT + 256 * tap, 256, outs.shrink_weight.at[tap])
    for number in range(small_loads):
        loads[number].wait()
    for layer in (0, 1):
        later = held[pl.ds(LATER_AT[layer] + LATER_SMALL, 16), :]
        res = held[pl.ds(SMALL_AT[layer], 24), :]
        outs.norm_gain[layer] = res[0:2]
        outs.norm_bias[layer] = res[2:4]
        outs.layer_gain[layer, 0:1, :] = res[4:5]
        outs.layer_gain[layer, 1:2, :] = later[2:3]
        outs.layer_bias[layer, 0:1, :] = res[5:6]
        outs.layer_bias[layer, 1:2, :] = later[3:4]
        outs.down_bias[layer : layer + 1, :] = later[0:1]
        outs.out_bias[layer : layer + 1, :] = later[1:2]
        for column in range(4):
            lanes = slice(256 * column, 256 * column + 256)
            outs.up_bias[layer : layer + 1, lanes] = later[4 + column : 5 + column]
            outs.snake_alpha[layer : layer + 1, lanes] = later[8 + column : 9 + column]
            outs.snake_beta[layer : layer + 1, lanes] = later[12 + column : 13 + column]
        summed = res[8:24]
        outs.time_bias[layer : layer + 1, :] = jnp.sum(summed, axis=0, keepdims=True)
        right = split(summed)
        blank = jnp.zeros((128 - 16, 256), F32)
        for column in range(4):
            tall = jnp.concatenate([held[pl.ds(EMBED_AT + 16 * column, 16), :], blank], 0)
            left = split(jnp.transpose(tall)[:, 0:16])
            held_time[layer, pl.ds(256 * column, 256), :] = dot_pair(left, right)
        time_copy = pltpu.make_async_copy(held_time.at[layer], outs.time_weight.at[layer], out_sems.at[46 + layer])
        stores.insert(0, (time_copy, 0))
    outs.shrink_bias[...] = held[pl.ds(SMALL_AT[1] + 6, 1), :]
    waited = small_loads
    for copy, needed in stores:
        for number in range(waited, needed):
            loads[number].wait()
        waited = max(waited, needed)
        copy.start()
    for copy, _ in stores:
        copy.wait()


def fused_local(shape, *args):
    groups = scratch_of(shape)
    given = Arguments(*args)
    specs = Arguments(*(WHOLE,) * 24)._replace(
        frames=ANY,
        lengths=pl.BlockSpec(memory_space=pltpu.SMEM),
        cotangent=ANY,
        conv_one=ANY,
        conv_two=ANY,
        res_weight=ANY,
        time_weight=ANY,
        qkv_weight=ANY,
        out_weight=ANY,
        up_weight=ANY,
        down_weight=ANY,
        shrink_weight=ANY,
    )
    output, input_grad, total = pl.pallas_call(
        lambda *refs: fused_kernel(shape, groups, *refs),
        out_shape=(
            jax.ShapeDtypeStruct(given.cotangent.shape, F32),
            jax.ShapeDtypeStruct(given.frames.shape, F32),
            jax.ShapeDtypeStruct((sum(BUCKET_ROWS), 256), F32),
        ),
        in_specs=list(specs),
        out_specs=(ANY,) * 3,
        scratch_shapes=[one for group in groups for one in group.values()],
        name="layers",
        compiler_params=pltpu.CompilerParams(
            collective_id=0, has_side_effects=True, vmem_limit_bytes=VMEM_BYTES
        ),
    )(*given)
    shapes = [s if len(s) > 1 else (1,) + s for s in GRAD_SHAPES]
    shapes = [output.shape, input_grad.shape] + shapes
    grads = pl.pallas_call(
        lambda *refs: unpack_kernel(shape, *refs),
        out_shape=tuple(jax.ShapeDtypeStruct(s, F32) for s in shapes),
        in_specs=[ANY] * 3,
        out_specs=(ANY, ANY)
        + tuple(
            Gradients(*(WHOLE,) * 20)._replace(
                time_weight=ANY,
                conv_one=ANY,
                conv_two=ANY,
                res_weight=ANY,
                qkv_weight=ANY,
                out_weight=ANY,
                up_weight=ANY,
                down_weight=ANY,
                shrink_weight=ANY,
            )
        ),
        scratch_shapes=[
            pltpu.VMEM((sum(BUCKET_ROWS), 256), F32),
            pltpu.VMEM(output.shape, F32),
            pltpu.VMEM(input_grad.shape, F32),
            pltpu.VMEM((2, 1024, 256), F32),
            pltpu.SemaphoreType.DMA((48,)),
            pltpu.SemaphoreType.DMA((48,)),
        ],
        name="unpack",
        compiler_params=pltpu.CompilerParams(vmem_limit_bytes=VMEM_BYTES),
    )(total, output, input_grad)
    grads = grads[:-1] + (grads[-1].reshape(256),)
    return tuple(grads)


VMEM_BYTES = 64 * 2**20 - 2**18


ARG_SPECS = (P("dp", "seq", None), P("dp", None), P("dp"), P("dp", "seq", None)) + (P(),) * 20
OUT_SPECS = (P("dp", "seq", None), P("dp", "seq", None)) + (P(),) * 20


def solution(mesh):
    shape = dict(mesh.shape)

    def local(*args):
        utterances, frames_in = args[0].shape[:2]
        if fits(shape, utterances, frames_in):
            return fused_local(shape, *args)
        return general_local(*args)

    return jax.shard_map(
        local, mesh=mesh, in_specs=ARG_SPECS, out_specs=OUT_SPECS, check_vma=False
    )
```
